32 devices in a mesh: dp: 4 (over z), seq: 4 (over x, core), hidden: 2 (over y).
Axes of the slice: x: 2, y: 2, z: 4, core: 2. Of those that a mesh axis runs over, the one named last changes fastest.
Arguments:
- tokens: bfloat16 [18432, 768], P(('dp', 'seq', 'hidden')), may hold values from -6 to 6
- segment: int32 [18432], P('dp'), may hold values from 0 to 43, as said below
- cotangent: bfloat16 [18432, 768], P(('dp', 'seq', 'hidden')), may hold values from -6 to 6
- ln1_gain: bfloat16 [768], P('dp'), may hold values from 0.099609375 to 1.8984375
- ln1_bias: bfloat16 [768], P('dp'), may hold values from -1.75 to 1.75
- qkv_weight: bfloat16 [3, 768, 768], P(None, 'dp', 'hidden'), may hold values from -0.21875 to 0.21875
- qk_gain: bfloat16 [2, 64], P(None, 'dp'), may hold values from 0.099609375 to 1.8984375
- out_weight: bfloat16 [768, 768], P('hidden', 'dp'), may hold values from -0.625 to 0.625
- out_bias: bfloat16 [768], P('dp'), may hold values from -1.75 to 1.75
- ln2_gain: bfloat16 [768], P('dp'), may hold values from 0.099609375 to 1.8984375
- ln2_bias: bfloat16 [768], P('dp'), may hold values from -1.75 to 1.75
- fc1_weight: bfloat16 [768, 3072], P('dp', 'hidden'), may hold values from -0.21875 to 0.21875
- fc2_weight: bfloat16 [3072, 768], P('hidden', 'dp'), may hold values from -0.109375 to 0.109375
- fc2_bias: bfloat16 [768], P('dp'), may hold values from -1.75 to 1.75
Outputs:
- output: bfloat16 [18432, 768], P(('dp', 'seq', 'hidden'))
- input_grad: bfloat16 [18432, 768], P(('dp', 'seq', 'hidden'))
- ln1_gain_grad: float32 [768], P('dp')
- ln1_bias_grad: float32 [768], P('dp')
- qkv_grad: float32 [3, 768, 768], P(None, 'dp', 'hidden')
- qk_gain_grad: float32 [2, 64], P(None, 'dp')
- out_weight_grad: float32 [768, 768], P('hidden', 'dp')
- out_bias_grad: float32 [768], P('dp')
- ln2_gain_grad: float32 [768], P('dp')
- ln2_bias_grad: float32 [768], P('dp')
- fc1_grad: float32 [768, 3072], P('dp', 'hidden')
- fc2_grad: float32 [3072, 768], P('hidden', 'dp')
- fc2_bias_grad: float32 [768], P('dp')
The draws below stay inside these ranges and needn't reach their ends.
Inputs may be any that keep to these rules, and one draw needn't show every extreme that they name: `segment`: within a pack of 4608 rows, an id marks either a sequence of 576 patches with a quarter of its rows in each block of 1152 rows, or an image of 64 patches inside one such block; ids in different packs are unrelated.
All inputs are finite; a program needn't handle non-finite values.
Results may differ from the reference program's by a relative error of at most 0.02.
Values may be sent and summed in bfloat16 or wider, within the bound.
A program may use at most 384 MiB of HBM per device.

```python
import jax
import jax.numpy as jnp
from jax import lax

D = 768
HEADS = 12
HEAD = 64
FF = 3072
LONG = 576
IMAGE = 64
LONGS = 8
QROWS = 1152
PACK = 4608
TOKENS = 18432
IMAGES = 9


def draw_segment(key, part):
    key = jax.random.fold_in(key, 11)
    first_key, second_key = jax.random.split(key)
    packs = TOKENS // PACK
    blocks = PACK // QROWS
    upper = jax.random.randint(first_key, (packs,), 0, 2)
    longs = jnp.where(jnp.arange(packs) == 0, LONGS // 2, LONGS // 2 * (1 + upper))
    offset = jax.random.randint(second_key, (packs, blocks), 0, QROWS)
    place = (jnp.arange(QROWS)[None, None, :] + offset[:, :, None]) % QROWS
    part_rows = LONG // blocks
    long_rows = longs[:, None, None] * part_rows
    which = jnp.arange(blocks)[None, :, None]
    labels = jnp.where(place < long_rows, place // part_rows, LONGS + which * IMAGES + (place - long_rows) // IMAGE)
    return labels.reshape(TOKENS).astype(jnp.int32)


def block_scale(rng, dims, cuts, low, largest):
    level, own = 1.0, jax.random.fold_in(rng, 6)
    for dim, shards_of in cuts:
        heights = jnp.exp(jax.random.uniform(jax.random.fold_in(own, dim), (shards_of,), jnp.float32, low / len(cuts), largest / len(cuts)))
        level = level * jnp.repeat(heights, dims[dim] // shards_of).reshape([-1 if axis == dim else 1 for axis in range(len(dims))])
    return level


def gaussian(key, shape, deviation, reach, shards=(), held_as=jnp.bfloat16):
    entries = deviation * jax.random.normal(key, shape, jnp.float32)
    if shards:
        entries = entries * block_scale(key, shape, shards, -0.22, 0.18)
    return jnp.clip(entries, -reach, reach).astype(held_as)


def setup_inputs(seed: int = 0) -> dict:
    streams_of = jax.random.split(jax.random.key(seed), 15)
    tokens = gaussian(streams_of[0], (TOKENS, D), 1.0, 6.0, ((0, 32),))
    segment = draw_segment(jax.random.fold_in(streams_of[14], 71), 0)
    cotangent = gaussian(streams_of[2], (TOKENS, D), 1.0, 6.0, ((0, 32),))
    ln1_gain = jnp.clip(1.0 + 0.18 * jax.random.normal(streams_of[3], (D,), jnp.float32), 0.099609375, 1.8984375).astype(jnp.bfloat16)
    ln1_bias = gaussian(streams_of[4], (D,), 0.3, 1.75, ((0, 4),))
    qkv_weight = gaussian(streams_of[5], (3, D, D), D ** -0.5, 0.21875, ((1, 4), (2, 2)))
    qk_gain = jnp.clip(1.0 + 0.18 * jax.random.normal(streams_of[6], (2, HEAD), jnp.float32), 0.099609375, 1.8984375).astype(jnp.bfloat16)
    out_weight = gaussian(streams_of[7], (D, D), (D // 8) ** -0.5, 0.625, ((0, 2), (1, 4)))
    out_bias = gaussian(streams_of[8], (D,), 0.3, 1.75, ((0, 4),))
    ln2_gain = jnp.clip(1.0 + 0.18 * jax.random.normal(streams_of[9], (D,), jnp.float32), 0.099609375, 1.8984375).astype(jnp.bfloat16)
    ln2_bias = gaussian(streams_of[10], (D,), 0.3, 1.75, ((0, 4),))
    fc1_weight = gaussian(streams_of[11], (D, FF), D ** -0.5, 0.21875, ((0, 4), (1, 2)))
    fc2_weight = gaussian(streams_of[12], (FF, D), FF ** -0.5, 0.109375, ((0, 2), (1, 4)))
    fc2_bias = gaussian(streams_of[13], (D,), 0.3, 1.75, ((0, 4),))
    return dict(tokens=tokens, segment=segment, cotangent=cotangent, ln1_gain=ln1_gain, ln1_bias=ln1_bias, qkv_weight=qkv_weight, qk_gain=qk_gain, out_weight=out_weight, out_bias=out_bias, ln2_gain=ln2_gain, ln2_bias=ln2_bias, fc1_weight=fc1_weight, fc2_weight=fc2_weight, fc2_bias=fc2_bias)


EPSILON = 1e-06

@jax.custom_vjp
def low(v):
    return lax.optimization_barrier(v.astype(jnp.bfloat16)).astype(jnp.float32)

@jax.custom_vjp
def low_back(v):
    return v

def low_keep(v):
    return (low(v), None)

def low_pass(kept, grad):
    return (grad,)

def back_keep(v):
    return (v, None)

def back_low(kept, grad):
    return (low(grad),)
low.defvjp(low_keep, low_pass)
low_back.defvjp(back_keep, back_low)

def highest(left, right):
    return jnp.dot(left, right, precision=lax.Precision.HIGHEST)

def standard(values, gain, shift):
    centred = values - lax.optimization_barrier(jnp.mean(values, axis=-1, keepdims=True))
    spread = lax.optimization_barrier(jnp.mean(centred * centred, axis=-1, keepdims=True))
    return centred * lax.rsqrt(spread + EPSILON) * gain + shift

def head_norm(values, gain):
    centred = values - lax.optimization_barrier(jnp.mean(values, axis=-1, keepdims=True))
    spread = lax.optimization_barrier(jnp.mean(centred * centred, axis=-1, keepdims=True))
    return centred * lax.rsqrt(spread + EPSILON) * gain

def layer_pack(params, inputs, labels):
    ln1_gain, ln1_bias, qkv_weight, qk_gain, out_weight, out_bias, ln2_gain, ln2_bias, fc1_weight, fc2_weight, fc2_bias = params
    rows = inputs.shape[0]
    score_scale = HEAD ** (-0.5)
    normed = low(standard(inputs, ln1_gain, ln1_bias))
    query_raw = low_back(highest(normed, qkv_weight[0])).reshape(rows, HEADS, HEAD)
    key_raw = low_back(highest(normed, qkv_weight[1])).reshape(rows, HEADS, HEAD)
    values = low(low_back(highest(normed, qkv_weight[2]))).reshape(rows, HEADS, HEAD)
    queries = low(head_norm(query_raw, qk_gain[0]))
    keys = low(head_norm(key_raw, qk_gain[1]))

    def attend(block):
        query_block, label_block = block
        scores = jnp.einsum('qhd,khd->hqk', query_block, keys, precision=lax.Precision.HIGHEST)
        scores = low_back(scores * score_scale)
        scores = jnp.where(label_block[None, :, None] == labels[None, None, :], scores, -1e+30)
        weights = low(jax.nn.softmax(scores, axis=-1))
        return jnp.einsum('hqk,khd->qhd', weights, values, precision=lax.Precision.HIGHEST)
    attended = lax.map(jax.checkpoint(attend), (queries.reshape(rows // LONG, LONG, HEADS, HEAD), labels.reshape(rows // LONG, LONG)))
    attended = low(low_back(attended.reshape(rows, D)))
    mixed = inputs + low_back(highest(attended, out_weight) + out_bias)
    normed_two = low(standard(mixed, ln2_gain, ln2_bias))
    hidden_pre = low_back(highest(normed_two, fc1_weight))
    activated = low(jax.nn.gelu(hidden_pre, approximate=False))
    return mixed + low_back(highest(activated, fc2_weight) + fc2_bias)

def reference(tokens, segment, cotangent, ln1_gain, ln1_bias, qkv_weight, qk_gain, out_weight, out_bias, ln2_gain, ln2_bias, fc1_weight, fc2_weight, fc2_bias):
    params = tuple((argument.astype(jnp.float32) for argument in (ln1_gain, ln1_bias, qkv_weight, qk_gain, out_weight, out_bias, ln2_gain, ln2_bias, fc1_weight, fc2_weight, fc2_bias)))
    packs = TOKENS // PACK
    inputs = tokens.astype(jnp.float32).reshape(packs, PACK, D)
    labels = segment.reshape(packs, PACK)

    def forward(params, inputs):

        def one_pack(pack_pair):
            return jax.checkpoint(layer_pack)(params, pack_pair[0], pack_pair[1])
        return lax.map(one_pack, (inputs, labels))
    result, pullback = jax.vjp(forward, params, inputs)
    param_grads, input_grads = pullback(cotangent.astype(jnp.float32).reshape(packs, PACK, D))
    return (result.reshape(TOKENS, D).astype(jnp.bfloat16), input_grads.reshape(TOKENS, D).astype(jnp.bfloat16), param_grads[0], param_grads[1], param_grads[2], param_grads[3], param_grads[4], param_grads[5], param_grads[6], param_grads[7], param_grads[8], param_grads[9], param_grads[10])
```

```python
import functools

import jax
import jax.numpy as jnp
from jax import lax
from jax.experimental import pallas as pl
from jax.experimental.pallas import tpu as pltpu
from jax.sharding import PartitionSpec as P

HEAD = 64
LONG = 576
IMAGE = 64
LABELS = 128
EPSILON = 1e-06
SCALE = HEAD ** (-0.5)
F32 = jnp.float32
BF16 = jnp.bfloat16

VMEM = pl.BlockSpec(memory_space=pltpu.VMEM)
SMEM = pl.BlockSpec(memory_space=pltpu.SMEM)
LN1_GAIN, LN1_BIAS, OUT_BIAS, LN2_GAIN, LN2_BIAS, FC2_BIAS, QK_GAIN = range(7)


def params(limit=56 << 20, **more):
    return pltpu.CompilerParams(vmem_limit_bytes=limit, **more)


def shape(dims, dtype=BF16):
    return jax.ShapeDtypeStruct(dims, dtype)


def dot(left, right):
    return jnp.dot(left, right, preferred_element_type=F32)


def dot_nt(left, right):
    return lax.dot_general(left, right, (((1,), (1,)), ((), ())), preferred_element_type=F32)


def dot_tn(left, right):
    return lax.dot_general(left, right, (((0,), (0,)), ((), ())), preferred_element_type=F32)


def iota(dims, dim):
    return lax.broadcasted_iota(jnp.int32, dims, dim)


def one_hot(test):
    return jnp.where(test, 1.0, 0.0).astype(BF16)


def two_part(values, matrix):
    high = values.astype(BF16)
    rest = (values - high.astype(F32)).astype(BF16)
    return dot(high, matrix) + dot(rest, matrix)


def head_mean_matrix(width):
    return jnp.where(
        iota((width, width), 0) // HEAD == iota((width, width), 1) // HEAD, 1.0 / HEAD, 0.0
    ).astype(BF16)


def row_norm(values):
    mean = jnp.mean(values, axis=-1, keepdims=True)
    centred = values - mean
    spread = jnp.mean(centred * centred, axis=-1, keepdims=True)
    scale = lax.rsqrt(spread + EPSILON)
    return centred * scale, scale


def row_norm_back(grad_unit, unit, scale):
    first = jnp.mean(grad_unit, axis=-1, keepdims=True)
    second = jnp.mean(grad_unit * unit, axis=-1, keepdims=True)
    return scale * (grad_unit - first - unit * second)


def normal_cdf(values):
    size = jnp.abs(values) * (2.0 ** -0.5)
    bell = jnp.exp(-0.5 * values * values)
    t = 1.0 / (1.0 + 0.3275911 * size)
    poly = 1.061405429 * t - 1.453152027
    poly = poly * t + 1.421413741
    poly = poly * t - 0.284496736
    poly = poly * t + 0.254829592
    tail = 0.5 * (poly * t) * bell
    return jnp.where(values < 0, tail, 1.0 - tail), bell * 0.3989422804014327


def place_kernel(row_ref, col_ref, place_row_ref, place_col_ref, mode_ref):
    rows = row_ref.shape[1]
    half = rows // 2
    chunk = LONG // 4
    by_row = one_hot(row_ref[...] == iota((LABELS, rows), 0))
    by_col = one_hot(col_ref[...] == iota((rows, LABELS), 1))
    count_col = jnp.sum(by_row.astype(F32), axis=1, keepdims=True)
    count_row = jnp.sum(by_col.astype(F32), axis=0, keepdims=True)
    cut = 0.5 * (chunk + IMAGE)
    long_col = jnp.where(count_col > cut, count_col, 0.0)
    long_row = jnp.where(count_row > cut, count_row, 0.0)
    small_col = count_col - long_col
    small_row = count_row - long_row
    total = jnp.sum(long_row, axis=1, keepdims=True)
    left = iota((LABELS, LABELS), 0)
    right = iota((LABELS, LABELS), 1)

    def before_col(counts):
        return jnp.sum(jnp.where(right < left, counts, 0.0), axis=1, keepdims=True)

    def before_row(counts):
        return jnp.sum(jnp.where(left < right, counts, 0.0), axis=0, keepdims=True)

    base_col = jnp.where(long_col > 0, before_col(long_row), total + before_col(small_row))
    base_row = jnp.where(long_row > 0, before_row(long_col), total + before_row(small_col))
    earlier = one_hot(iota((rows, rows), 0) < iota((rows, rows), 1))
    later = one_hot(iota((rows, rows), 1) < iota((rows, rows), 0))
    rank_row = dot(by_row, earlier)
    rank_col = dot(later, by_col)
    place_row = jnp.sum(by_row.astype(F32) * (rank_row + base_col), axis=0, keepdims=True)
    place_col = jnp.sum(by_col.astype(F32) * (rank_col + base_row), axis=1, keepdims=True)
    place_row = place_row.astype(jnp.int32)
    place_row_ref[0:1, :] = place_row[:, :half]
    place_row_ref[1:2, :] = place_row[:, half:]
    place_col_ref[...] = place_col.astype(jnp.int32)
    mode_ref[0] = (jnp.sum(long_row) > rows - IMAGE).astype(jnp.int32)


def place_rows(labels):
    rows = labels.shape[0]
    return pl.pallas_call(
        place_kernel,
        out_shape=(
            shape((2, rows // 2), jnp.int32),
            shape((rows, 1), jnp.int32),
            shape((1,), jnp.int32),
        ),
        in_specs=[VMEM, VMEM],
        out_specs=(VMEM, VMEM, SMEM),
        compiler_params=params(),
        name="place_rows",
    )(labels.reshape(1, rows), labels.reshape(rows, 1))


def sort_kernel(here_ref, place_ref, own_ref, other_ref, *refs):
    sorted_refs, send_refs = refs[:2], refs[2:]
    half = own_ref.shape[0]
    seqs = len(send_refs) // 2 + 1
    chunk = half // seqs
    first = here_ref[1] == 0
    place_own = jnp.where(first, place_ref[0:1, :], place_ref[1:2, :])
    place_other = jnp.where(first, place_ref[1:2, :], place_ref[0:1, :])
    for part in range(2):
        target = iota((half, half), 0) + part * half
        rows = dot(one_hot(target == place_own), own_ref[...])
        rows = rows + dot(one_hot(target == place_other), other_ref[...])
        sorted_refs[part][...] = rows.astype(BF16)
        for step in range(1, seqs):
            start = pl.multiple_of((here_ref[0] ^ step) * chunk, 16)
            send_refs[part * (seqs - 1) + step - 1][...] = sorted_refs[part][pl.ds(start, chunk), :]


def sort_rows(here, place_row, own, other, seqs):
    half, width = own.shape
    chunk = half // seqs
    results = pl.pallas_call(
        sort_kernel,
        out_shape=[shape((half, width))] * 2 + [shape((chunk, width))] * (2 * (seqs - 1)),
        in_specs=[SMEM, VMEM, VMEM, VMEM],
        out_specs=[VMEM] * (2 * seqs),
        compiler_params=params(),
        name="sort_rows",
        cost_estimate=pl.CostEstimate(
            flops=8 * half * half * width, bytes_accessed=8 * half * width, transcendentals=0
        ),
    )(here, place_row, own, other)
    return results[:2], (results[2 : seqs + 1], results[seqs + 1 :])


def fill_sequence(here_ref, mode_ref, sorted_ref, got_refs, rows_ref, part):
    half = rows_ref.shape[0]
    chunk = half // (len(got_refs) + 1)
    home = sorted_ref[pl.ds(pl.multiple_of(here_ref[0] * chunk, 16), chunk), :]
    for step in range(len(got_refs) + 1):
        rows = home if step == 0 else got_refs[step - 1][...]
        if part == 1:
            local = sorted_ref[step * chunk : (step + 1) * chunk, :]
            rows = jnp.where(mode_ref[0] == 1, rows.astype(F32), local.astype(F32)).astype(BF16)
        rows_ref[step * chunk : (step + 1) * chunk, :] = rows


def image_mask(mode_ref, rows):
    same = iota((rows, rows), 0) // IMAGE == iota((rows, rows), 1) // IMAGE
    return jnp.where(same, 1.0, jnp.where(mode_ref[0] == 1, 1.0, 0.0))


def attend_kernel(
    part,
    here_ref,
    mode_ref,
    sorted_ref,
    *refs,
):
    got_refs, refs = refs[:3], refs[3:]
    (
        weight_ref,
        vec_ref,
        attended_ref,
        normed_ref,
        unit_ref,
        low_ref,
        value_ref,
        head_unit_ref,
        head_scale_ref,
        rows_ref,
        raw_ref,
        mask_ref,
    ) = refs
    half, width = rows_ref.shape
    inner = value_ref.shape[1]
    chunk = half // 4
    fill_sequence(here_ref, mode_ref, sorted_ref, got_refs, rows_ref, part)
    for step in range(4):
        rows = slice(step * chunk, (step + 1) * chunk)
        unit, _ = row_norm(rows_ref[rows, :].astype(F32))
        unit_ref[rows, :] = unit.astype(BF16)
        normed = unit * vec_ref[LN1_GAIN : LN1_GAIN + 1, :] + vec_ref[LN1_BIAS : LN1_BIAS + 1, :]
        normed_ref[rows, :] = normed.astype(BF16)
    raw_ref[:, :inner] = dot(normed_ref[...], weight_ref[0])
    raw_ref[:, inner:] = dot(normed_ref[...], weight_ref[1])
    value_ref[...] = dot(normed_ref[...], weight_ref[2]).astype(BF16)
    group = 4 * HEAD
    means = head_mean_matrix(group)
    for first in range(0, 2 * inner, group):
        cols = slice(first, first + group)
        raw = raw_ref[:, cols]
        centred = raw - two_part(raw, means)
        scale = lax.rsqrt(two_part(centred * centred, means) + EPSILON)
        unit = centred * scale
        head_unit_ref[:, cols] = unit
        head_scale_ref[:, cols] = scale
        low_ref[:, cols] = (unit * vec_ref[QK_GAIN : QK_GAIN + 1, cols]).astype(BF16)
    pair = 2 * HEAD
    lane = iota((half, pair), 1)
    if part == 1:
        mask_ref[...] = image_mask(mode_ref, half).astype(BF16)
    for first in range(0, inner, pair):
        query = low_ref[:, first : first + pair] * SCALE
        key = low_ref[:, inner + first : inner + first + pair]
        value = jnp.concatenate(
            [value_ref[:, first : first + pair], jnp.ones((half, pair), BF16)], axis=1
        )
        found = []
        for head in range(2):
            mine = (lane // HEAD) == head
            scores = dot_nt(jnp.where(mine, query, jnp.zeros_like(query)), key)
            weights = jnp.exp(scores).astype(BF16)
            if part == 1:
                weights = weights * mask_ref[...]
            both = dot(weights, value)
            found.append(both[:, :pair] / both[:, pair:])
        result = jnp.where(lane < HEAD, found[0], found[1]).astype(BF16)
        for step in range(4):
            attended_ref[step, :, first : first + pair] = result[
                step * chunk : (step + 1) * chunk, :
            ]


def attend(part, here, mode, ordered, got, weight, vectors):
    half, width = ordered.shape
    seqs = len(got) + 1
    chunk = half // seqs
    inner = weight.shape[2]
    return pl.pallas_call(
        functools.partial(attend_kernel, part),
        out_shape=(
            shape((seqs, chunk, inner)),
            shape((half, width)),
            shape((half, width)),
            shape((half, 2 * inner)),
            shape((half, inner)),
            shape((half, 2 * inner), F32),
            shape((half, 2 * inner), F32),
        ),
        in_specs=[SMEM, SMEM] + [VMEM] * (seqs + 2),
        out_specs=(VMEM,) * 7,
        scratch_shapes=[
            pltpu.VMEM((half, width), BF16),
            pltpu.VMEM((half, 2 * inner), F32),
            pltpu.VMEM((half, half), BF16),
        ],
        compiler_params=params(),
        name="attend",
        cost_estimate=pl.CostEstimate(
            flops=2 * half * width * 3 * inner + 8 * half * half * inner,
            bytes_accessed=16 * half * width,
            transcendentals=half * half * inner // HEAD,
        ),
    )(here, mode, ordered, *got, weight, vectors)


def gather_kernel(here_ref, mode_ref, *refs):
    homes, gots, out_ref = refs[:2], refs[2:-1], refs[-1]
    half = out_ref.shape[0] // 2
    seqs = homes[0].shape[0]
    chunk = half // seqs
    for part in range(2):
        if part == 1:
            for step in range(seqs):
                out_ref[half + step * chunk : half + (step + 1) * chunk, :] = homes[1][step]
        for step in range(seqs):
            start = pl.multiple_of(part * half + (here_ref[0] ^ step) * chunk, 16)
            piece = homes[part].at[0] if step == 0 else gots[part * (seqs - 1) + step - 1]
            if part == 0:
                out_ref[pl.ds(start, chunk), :] = piece[...]
            else:

                @pl.when(mode_ref[0] == 1)
                def _(piece=piece, start=start):
                    out_ref[pl.ds(start, chunk), :] = piece[...]


def gather_rows(here, mode, homes, gots):
    seqs, chunk, width = homes[0].shape
    flat = [homes[0], homes[1], *gots[0], *gots[1]]
    return pl.pallas_call(
        gather_kernel,
        out_shape=shape((2 * seqs * chunk, width)),
        in_specs=[SMEM, SMEM] + [VMEM] * len(flat),
        out_specs=VMEM,
        compiler_params=params(),
        name="gather_rows",
    )(here, mode, *flat)


def unsort_kernel(place_own_ref, place_other_ref, rows_ref, own_ref, other_ref):
    half = own_ref.shape[0]
    rows = rows_ref.shape[0]
    for place_ref, out_ref in ((place_other_ref, other_ref), (place_own_ref, own_ref)):
        out_ref[...] = dot(
            one_hot(place_ref[...] == iota((half, rows), 1)), rows_ref[...]
        ).astype(BF16)


def unsort_rows(place_own, place_other, rows):
    half, width = rows.shape[0] // 2, rows.shape[1]
    return pl.pallas_call(
        unsort_kernel,
        out_shape=(shape((half, width)),) * 2,
        in_specs=[VMEM] * 3,
        out_specs=(VMEM,) * 2,
        compiler_params=params(),
        name="unsort_rows",
        cost_estimate=pl.CostEstimate(
            flops=8 * half * half * width, bytes_accessed=8 * half * width, transcendentals=0
        ),
    )(place_own, place_other, rows)


def feed_kernel(
    own,
    token_ref,
    cot_ref,
    place_ref,
    mine_ref,
    theirs_ref,
    out_mine_ref,
    out_theirs_ref,
    fc1_ref,
    fc2_ref,
    vec_ref,
    act_ref,
    grad_hidden_ref,
    normed_ref,
    grad_ref,
    sum_ref,
    *more,
):
    tile = token_ref.shape[0]
    rows = mine_ref.shape[0]
    units = fc1_ref.shape[1]
    back = one_hot(place_ref[...] == iota((tile, rows), 1))
    mine = dot(back, mine_ref[...]).astype(BF16)
    theirs = dot(back, theirs_ref[...]).astype(BF16)
    mixed = (
        token_ref[...].astype(F32)
        + (dot(mine, out_mine_ref[...]) + dot(theirs, out_theirs_ref[...]))
        + vec_ref[OUT_BIAS : OUT_BIAS + 1, :]
    )
    unit, _ = row_norm(mixed)
    normed = unit * vec_ref[LN2_GAIN : LN2_GAIN + 1, :] + vec_ref[LN2_BIAS : LN2_BIAS + 1, :]
    normed = normed.astype(BF16)
    normed_ref[...] = normed
    cot = cot_ref[...]
    total = None
    step = 512
    for first in range(0, units, step):
        cols = slice(first, first + step)
        pre = dot(normed, fc1_ref[:, cols])
        grad_act = dot_nt(cot, fc2_ref[cols, :])
        cdf, density = normal_cdf(pre)
        act_ref[:, cols] = (pre * cdf).astype(BF16)
        grad_hidden = (grad_act * (cdf + pre * density)).astype(BF16)
        grad_hidden_ref[:, cols] = grad_hidden
        add = dot_nt(grad_hidden, fc1_ref[:, cols])
        total = add if total is None else total + add
    grad_ref[...] = total.astype(grad_ref.dtype)

    @pl.when(pl.program_id(0) == 0)
    def _():
        sum_ref[...] = jnp.zeros_like(sum_ref)

    sum_ref[0:1, :] += jnp.sum(total * unit, axis=0, keepdims=True)
    sum_ref[1:2, :] += jnp.sum(total, axis=0, keepdims=True)
    if own:
        mixed_ref, attended_ref = more
        mixed_ref[...] = mixed
        attended_ref[:, : mine.shape[1]] = mine
        attended_ref[:, mine.shape[1] :] = theirs
        sum_ref[2:3, :] += jnp.sum(cot.astype(F32), axis=0, keepdims=True)


def feed_forward(own, token, cot, place, mine, theirs, out_mine, out_theirs, fc1, fc2, vectors):
    half, width = token.shape
    rows, inner = mine.shape
    units = fc1.shape[1]
    tile = half // 2
    by_row = lambda cols: pl.BlockSpec((tile, cols), lambda i: (i, 0))
    fixed = lambda array: pl.BlockSpec(array.shape, lambda i: (0,) * array.ndim)
    outs = [
        shape((half, units)),
        shape((half, units)),
        shape((half, width)),
        shape((half, width), F32 if own else BF16),
        shape((8, width), F32),
    ]
    out_specs = [
        by_row(units),
        by_row(units),
        by_row(width),
        by_row(width),
        pl.BlockSpec((8, width), lambda i: (0, 0)),
    ]
    if own:
        outs += [shape((half, width), F32), shape((half, 2 * inner))]
        out_specs += [by_row(width), by_row(2 * inner)]
    return pl.pallas_call(
        functools.partial(feed_kernel, own),
        out_shape=outs,
        grid=(half // tile,),
        in_specs=[by_row(width), by_row(width), by_row(1)]
        + [fixed(a) for a in (mine, theirs, out_mine, out_theirs, fc1, fc2, vectors)],
        out_specs=out_specs,
        compiler_params=params(dimension_semantics=("arbitrary",)),
        name="feed_own" if own else "feed_other",
        cost_estimate=pl.CostEstimate(
            flops=2 * half * width * (rows + width + 3 * units),
            bytes_accessed=4 * width * units + 12 * half * units,
            transcendentals=half * units,
        ),
    )(token, cot, place, mine, theirs, out_mine, out_theirs, fc1, fc2, vectors)


def mix_back_kernel(
    mixed_ref,
    here_ref,
    got_ref,
    cot_ref,
    out_mine_ref,
    out_theirs_ref,
    vec_ref,
    grad_mixed_ref,
    grad_attn_ref,
    mine_ref,
    theirs_ref,
    sum_ref,
):
    unit, scale = row_norm(mixed_ref[...])
    grad = here_ref[...] + got_ref[...].astype(F32)
    grad = row_norm_back(grad * vec_ref[LN2_GAIN : LN2_GAIN + 1, :], unit, scale)
    grad = grad + cot_ref[...].astype(F32)
    grad_mixed_ref[...] = grad
    low = grad.astype(BF16)
    grad_attn_ref[...] = low
    theirs_ref[...] = dot_nt(low, out_theirs_ref[...]).astype(BF16)
    mine_ref[...] = dot_nt(low, out_mine_ref[...]).astype(BF16)

    @pl.when(pl.program_id(0) == 0)
    def _():
        sum_ref[...] = jnp.zeros_like(sum_ref)

    sum_ref[0:1, :] += jnp.sum(low.astype(F32), axis=0, keepdims=True)


def mix_back(mixed, here, got, cot, out_mine, out_theirs, vectors):
    half, width = mixed.shape
    inner = out_mine.shape[0]
    tile = half // 2
    by_row = lambda cols: pl.BlockSpec((tile, cols), lambda i: (i, 0))
    fixed = lambda array: pl.BlockSpec(array.shape, lambda i: (0,) * array.ndim)
    return pl.pallas_call(
        mix_back_kernel,
        out_shape=(
            shape((half, width), F32),
            shape((half, width)),
            shape((half, inner)),
            shape((half, inner)),
            shape((8, width), F32),
        ),
        grid=(half // tile,),
        in_specs=[by_row(width)] * 4 + [fixed(a) for a in (out_mine, out_theirs, vectors)],
        out_specs=(
            by_row(width),
            by_row(width),
            by_row(inner),
            by_row(inner),
            pl.BlockSpec((8, width), lambda i: (0, 0)),
        ),
        compiler_params=params(dimension_semantics=("arbitrary",)),
        name="mix_back",
        cost_estimate=pl.CostEstimate(
            flops=2 * half * width * width, bytes_accessed=16 * half * width, transcendentals=0
        ),
    )(mixed, here, got, cot, out_mine, out_theirs, vectors)


def attend_back_kernel(part, here_ref, mode_ref, sorted_ref, *refs):
    got_refs, refs = refs[:3], refs[3:]
    (
        low_ref,
        value_ref,
        head_unit_ref,
        head_scale_ref,
        unit_ref,
        weight_ref,
        vec_ref,
        grad_low_ref,
        grad_normed_ref,
        sum_ref,
        rows_ref,
        raw_ref,
        mask_ref,
    ) = refs
    half, inner = rows_ref.shape
    chunk = half // 4
    fill_sequence(here_ref, mode_ref, sorted_ref, got_refs, rows_ref, part)
    pair = 2 * HEAD
    lane = iota((half, pair), 1)
    if part == 1:
        mask_ref[...] = image_mask(mode_ref, half)
    for first in range(0, inner, pair):
        query = low_ref[:, first : first + pair] * SCALE
        key = low_ref[:, inner + first : inner + first + pair]
        value = value_ref[:, first : first + pair]
        grad = rows_ref[:, first : first + pair]
        key_turned = (key.astype(F32) * SCALE).T.astype(BF16)
        grad_values, grad_keys, grad_queries = [], [], []
        for head in range(2):
            mine = (lane // HEAD) == head
            query_head = jnp.where(mine, query, jnp.zeros_like(query))
            grad_head = jnp.where(mine, grad, jnp.zeros_like(grad))
            weights = jnp.exp(dot_nt(key, query_head))
            if part == 1:
                weights = weights * mask_ref[...]
            weights = weights * (1.0 / jnp.sum(weights, axis=0, keepdims=True))
            grad_weights = dot_nt(value, grad_head)
            shared = jnp.sum(weights * grad_weights, axis=0, keepdims=True)
            grad_scores = (weights * (grad_weights - shared)).astype(BF16)
            grad_values.append(dot(weights.astype(BF16), grad))
            grad_keys.append(dot(grad_scores, query))
            grad_queries.append(
                dot(key_turned[head * HEAD : (head + 1) * HEAD, :], grad_scores)
            )
        raw_ref[:, first : first + pair] = jnp.concatenate(grad_queries, axis=0).T
        raw_ref[:, inner + first : inner + first + pair] = jnp.where(
            lane < HEAD, grad_keys[0], grad_keys[1]
        )
        grad_low_ref[:, 2 * inner + first : 2 * inner + first + pair] = jnp.where(
            lane < HEAD, grad_values[0], grad_values[1]
        ).astype(BF16)
    group = 4 * HEAD
    means = head_mean_matrix(group)
    sum_ref[...] = jnp.zeros_like(sum_ref)
    for first in range(0, 2 * inner, group):
        cols = slice(first, first + group)
        grad = raw_ref[:, cols]
        unit = head_unit_ref[:, cols]
        sum_ref[2:3, cols] = jnp.sum(grad * unit, axis=0, keepdims=True)
        grad = grad * vec_ref[QK_GAIN : QK_GAIN + 1, cols]
        grad = head_scale_ref[:, cols] * (
            grad - two_part(grad, means) - unit * two_part(grad * unit, means)
        )
        grad_low_ref[:, cols] = grad.astype(BF16)
    total = dot_nt(grad_low_ref[:, :inner], weight_ref[0])
    total = total + dot_nt(grad_low_ref[:, inner : 2 * inner], weight_ref[1])
    total = total + dot_nt(grad_low_ref[:, 2 * inner :], weight_ref[2])
    sum_ref[0:1, :] = jnp.sum(total * unit_ref[...].astype(F32), axis=0, keepdims=True)
    sum_ref[1:2, :] = jnp.sum(total, axis=0, keepdims=True)
    for step in range(4):
        grad_normed_ref[step] = total[step * chunk : (step + 1) * chunk, :].astype(BF16)


def attend_back(part, here, mode, ordered, got, low, value, head_unit, head_scale, unit, weight, vectors):
    half, inner = ordered.shape
    seqs = len(got) + 1
    chunk = half // seqs
    width = unit.shape[1]
    return pl.pallas_call(
        functools.partial(attend_back_kernel, part),
        out_shape=(
            shape((half, 3 * inner)),
            shape((seqs, chunk, width)),
            shape((8, width), F32),
        ),
        in_specs=[SMEM, SMEM] + [VMEM] * (seqs + 7),
        out_specs=(VMEM,) * 3,
        scratch_shapes=[
            pltpu.VMEM((half, inner), BF16),
            pltpu.VMEM((half, 2 * inner), F32),
            pltpu.VMEM((half, half), F32),
        ],
        compiler_params=params(),
        name="attend_back",
        cost_estimate=pl.CostEstimate(
            flops=2 * half * width * 3 * inner + 24 * half * half * inner,
            bytes_accessed=20 * half * width,
            transcendentals=half * half * inner // HEAD,
        ),
    )(here, mode, ordered, *got, low, value, head_unit, head_scale, unit, weight, vectors)


def norm_back_kernel(token_ref, own_ref, got_ref, grad_mixed_ref, vec_ref, out_ref):
    unit, scale = row_norm(token_ref[...].astype(F32))
    grad = own_ref[...].astype(F32) + got_ref[...].astype(F32)
    grad = row_norm_back(grad * vec_ref[LN1_GAIN : LN1_GAIN + 1, :], unit, scale)
    out_ref[...] = (grad_mixed_ref[...] + grad).astype(BF16)


def norm_back(token, own, got, grad_mixed, vectors):
    half, width = token.shape
    tile = half // 4
    by_row = pl.BlockSpec((tile, width), lambda i: (i, 0))
    return pl.pallas_call(
        norm_back_kernel,
        out_shape=shape((half, width)),
        grid=(half // tile,),
        in_specs=[by_row] * 4 + [pl.BlockSpec(vectors.shape, lambda i: (0, 0))],
        out_specs=by_row,
        compiler_params=params(dimension_semantics=("arbitrary",)),
        name="norm_back",
    )(token, own, got, grad_mixed, vectors)


def swap(array, axis, step):
    pairs = [(index, index ^ step) for index in range(lax.axis_size(axis))]
    return lax.ppermute(array, axis, pairs)


def owned_sum(part, dim):
    total = lax.psum_scatter(part.astype(BF16), "dp", scatter_dimension=dim, tiled=True)
    total = (total.astype(F32) + swap(total, "seq", 1).astype(F32)).astype(BF16)
    return total.astype(F32) + swap(total, "seq", 2).astype(F32)


def local(
    tokens,
    segment,
    cotangent,
    ln1_gain,
    ln1_bias,
    qkv_weight,
    qk_gain,
    out_weight,
    out_bias,
    ln2_gain,
    ln2_bias,
    fc1_weight,
    fc2_weight,
    fc2_bias,
):
    half, width = tokens.shape
    quarter = half * lax.axis_size("hidden")
    seqs = lax.axis_size("seq")
    packs = lax.axis_size("dp")
    inner = qkv_weight.shape[2]
    heads = inner // HEAD
    seq, side = lax.axis_index("seq"), lax.axis_index("hidden")
    here = jnp.stack([seq, side]).astype(jnp.int32)

    tokens_other = swap(tokens, "hidden", 1)
    qkv_full = lax.all_gather(qkv_weight, "dp", axis=1, tiled=True)
    pieces = jnp.concatenate(
        [
            jnp.stack([ln1_gain, ln1_bias, out_bias, ln2_gain, ln2_bias, fc2_bias]).reshape(-1),
            qk_gain.reshape(-1),
        ]
    )
    pieces = lax.all_gather(pieces, "dp").astype(F32)
    share = ln1_gain.shape[0]
    wide = jnp.moveaxis(pieces[:, : 6 * share].reshape(packs, 6, share), 0, 1).reshape(6, width)
    gains = jnp.moveaxis(pieces[:, 6 * share :].reshape(packs, 2, -1), 0, 1).reshape(2, 1, HEAD)
    gains = jnp.broadcast_to(gains, (2, heads, HEAD)).reshape(1, width)
    vectors = jnp.concatenate([wide, gains, jnp.zeros((1, width), F32)], axis=0)
    cot_other = swap(cotangent, "hidden", 1)
    out_mine = lax.all_gather(out_weight, "dp", axis=1, tiled=True)
    out_theirs = swap(out_mine, "hidden", 1)
    fc1_full = lax.all_gather(fc1_weight, "dp", axis=0, tiled=True)
    fc2_full = lax.all_gather(fc2_weight, "dp", axis=1, tiled=True)

    labels = lax.dynamic_slice_in_dim(segment, seq * quarter, quarter, 0)
    place_row, place_col, mode = place_rows(labels)
    place_own = lax.dynamic_slice_in_dim(place_col, side * half, half, 0)
    place_other = lax.dynamic_slice_in_dim(place_col, (1 - side) * half, half, 0)

    ordered, sends = sort_rows(here, place_row, tokens, tokens_other, seqs)
    got = [[swap(send, "seq", step + 1) for step, send in enumerate(part)] for part in sends]
    kept, attended, returned = [], [], []
    for part in range(2):
        rows, *rest = attend(part, here, mode, ordered[part], got[part], qkv_full, vectors)
        kept.append(rest)
        attended.append(rows)
        returned.append([swap(rows[step], "seq", step) for step in range(1, seqs)])
    mine = gather_rows(here, mode, attended, returned)
    theirs = swap(mine, "hidden", 1)

    feed = (mine, theirs, out_mine, out_theirs, fc1_full, fc2_full, vectors)
    act_other, hidden_other, normed_other, grad_other, sums_other = feed_forward(
        False, tokens_other, cot_other, place_other, *feed
    )
    grad_got = swap(grad_other, "hidden", 1)
    act_own, hidden_own, normed_own, grad_own, sums_own, mixed, attended_own = feed_forward(
        True, tokens, cotangent, place_own, *feed
    )

    grad_mixed, grad_attn, mine_back, theirs_back, sums_mix = mix_back(
        mixed, grad_own, grad_got, cotangent, out_mine, out_theirs, vectors
    )
    back_got = swap(theirs_back, "hidden", 1)
    result_got = swap(dot(act_other, fc2_full).astype(BF16), "hidden", 1)
    result = dot(act_own, fc2_full) + mixed + vectors[FC2_BIAS][None, :]
    output = (result + result_got.astype(F32)).astype(BF16)
    fc2_part = dot_tn(act_own, cotangent) + dot_tn(act_other, cot_other)
    fc1_part = dot_tn(normed_own, hidden_own) + dot_tn(normed_other, hidden_other)
    fc2_owned = owned_sum(fc2_part, 1)
    fc1_owned = owned_sum(fc1_part, 0)
    out_both = dot_tn(attended_own, grad_attn)
    out_part = out_both[:inner] + swap(out_both[inner:].astype(BF16), "hidden", 1).astype(F32)
    out_owned = owned_sum(out_part, 1)

    ordered_back, sends_back = sort_rows(here, place_row, mine_back, back_got, seqs)
    got_back = [[swap(send, "seq", step + 1) for step, send in enumerate(part)] for part in sends_back]
    grads, homes, returned, sums_heads = [], [], [], []
    for part in range(2):
        normed, unit, low, value, head_unit, head_scale = kept[part]
        grad_low, grad_normed, sums = attend_back(
            part, here, mode, ordered_back[part], got_back[part], low, value, head_unit, head_scale, unit,
            qkv_full, vectors,
        )
        grads.append(grad_low)
        homes.append(grad_normed)
        sums_heads.append(sums)
        returned.append([swap(grad_normed[step], "seq", step) for step in range(1, seqs)])
    qkv_part = dot_tn(kept[0][0], grads[0]) + dot_tn(kept[1][0], grads[1])
    qkv_part = jnp.moveaxis(qkv_part.reshape(width, 3, inner), 1, 0)
    qkv_owned = owned_sum(qkv_part, 1)

    heads_sum = sums_heads[0] + sums_heads[1]
    sums_feed = sums_own + sums_other
    qk_sum = heads_sum[2].reshape(2, heads, HEAD).sum(axis=1)
    small = jnp.concatenate(
        [
            jnp.stack(
                [heads_sum[0], heads_sum[1], sums_mix[0], sums_feed[0], sums_feed[1], sums_feed[2]]
            ).reshape(6, packs, share).swapaxes(0, 1).reshape(packs, 6 * share),
            qk_sum.reshape(2, packs, HEAD // packs).swapaxes(0, 1).reshape(packs, -1),
        ],
        axis=1,
    )
    small = small + swap(small, "hidden", 1)
    small = small + swap(small, "seq", 1)
    small = small + swap(small, "seq", 2)
    small = lax.psum_scatter(small, "dp", scatter_dimension=0, tiled=True)[0]
    vec = small[: 6 * share].reshape(6, share)
    qk_owned = small[6 * share :].reshape(2, HEAD // packs)

    back = gather_rows(here, mode, homes, returned)
    back_own, back_other = unsort_rows(place_own, place_other, back)
    back_got = swap(back_other, "hidden", 1)
    input_grad = norm_back(tokens, back_own, back_got, grad_mixed, vectors)
    return (
        output,
        input_grad,
        vec[0],
        vec[1],
        qkv_owned,
        qk_owned,
        out_owned,
        vec[2],
        vec[3],
        vec[4],
        fc1_owned,
        fc2_owned,
        vec[5],
    )


def solution(mesh):
    rows = P(("dp", "seq", "hidden"), None)
    in_specs = (
        rows,
        P("dp"),
        rows,
        P("dp"),
        P("dp"),
        P(None, "dp", "hidden"),
        P(None, "dp"),
        P("hidden", "dp"),
        P("dp"),
        P("dp"),
        P("dp"),
        P("dp", "hidden"),
        P("hidden", "dp"),
        P("dp"),
    )
    out_specs = (
        rows,
        rows,
        P("dp"),
        P("dp"),
        P(None, "dp", "hidden"),
        P(None, "dp"),
        P("hidden", "dp"),
        P("dp"),
        P("dp"),
        P("dp"),
        P("dp", "hidden"),
        P("hidden", "dp"),
        P("dp"),
    )
    return jax.shard_map(local, mesh=mesh, in_specs=in_specs, out_specs=out_specs, check_vma=False)
```

```python
import functools

import jax
import jax.numpy as jnp
from jax import lax
from jax.experimental import pallas as pl
from jax.experimental.pallas import tpu as pltpu
from jax.sharding import PartitionSpec as P

HEAD = 64
LONG = 576
IMAGE = 64
LABELS = 128
EPSILON = 1e-06
SCALE = HEAD ** (-0.5)
F32 = jnp.float32
BF16 = jnp.bfloat16

VMEM = pl.BlockSpec(memory_space=pltpu.VMEM)
SMEM = pl.BlockSpec(memory_space=pltpu.SMEM)
HERE = pl.BlockSpec(memory_space=pl.ANY)
LN1_GAIN, LN1_BIAS, OUT_BIAS, LN2_GAIN, LN2_BIAS, FC2_BIAS, QK_GAIN = range(7)


def params(limit=56 << 20, **more):
    return pltpu.CompilerParams(vmem_limit_bytes=limit, **more)


def shape(dims, dtype=BF16):
    return jax.ShapeDtypeStruct(dims, dtype)


def dot(left, right):
    return jnp.dot(left, right, preferred_element_type=F32)


def dot_nt(left, right):
    return lax.dot_general(left, right, (((1,), (1,)), ((), ())), preferred_element_type=F32)


def dot_tn(left, right):
    return lax.dot_general(left, right, (((0,), (0,)), ((), ())), preferred_element_type=F32)


def iota(dims, dim):
    return lax.broadcasted_iota(jnp.int32, dims, dim)


def one_hot(test):
    return jnp.where(test, 1.0, 0.0).astype(BF16)


def two_part(values, matrix):
    high = values.astype(BF16)
    rest = (values - high.astype(F32)).astype(BF16)
    return dot(high, matrix) + dot(rest, matrix)


def head_mean_matrix(width):
    return jnp.where(
        iota((width, width), 0) // HEAD == iota((width, width), 1) // HEAD, 1.0 / HEAD, 0.0
    ).astype(BF16)


def row_norm(values):
    mean = jnp.mean(values, axis=-1, keepdims=True)
    centred = values - mean
    spread = jnp.mean(centred * centred, axis=-1, keepdims=True)
    scale = lax.rsqrt(spread + EPSILON)
    return centred * scale, scale


def row_norm_back(grad_unit, unit, scale):
    first = jnp.mean(grad_unit, axis=-1, keepdims=True)
    second = jnp.mean(grad_unit * unit, axis=-1, keepdims=True)
    return scale * (grad_unit - first - unit * second)


def normal_cdf(values):
    size = jnp.abs(values) * (2.0 ** -0.5)
    bell = jnp.exp(-0.5 * values * values)
    t = 1.0 / (1.0 + 0.3275911 * size)
    poly = 1.061405429 * t - 1.453152027
    poly = poly * t + 1.421413741
    poly = poly * t - 0.284496736
    poly = poly * t + 0.254829592
    tail = 0.5 * (poly * t) * bell
    return jnp.where(values < 0, tail, 1.0 - tail), bell * 0.3989422804014327


def other_of(value, step):
    return lax.bitwise_xor(value, jnp.int32(step))


def rows_at(start, size):
    return pl.ds(pl.multiple_of(start, 16), size)


class Copies:
    def __init__(self, send_sem, recv_sem):
        self.send_sem, self.recv_sem = send_sem, recv_sem
        self.made = []

    def start(self, source, target, device):
        index = len(self.made)
        copy = pltpu.make_async_remote_copy(
            src_ref=source,
            dst_ref=target,
            send_sem=self.send_sem.at[index],
            recv_sem=self.recv_sem.at[index],
            device_id=device,
            device_id_type=pl.DeviceIdType.MESH,
        )
        copy.start()
        self.made.append(copy)
        return copy

    def finish(self):
        for copy in self.made:
            copy.wait_send()


class Locals:
    def __init__(self, sem):
        self.sem, self.made = sem, []

    def start(self, source, target):
        copy = pltpu.make_async_copy(source, target, self.sem.at[len(self.made)])
        copy.start()
        self.made.append(copy)
        return copy

    def finish(self):
        for copy in self.made:
            copy.wait()


def greet(devices):
    barrier = pltpu.get_barrier_semaphore()
    for device in devices:
        pl.semaphore_signal(barrier, inc=1, device_id=device, device_id_type=pl.DeviceIdType.MESH)
    pl.semaphore_wait(barrier, len(devices))


def place_rows(row_ref, col_ref, place_row_ref, place_col_ref, mode_ref):
    rows = row_ref.shape[1]
    half = rows // 2
    chunk = LONG // 4
    by_row = one_hot(row_ref[...] == iota((LABELS, rows), 0))
    by_col = one_hot(col_ref[...] == iota((rows, LABELS), 1))
    count_col = jnp.sum(by_row.astype(F32), axis=1, keepdims=True)
    count_row = jnp.sum(by_col.astype(F32), axis=0, keepdims=True)
    cut = 0.5 * (chunk + IMAGE)
    long_col = jnp.where(count_col > cut, count_col, 0.0)
    long_row = jnp.where(count_row > cut, count_row, 0.0)
    small_col = count_col - long_col
    small_row = count_row - long_row
    total = jnp.sum(long_row, axis=1, keepdims=True)
    left = iota((LABELS, LABELS), 0)
    right = iota((LABELS, LABELS), 1)

    def before_col(counts):
        return jnp.sum(jnp.where(right < left, counts, 0.0), axis=1, keepdims=True)

    def before_row(counts):
        return jnp.sum(jnp.where(left < right, counts, 0.0), axis=0, keepdims=True)

    base_col = jnp.where(long_col > 0, before_col(long_row), total + before_col(small_row))
    base_row = jnp.where(long_row > 0, before_row(long_col), total + before_row(small_col))
    earlier = one_hot(iota((rows, rows), 0) < iota((rows, rows), 1))
    later = one_hot(iota((rows, rows), 1) < iota((rows, rows), 0))
    rank_row = dot(by_row, earlier)
    rank_col = dot(later, by_col)
    place_row = jnp.sum(by_row.astype(F32) * (rank_row + base_col), axis=0, keepdims=True)
    place_col = jnp.sum(by_col.astype(F32) * (rank_col + base_row), axis=1, keepdims=True)
    place_row = place_row.astype(jnp.int32)
    place_row_ref[0:1, :] = place_row[:, :half]
    place_row_ref[1:2, :] = place_row[:, half:]
    place_col_ref[...] = place_col.astype(jnp.int32)
    mode_ref[...] = jnp.broadcast_to(jnp.where(total > rows - IMAGE, 1.0, 0.0), mode_ref.shape)


def sort_into(place_ref, side, own_ref, other_ref, sorted_ref, cols):
    half = own_ref.shape[0]
    first = side == 0
    place_own = jnp.where(first, place_ref[0:1, :], place_ref[1:2, :])
    place_other = jnp.where(first, place_ref[1:2, :], place_ref[0:1, :])
    for part in range(2):
        target = iota((half, half), 0) + part * half
        rows = dot(one_hot(target == place_own), own_ref[:, cols])
        rows = rows + dot(one_hot(target == place_other), other_ref[:, cols])
        sorted_ref[part * half : (part + 1) * half, cols] = rows.astype(BF16)


def fill_sequence(part, seq, mode_ref, sorted_ref, got_ref, rows_ref):
    half = rows_ref.shape[0]
    chunk = half // 4
    home = sorted_ref[rows_at(part * half + seq * chunk, chunk), :]
    for step in range(4):
        rows = home if step == 0 else got_ref[part, step * chunk : (step + 1) * chunk, :]
        if part == 1:
            local = sorted_ref[half + step * chunk : half + (step + 1) * chunk, :]
            rows = jnp.where(mode_ref[0:1, 0:1] > 0, rows.astype(F32), local.astype(F32))
        rows_ref[step * chunk : (step + 1) * chunk, :] = rows.astype(BF16)


def image_mask(mode_ref, rows):
    same = lax.shift_right_logical(iota((rows, rows), 0), 6) == lax.shift_right_logical(
        iota((rows, rows), 1), 6
    )
    return jnp.where(same, 1.0, mode_ref[0:1, 0:1])


def project(part, rows_ref, weight_ref, vec_ref, kept, raw_ref):
    normed_ref, unit_ref, low_ref, value_ref, head_unit_ref, head_scale_ref = (
        ref.at[part] for ref in kept
    )
    half, width = rows_ref.shape
    inner = value_ref.shape[1]
    chunk = half // 4
    for step in range(4):
        rows = slice(step * chunk, (step + 1) * chunk)
        unit, _ = row_norm(rows_ref[rows, :].astype(F32))
        unit_ref[rows, :] = unit.astype(BF16)
        normed = unit * vec_ref[LN1_GAIN : LN1_GAIN + 1, :] + vec_ref[LN1_BIAS : LN1_BIAS + 1, :]
        normed_ref[rows, :] = normed.astype(BF16)
    raw_ref[:, :inner] = dot(normed_ref[...], weight_ref[0])
    raw_ref[:, inner:] = dot(normed_ref[...], weight_ref[1])
    value_ref[...] = dot(normed_ref[...], weight_ref[2]).astype(BF16)
    group = 4 * HEAD
    means = head_mean_matrix(group)
    for first in range(0, 2 * inner, group):
        cols = slice(first, first + group)
        raw = raw_ref[:, cols]
        centred = raw - two_part(raw, means)
        scale = lax.rsqrt(two_part(centred * centred, means) + EPSILON)
        unit = centred * scale
        head_unit_ref[:, cols] = unit
        head_scale_ref[:, cols] = scale
        low_ref[:, cols] = (unit * vec_ref[QK_GAIN : QK_GAIN + 1, cols]).astype(BF16)


def attend(part, kept, mask_ref, attended_ref):
    low_ref, value_ref = kept[2].at[part], kept[3].at[part]
    half, inner = value_ref.shape
    pair = 2 * HEAD
    lane = iota((half, pair), 1)

    def one_pair(index, carry):
        cols = pl.ds(pl.multiple_of(index * pair, pair), pair)
        key_cols = pl.ds(pl.multiple_of(inner + index * pair, pair), pair)
        query = low_ref[:, cols] * SCALE
        key = low_ref[:, key_cols]
        value = jnp.concatenate([value_ref[:, cols], jnp.ones((half, pair), BF16)], axis=1)
        found = []
        for head in range(2):
            mine = lane < HEAD if head == 0 else lane >= HEAD
            scores = dot_nt(jnp.where(mine, query, jnp.zeros_like(query)), key)
            weights = jnp.exp(scores).astype(BF16)
            if part == 1:
                weights = weights * mask_ref[...]
            both = dot(weights, value)
            found.append(both[:, :pair] / both[:, pair:])
        attended_ref[part, :, cols] = jnp.where(lane < HEAD, found[0], found[1]).astype(BF16)
        return carry

    lax.fori_loop(0, inner // pair, one_pair, 0)


KEPT = 6


def front_kernel(gathers, *refs):
    (tok_ref, cot_ref, row_ref, col_ref, vec_part_ref, qkv_ref, out_ref, fc1_ref, fc2_ref) = refs[:9]
    (
        tok_other_ref,
        cot_other_ref,
        place_row_ref,
        place_col_ref,
        mode_ref,
        vec_ref,
        mine_ref,
        theirs_ref,
        qkv_all_ref,
        out_all_ref,
        out_theirs_ref,
        fc1_all_ref,
        fc2_all_ref,
        out_pair_ref,
    ) = refs[9:23]
    kept_out = refs[23 : 23 + KEPT]
    (
        sorted_ref,
        got_ref,
        rows_ref,
        raw_ref,
        mask_ref,
        attended_ref,
        back_ref,
        vec_got_ref,
    ) = refs[23 + KEPT : 31 + KEPT]
    kept = refs[31 + KEPT : 31 + 2 * KEPT]
    send_sem, recv_sem, local_sem = refs[31 + 2 * KEPT :]
    pack, seq, side = lax.axis_index("dp"), lax.axis_index("seq"), lax.axis_index("hidden")
    core = lax.bitwise_and(seq, 1)
    half, width = tok_ref.shape
    chunk = half // 4
    steps = range(1, 4)
    across = {"hidden": 1 - side}
    seq_mate = [{"seq": other_of(seq, step)} for step in range(4)]
    pack_mate = [{"dp": other_of(pack, step)} for step in range(4)]
    greet([across] + seq_mate[1:] + (pack_mate[1:] if gathers else []))
    copies, locals_ = Copies(send_sem, recv_sem), Locals(local_sem)

    wide = width // 2
    pieces = [slice(0, wide), slice(wide, width)]
    tokens = [copies.start(tok_ref.at[:, c], tok_other_ref.at[:, c], across) for c in pieces]
    whole = fc1_ref.shape[0]
    in_flight = []

    def rows_of(ref, index, piece, size):
        rows = rows_at(index * whole + piece * size, size)
        return ref.at[:, rows, :] if len(ref.shape) == 3 else ref.at[rows, :]

    class Half:
        def __init__(self, source, target):
            self.target, self.size = target, whole // 2
            self.first = [
                copies.start(
                    rows_of(source, 0, core, self.size),
                    rows_of(target, pack, core, self.size),
                    pack_mate[k],
                )
                for k in steps
            ]

        def share(self):
            for k in steps:
                self.first[k - 1].wait_recv()
                there = rows_of(self.target, other_of(pack, k), core, self.size)
                in_flight.append(copies.start(there, there, seq_mate[1]))

    class Quarter:
        def __init__(self, source, target):
            self.target, self.size = target, whole // 4
            self.first = [
                copies.start(
                    rows_of(source, 0, seq, self.size),
                    rows_of(target, pack, seq, self.size),
                    pack_mate[k],
                )
                for k in steps
            ]
            self.second = []

        def there(self, k, piece):
            return rows_of(self.target, other_of(pack, k), piece, self.size)

        def pass_on(self):
            for k in steps:
                self.first[k - 1].wait_recv()
                there = self.there(k, seq)
                self.second.append(copies.start(there, there, seq_mate[2]))
            for k in steps:
                there = self.there(k, seq)
                in_flight.append(copies.start(there, there, seq_mate[1]))

        def share(self):
            for k in steps:
                self.second[k - 1].wait_recv()
                there = self.there(k, other_of(seq, 2))
                in_flight.append(copies.start(there, there, seq_mate[1]))

    if gathers:
        gather_vec = [copies.start(vec_part_ref, vec_got_ref.at[k - 1], pack_mate[k]) for k in steps]
        gather_qkv = Quarter(qkv_ref, qkv_all_ref)
        pair_out = copies.start(out_ref, out_pair_ref, across)
        gather_out = Half(out_ref, out_all_ref)
        gather_fc2 = Quarter(fc2_ref, fc2_all_ref)
        keep = [
            locals_.start(qkv_ref, qkv_all_ref.at[:, rows_at(pack * whole, whole), :]),
            locals_.start(out_ref, out_all_ref.at[rows_at(pack * whole, whole), :]),
            locals_.start(fc1_ref, fc1_all_ref.at[rows_at(pack * whole, whole), :]),
            locals_.start(fc2_ref, fc2_all_ref.at[rows_at(pack * whole, whole), :]),
        ]
    else:
        keep = [locals_.start(qkv_ref, qkv_all_ref)]
    place_rows(row_ref, col_ref, place_row_ref, place_col_ref, mode_ref)
    mask_ref[...] = image_mask(mode_ref, half).astype(BF16)

    if gathers:
        gather_qkv.pass_on()
    moved = [[], []]
    for piece, cols in enumerate(pieces):
        tokens[piece].wait_recv()
        sort_into(place_row_ref, side, tok_ref, tok_other_ref, sorted_ref, cols)
        for part in range(2):
            for k in steps:
                start = part * half + other_of(seq, k) * chunk
                moved[part].append(
                    copies.start(
                        sorted_ref.at[rows_at(start, chunk), cols],
                        got_ref.at[part, k * chunk : (k + 1) * chunk, cols],
                        seq_mate[k],
                    )
                )
    cots = copies.start(cot_ref, cot_other_ref, across)
    if gathers:
        pair_out.wait_recv()
        keep.append(locals_.start(out_pair_ref, out_theirs_ref.at[rows_at(pack * whole, whole), :]))
        gather_theirs = Half(out_pair_ref, out_theirs_ref)
        gather_fc1 = Half(fc1_ref, fc1_all_ref)
        gather_qkv.share()
        needed = list(in_flight)
        total = vec_part_ref[...]
        for k in steps:
            gather_vec[k - 1].wait_recv()
        vec_ref[...] = (total + vec_got_ref[0]) + (vec_got_ref[1] + vec_got_ref[2])
        for copy in needed:
            copy.wait_recv()
            in_flight.remove(copy)
    else:
        vec_ref[...] = vec_part_ref[...]
    keep[0].wait()

    def begin(part):
        for copy in moved[part]:
            copy.wait_recv()
        fill_sequence(part, seq, mode_ref, sorted_ref, got_ref, rows_ref)
        project(part, rows_ref, qkv_all_ref, vec_ref, kept, raw_ref)

    def give_back(part, target_ref):
        target_ref[rows_at(seq * chunk, chunk), :] = attended_ref[part, 0:chunk, :]
        given = [
            copies.start(
                attended_ref.at[part, k * chunk : (k + 1) * chunk, :],
                target_ref.at[rows_at(seq * chunk, chunk), :],
                seq_mate[k],
            )
            for k in steps
        ]
        for ref, out in zip(kept, kept_out):
            locals_.start(ref.at[part], out.at[part])
        return given

    begin(0)
    if gathers:
        gather_out.share()
        gather_fc2.pass_on()
    attend(0, kept, mask_ref, attended_ref)
    given = give_back(0, mine_ref)
    begin(1)
    for copy in given:
        copy.wait_recv()
    first = copies.start(mine_ref.at[0:half, :], theirs_ref.at[0:half, :], across)
    attend(1, kept, mask_ref, attended_ref)
    for copy in give_back(1, back_ref):
        copy.wait_recv()
    mine_ref[half:, :] = jnp.where(
        mode_ref[0:1, 0:1] > 0, back_ref[...].astype(F32), attended_ref[1].astype(F32)
    ).astype(BF16)
    second = copies.start(mine_ref.at[half : 2 * half, :], theirs_ref.at[half : 2 * half, :], across)
    if gathers:
        gather_theirs.share()
        gather_fc2.share()
        gather_fc1.share()
        for copy in in_flight:
            copy.wait_recv()
    cots.wait_recv()
    first.wait_recv()
    second.wait_recv()
    copies.finish()
    for copy in locals_.made[1:]:
        copy.wait()


def front(gathers, tokens, cotangent, labels, vectors, qkv, out, fc1, fc2, packs):
    half, width = tokens.shape
    rows = labels.shape[0]
    share, inner = out.shape
    units = fc1.shape[1]
    kept = [
        ((2, half, width), BF16),
        ((2, half, width), BF16),
        ((2, half, 2 * inner), BF16),
        ((2, half, inner), BF16),
        ((2, half, 2 * inner), F32),
        ((2, half, 2 * inner), F32),
    ]
    whole = width if gathers else share
    outs = [
        (shape((half, width)), VMEM),
        (shape((half, width)), HERE),
        (shape((2, half), jnp.int32), VMEM),
        (shape((rows, 1), jnp.int32), VMEM),
        (shape((8, 128), F32), VMEM),
        (shape((8, width), F32), VMEM),
        (shape((rows, inner)), VMEM),
        (shape((rows, inner)), VMEM),
        (shape((3, width, inner)), VMEM),
        (shape((whole, inner)), HERE),
        (shape((whole, inner)), HERE),
        (shape((whole, units)), HERE),
        (shape((whole, units)), HERE),
        (shape((share, inner)), HERE),
    ] + [(shape(dims, kind), HERE) for dims, kind in kept]
    copies = 2 + 12 + 1 + 6 + 2 + (3 + 1 + 2 * 12 + 3 * 6 if gathers else 0)
    return pl.pallas_call(
        functools.partial(front_kernel, gathers),
        out_shape=[o[0] for o in outs],
        in_specs=[VMEM, HERE, VMEM, VMEM, VMEM] + [HERE] * 4,
        out_specs=[o[1] for o in outs],
        scratch_shapes=[
            pltpu.VMEM((rows, width), BF16),
            pltpu.VMEM((2, half, width), BF16),
            pltpu.VMEM((half, width), BF16),
            pltpu.VMEM((half, 2 * inner), F32),
            pltpu.VMEM((half, half), BF16),
            pltpu.VMEM((2, half, inner), BF16),
            pltpu.VMEM((half, inner), BF16),
            pltpu.VMEM((3, 8, width), F32),
        ]
        + [pltpu.VMEM(dims, kind) for dims, kind in kept]
        + [
            pltpu.SemaphoreType.DMA((copies,)),
            pltpu.SemaphoreType.DMA((copies,)),
            pltpu.SemaphoreType.DMA((5 + 2 * KEPT,)),
        ],
        compiler_params=params(collective_id=0, has_side_effects=True),
        name="front",
    )(tokens, cotangent, labels.reshape(1, rows), labels.reshape(rows, 1), vectors, qkv, out, fc1, fc2)


def sort_kernel(here_ref, place_ref, own_ref, other_ref, *refs):
    sorted_refs, send_refs = refs[:2], refs[2:]
    half = own_ref.shape[0]
    seqs = len(send_refs) // 2 + 1
    chunk = half // seqs
    first = here_ref[1] == 0
    place_own = jnp.where(first, place_ref[0:1, :], place_ref[1:2, :])
    place_other = jnp.where(first, place_ref[1:2, :], place_ref[0:1, :])
    for part in range(2):
        target = iota((half, half), 0) + part * half
        rows = dot(one_hot(target == place_own), own_ref[...])
        rows = rows + dot(one_hot(target == place_other), other_ref[...])
        sorted_refs[part][...] = rows.astype(BF16)
        for step in range(1, seqs):
            start = pl.multiple_of((here_ref[0] ^ step) * chunk, 16)
            send_refs[part * (seqs - 1) + step - 1][...] = sorted_refs[part][pl.ds(start, chunk), :]


def sort_rows(here, place_row, own, other, seqs):
    half, width = own.shape
    chunk = half // seqs
    results = pl.pallas_call(
        sort_kernel,
        out_shape=[shape((half, width))] * 2 + [shape((chunk, width))] * (2 * (seqs - 1)),
        in_specs=[SMEM, VMEM, VMEM, VMEM],
        out_specs=[VMEM] * (2 * seqs),
        compiler_params=params(),
        name="sort_rows",
        cost_estimate=pl.CostEstimate(
            flops=8 * half * half * width, bytes_accessed=8 * half * width, transcendentals=0
        ),
    )(here, place_row, own, other)
    return results[:2], (results[2 : seqs + 1], results[seqs + 1 :])


def fill_back(here_ref, mode_ref, sorted_ref, got_refs, rows_ref, part):
    half = rows_ref.shape[0]
    chunk = half // (len(got_refs) + 1)
    home = sorted_ref[pl.ds(pl.multiple_of(here_ref[0] * chunk, 16), chunk), :]
    for step in range(len(got_refs) + 1):
        rows = home if step == 0 else got_refs[step - 1][...]
        if part == 1:
            local = sorted_ref[step * chunk : (step + 1) * chunk, :]
            rows = jnp.where(mode_ref[0:1, 0:1] > 0, rows.astype(F32), local.astype(F32)).astype(BF16)
        rows_ref[step * chunk : (step + 1) * chunk, :] = rows


def gather_kernel(here_ref, mode_ref, *refs):
    homes, gots, out_ref = refs[:2], refs[2:-1], refs[-1]
    half = out_ref.shape[0] // 2
    seqs = homes[0].shape[0]
    chunk = half // seqs
    for part in range(2):
        if part == 1:
            for step in range(seqs):
                out_ref[half + step * chunk : half + (step + 1) * chunk, :] = homes[1][step]
        for step in range(seqs):
            start = pl.multiple_of(part * half + (here_ref[0] ^ step) * chunk, 16)
            piece = homes[part].at[0] if step == 0 else gots[part * (seqs - 1) + step - 1]
            if part == 0:
                out_ref[pl.ds(start, chunk), :] = piece[...]
            else:

                local = out_ref[pl.ds(start, chunk), :].astype(F32)
                out_ref[pl.ds(start, chunk), :] = jnp.where(
                    mode_ref[0:1, 0:1] > 0, piece[...].astype(F32), local
                ).astype(BF16)


def gather_rows(here, mode, homes, gots):
    seqs, chunk, width = homes[0].shape
    flat = [homes[0], homes[1], *gots[0], *gots[1]]
    return pl.pallas_call(
        gather_kernel,
        out_shape=shape((2 * seqs * chunk, width)),
        in_specs=[SMEM, VMEM] + [VMEM] * len(flat),
        out_specs=VMEM,
        compiler_params=params(),
        name="gather_rows",
    )(here, mode, *flat)


def unsort_kernel(place_own_ref, place_other_ref, rows_ref, own_ref, other_ref):
    half = own_ref.shape[0]
    rows = rows_ref.shape[0]
    for place_ref, out_ref in ((place_other_ref, other_ref), (place_own_ref, own_ref)):
        out_ref[...] = dot(
            one_hot(place_ref[...] == iota((half, rows), 1)), rows_ref[...]
        ).astype(BF16)


def unsort_rows(place_own, place_other, rows):
    half, width = rows.shape[0] // 2, rows.shape[1]
    return pl.pallas_call(
        unsort_kernel,
        out_shape=(shape((half, width)),) * 2,
        in_specs=[VMEM] * 3,
        out_specs=(VMEM,) * 2,
        compiler_params=params(),
        name="unsort_rows",
        cost_estimate=pl.CostEstimate(
            flops=8 * half * half * width, bytes_accessed=8 * half * width, transcendentals=0
        ),
    )(place_own, place_other, rows)


def feed_kernel(
    own,
    token_ref,
    cot_ref,
    place_ref,
    mine_ref,
    theirs_ref,
    out_mine_ref,
    out_theirs_ref,
    fc1_ref,
    fc2_ref,
    vec_ref,
    act_ref,
    grad_hidden_ref,
    normed_ref,
    grad_ref,
    sum_ref,
    *more,
):
    tile = token_ref.shape[0]
    rows = mine_ref.shape[0]
    units = fc1_ref.shape[1]
    back = one_hot(place_ref[...] == iota((tile, rows), 1))
    mine = dot(back, mine_ref[...]).astype(BF16)
    theirs = dot(back, theirs_ref[...]).astype(BF16)
    mixed = (
        token_ref[...].astype(F32)
        + (dot_nt(mine, out_mine_ref[...]) + dot_nt(theirs, out_theirs_ref[...]))
        + vec_ref[OUT_BIAS : OUT_BIAS + 1, :]
    )
    unit, _ = row_norm(mixed)
    normed = unit * vec_ref[LN2_GAIN : LN2_GAIN + 1, :] + vec_ref[LN2_BIAS : LN2_BIAS + 1, :]
    normed = normed.astype(BF16)
    normed_ref[...] = normed
    cot = cot_ref[...]
    total = None
    step = 512
    for first in range(0, units, step):
        cols = slice(first, first + step)
        pre = dot(normed, fc1_ref[:, cols])
        grad_act = dot(cot, fc2_ref[:, cols])
        cdf, density = normal_cdf(pre)
        act_ref[:, cols] = (pre * cdf).astype(BF16)
        grad_hidden = (grad_act * (cdf + pre * density)).astype(BF16)
        grad_hidden_ref[:, cols] = grad_hidden
        add = dot_nt(grad_hidden, fc1_ref[:, cols])
        total = add if total is None else total + add
    grad_ref[...] = total.astype(grad_ref.dtype)

    @pl.when(pl.program_id(0) == 0)
    def _():
        sum_ref[...] = jnp.zeros_like(sum_ref)

    sum_ref[0:1, :] += jnp.sum(total * unit, axis=0, keepdims=True)
    sum_ref[1:2, :] += jnp.sum(total, axis=0, keepdims=True)
    if own:
        mixed_ref, attended_ref = more
        mixed_ref[...] = mixed
        attended_ref[:, : mine.shape[1]] = mine
        attended_ref[:, mine.shape[1] :] = theirs
        sum_ref[2:3, :] += jnp.sum(cot.astype(F32), axis=0, keepdims=True)


def feed_forward(own, token, cot, place, mine, theirs, out_mine, out_theirs, fc1, fc2, vectors):
    half, width = token.shape
    rows, inner = mine.shape
    units = fc1.shape[1]
    tile = half // 2
    by_row = lambda cols: pl.BlockSpec((tile, cols), lambda i: (i, 0))
    fixed = lambda array: pl.BlockSpec(array.shape, lambda i: (0,) * array.ndim)
    outs = [
        shape((half, units)),
        shape((half, units)),
        shape((half, width)),
        shape((half, width), F32 if own else BF16),
        shape((8, width), F32),
    ]
    out_specs = [
        by_row(units),
        by_row(units),
        by_row(width),
        by_row(width),
        pl.BlockSpec((8, width), lambda i: (0, 0)),
    ]
    if own:
        outs += [shape((half, width), F32), shape((half, 2 * inner))]
        out_specs += [by_row(width), by_row(2 * inner)]
    return pl.pallas_call(
        functools.partial(feed_kernel, own),
        out_shape=outs,
        grid=(half // tile,),
        in_specs=[by_row(width), by_row(width), by_row(1)]
        + [fixed(a) for a in (mine, theirs, out_mine, out_theirs, fc1, fc2, vectors)],
        out_specs=out_specs,
        compiler_params=params(dimension_semantics=("arbitrary",)),
        name="feed_own" if own else "feed_other",
        cost_estimate=pl.CostEstimate(
            flops=2 * half * width * (rows + width + 3 * units),
            bytes_accessed=4 * width * units + 12 * half * units,
            transcendentals=half * units,
        ),
    )(token, cot, place, mine, theirs, out_mine, out_theirs, fc1, fc2, vectors)


def mix_back_kernel(
    mixed_ref,
    here_ref,
    got_ref,
    cot_ref,
    out_mine_ref,
    out_theirs_ref,
    vec_ref,
    grad_mixed_ref,
    grad_attn_ref,
    mine_ref,
    theirs_ref,
    sum_ref,
):
    unit, scale = row_norm(mixed_ref[...])
    grad = here_ref[...] + got_ref[...].astype(F32)
    grad = row_norm_back(grad * vec_ref[LN2_GAIN : LN2_GAIN + 1, :], unit, scale)
    grad = grad + cot_ref[...].astype(F32)
    grad_mixed_ref[...] = grad
    low = grad.astype(BF16)
    grad_attn_ref[...] = low
    theirs_ref[...] = dot(low, out_theirs_ref[...]).astype(BF16)
    mine_ref[...] = dot(low, out_mine_ref[...]).astype(BF16)

    @pl.when(pl.program_id(0) == 0)
    def _():
        sum_ref[...] = jnp.zeros_like(sum_ref)

    sum_ref[0:1, :] += jnp.sum(low.astype(F32), axis=0, keepdims=True)


def mix_back(mixed, here, got, cot, out_mine, out_theirs, vectors):
    half, width = mixed.shape
    inner = out_mine.shape[1]
    tile = half // 2
    by_row = lambda cols: pl.BlockSpec((tile, cols), lambda i: (i, 0))
    fixed = lambda array: pl.BlockSpec(array.shape, lambda i: (0,) * array.ndim)
    return pl.pallas_call(
        mix_back_kernel,
        out_shape=(
            shape((half, width), F32),
            shape((half, width)),
            shape((half, inner)),
            shape((half, inner)),
            shape((8, width), F32),
        ),
        grid=(half // tile,),
        in_specs=[by_row(width)] * 4 + [fixed(a) for a in (out_mine, out_theirs, vectors)],
        out_specs=(
            by_row(width),
            by_row(width),
            by_row(inner),
            by_row(inner),
            pl.BlockSpec((8, width), lambda i: (0, 0)),
        ),
        compiler_params=params(dimension_semantics=("arbitrary",)),
        name="mix_back",
        cost_estimate=pl.CostEstimate(
            flops=2 * half * width * width, bytes_accessed=16 * half * width, transcendentals=0
        ),
    )(mixed, here, got, cot, out_mine, out_theirs, vectors)


def attend_back_kernel(part, here_ref, mode_ref, sorted_ref, *refs):
    got_refs, refs = refs[:3], refs[3:]
    (
        low_ref,
        value_ref,
        head_unit_ref,
        head_scale_ref,
        unit_ref,
        weight_ref,
        vec_ref,
        grad_low_ref,
        grad_normed_ref,
        sum_ref,
        rows_ref,
        raw_ref,
        mask_ref,
    ) = refs
    half, inner = rows_ref.shape
    chunk = half // 4
    fill_back(here_ref, mode_ref, sorted_ref, got_refs, rows_ref, part)
    pair = 2 * HEAD
    lane = iota((half, pair), 1)
    if part == 1:
        mask_ref[...] = image_mask(mode_ref, half)
    for first in range(0, inner, pair):
        query = low_ref[:, first : first + pair] * SCALE
        key = low_ref[:, inner + first : inner + first + pair]
        value = value_ref[:, first : first + pair]
        grad = rows_ref[:, first : first + pair]
        key_turned = (key.astype(F32) * SCALE).T.astype(BF16)
        grad_values, grad_keys, grad_queries = [], [], []
        for head in range(2):
            mine = lane < HEAD if head == 0 else lane >= HEAD
            query_head = jnp.where(mine, query, jnp.zeros_like(query))
            grad_head = jnp.where(mine, grad, jnp.zeros_like(grad))
            weights = jnp.exp(dot_nt(key, query_head))
            if part == 1:
                weights = weights * mask_ref[...]
            weights = weights * (1.0 / jnp.sum(weights, axis=0, keepdims=True))
            grad_weights = dot_nt(value, grad_head)
            shared = jnp.sum(weights * grad_weights, axis=0, keepdims=True)
            grad_scores = (weights * (grad_weights - shared)).astype(BF16)
            grad_values.append(dot(weights.astype(BF16), grad))
            grad_keys.append(dot(grad_scores, query))
            grad_queries.append(
                dot(key_turned[head * HEAD : (head + 1) * HEAD, :], grad_scores)
            )
        raw_ref[:, first : first + pair] = jnp.concatenate(grad_queries, axis=0).T
        raw_ref[:, inner + first : inner + first + pair] = jnp.where(
            lane < HEAD, grad_keys[0], grad_keys[1]
        )
        grad_low_ref[:, 2 * inner + first : 2 * inner + first + pair] = jnp.where(
            lane < HEAD, grad_values[0], grad_values[1]
        ).astype(BF16)
    group = 4 * HEAD
    means = head_mean_matrix(group)
    sum_ref[...] = jnp.zeros_like(sum_ref)
    for first in range(0, 2 * inner, group):
        cols = slice(first, first + group)
        grad = raw_ref[:, cols]
        unit = head_unit_ref[:, cols]
        sum_ref[2:3, cols] = jnp.sum(grad * unit, axis=0, keepdims=True)
        grad = grad * vec_ref[QK_GAIN : QK_GAIN + 1, cols]
        grad = head_scale_ref[:, cols] * (
            grad - two_part(grad, means) - unit * two_part(grad * unit, means)
        )
        grad_low_ref[:, cols] = grad.astype(BF16)
    total = dot_nt(grad_low_ref[:, :inner], weight_ref[0])
    total = total + dot_nt(grad_low_ref[:, inner : 2 * inner], weight_ref[1])
    total = total + dot_nt(grad_low_ref[:, 2 * inner :], weight_ref[2])
    sum_ref[0:1, :] = jnp.sum(total * unit_ref[...].astype(F32), axis=0, keepdims=True)
    sum_ref[1:2, :] = jnp.sum(total, axis=0, keepdims=True)
    for step in range(4):
        grad_normed_ref[step] = total[step * chunk : (step + 1) * chunk, :].astype(BF16)


def attend_back(part, here, mode, ordered, got, low, value, head_unit, head_scale, unit, weight, vectors):
    half, inner = ordered.shape
    seqs = len(got) + 1
    chunk = half // seqs
    width = unit.shape[1]
    return pl.pallas_call(
        functools.partial(attend_back_kernel, part),
        out_shape=(
            shape((half, 3 * inner)),
            shape((seqs, chunk, width)),
            shape((8, width), F32),
        ),
        in_specs=[SMEM] + [VMEM] * (seqs + 8),
        out_specs=(VMEM,) * 3,
        scratch_shapes=[
            pltpu.VMEM((half, inner), BF16),
            pltpu.VMEM((half, 2 * inner), F32),
            pltpu.VMEM((half, half), F32),
        ],
        compiler_params=params(),
        name="attend_back",
        cost_estimate=pl.CostEstimate(
            flops=2 * half * width * 3 * inner + 24 * half * half * inner,
            bytes_accessed=20 * half * width,
            transcendentals=half * half * inner // HEAD,
        ),
    )(here, mode, ordered, *got, low, value, head_unit, head_scale, unit, weight, vectors)


def norm_back_kernel(token_ref, own_ref, got_ref, grad_mixed_ref, vec_ref, out_ref):
    unit, scale = row_norm(token_ref[...].astype(F32))
    grad = own_ref[...].astype(F32) + got_ref[...].astype(F32)
    grad = row_norm_back(grad * vec_ref[LN1_GAIN : LN1_GAIN + 1, :], unit, scale)
    out_ref[...] = (grad_mixed_ref[...] + grad).astype(BF16)


def norm_back(token, own, got, grad_mixed, vectors):
    half, width = token.shape
    tile = half // 4
    by_row = pl.BlockSpec((tile, width), lambda i: (i, 0))
    return pl.pallas_call(
        norm_back_kernel,
        out_shape=shape((half, width)),
        grid=(half // tile,),
        in_specs=[by_row] * 4 + [pl.BlockSpec(vectors.shape, lambda i: (0, 0))],
        out_specs=by_row,
        compiler_params=params(dimension_semantics=("arbitrary",)),
        name="norm_back",
    )(token, own, got, grad_mixed, vectors)


def swap(array, axis, step):
    pairs = [(index, index ^ step) for index in range(lax.axis_size(axis))]
    return lax.ppermute(array, axis, pairs)


def owned_sum(part, dim):
    total = lax.psum_scatter(part.astype(BF16), "dp", scatter_dimension=dim, tiled=True)
    total = (total.astype(F32) + swap(total, "seq", 1).astype(F32)).astype(BF16)
    return total.astype(F32) + swap(total, "seq", 2).astype(F32)


def local(
    tokens,
    segment,
    cotangent,
    ln1_gain,
    ln1_bias,
    qkv_weight,
    qk_gain,
    out_weight,
    out_bias,
    ln2_gain,
    ln2_bias,
    fc1_weight,
    fc2_weight,
    fc2_bias,
):
    half, width = tokens.shape
    quarter = half * lax.axis_size("hidden")
    seqs = lax.axis_size("seq")
    packs = lax.axis_size("dp")
    inner = qkv_weight.shape[2]
    heads = inner // HEAD
    seq, side = lax.axis_index("seq"), lax.axis_index("hidden")
    here = jnp.stack([seq, side]).astype(jnp.int32)

    share = ln1_gain.shape[0]
    gathers = packs == 4
    lanes = jnp.arange(width)
    pieces = jnp.stack([ln1_gain, ln1_bias, out_bias, ln2_gain, ln2_bias, fc2_bias]).astype(F32)
    pack = lax.axis_index("dp")
    vectors = jnp.where(lanes // share == pack, jnp.tile(pieces, (1, packs)), 0.0)
    gains = jnp.tile(qk_gain.astype(F32), (1, width // (2 * qk_gain.shape[1]))).reshape(1, width)
    gains = jnp.where(lanes % HEAD // qk_gain.shape[1] == pack, gains, 0.0)
    vectors = jnp.concatenate([vectors, gains, jnp.zeros((1, width), F32)], axis=0)
    if not gathers:
        vectors = lax.psum(vectors, "dp")
        qkv_weight = lax.all_gather(qkv_weight, "dp", axis=1, tiled=True)
    labels = lax.dynamic_slice_in_dim(segment, seq * quarter, quarter, 0)
    (
        tokens_other,
        cot_other,
        place_row,
        place_col,
        mode,
        vectors,
        mine,
        theirs,
        qkv_full,
        out_mine,
        out_theirs,
        fc1_full,
        fc2_full,
        _,
        *kept,
    ) = front(
        gathers, tokens, cotangent, labels, vectors, qkv_weight, out_weight.T, fc1_weight,
        fc2_weight.T, packs,
    )
    if not gathers:
        out_mine = lax.all_gather(out_weight.T, "dp", axis=0, tiled=True)
        out_theirs = swap(out_mine, "hidden", 1)
        fc1_full = lax.all_gather(fc1_weight, "dp", axis=0, tiled=True)
        fc2_full = lax.all_gather(fc2_weight.T, "dp", axis=0, tiled=True)
    kept = [[array[part] for array in kept] for part in range(2)]
    place_own = lax.dynamic_slice_in_dim(place_col, side * half, half, 0)
    place_other = lax.dynamic_slice_in_dim(place_col, (1 - side) * half, half, 0)

    feed = (mine, theirs, out_mine, out_theirs, fc1_full, fc2_full, vectors)
    act_other, hidden_other, normed_other, grad_other, sums_other = feed_forward(
        False, tokens_other, cot_other, place_other, *feed
    )
    grad_got = swap(grad_other, "hidden", 1)
    act_own, hidden_own, normed_own, grad_own, sums_own, mixed, attended_own = feed_forward(
        True, tokens, cotangent, place_own, *feed
    )

    grad_mixed, grad_attn, mine_back, theirs_back, sums_mix = mix_back(
        mixed, grad_own, grad_got, cotangent, out_mine, out_theirs, vectors
    )
    back_got = swap(theirs_back, "hidden", 1)
    result_got = swap(dot_nt(act_other, fc2_full).astype(BF16), "hidden", 1)
    result = dot_nt(act_own, fc2_full) + mixed + vectors[FC2_BIAS][None, :]
    output = (result + result_got.astype(F32)).astype(BF16)
    fc2_part = dot_tn(cotangent, act_own) + dot_tn(cot_other, act_other)
    fc1_part = dot_tn(normed_own, hidden_own) + dot_tn(normed_other, hidden_other)
    fc2_owned = owned_sum(fc2_part, 0).T
    fc1_owned = owned_sum(fc1_part, 0)
    out_both = dot_tn(grad_attn, attended_own)
    out_part = out_both[:, :inner] + swap(out_both[:, inner:].astype(BF16), "hidden", 1).astype(F32)
    out_owned = owned_sum(out_part, 0).T

    ordered_back, sends_back = sort_rows(here, place_row, mine_back, back_got, seqs)
    got_back = [[swap(send, "seq", step + 1) for step, send in enumerate(part)] for part in sends_back]
    grads, homes, returned, sums_heads = [], [], [], []
    for part in range(2):
        normed, unit, low, value, head_unit, head_scale = kept[part]
        grad_low, grad_normed, sums = attend_back(
            part, here, mode, ordered_back[part], got_back[part], low, value, head_unit, head_scale, unit,
            qkv_full, vectors,
        )
        grads.append(grad_low)
        homes.append(grad_normed)
        sums_heads.append(sums)
        returned.append([swap(grad_normed[step], "seq", step) for step in range(1, seqs)])
    qkv_part = dot_tn(kept[0][0], grads[0]) + dot_tn(kept[1][0], grads[1])
    qkv_part = jnp.moveaxis(qkv_part.reshape(width, 3, inner), 1, 0)
    qkv_owned = owned_sum(qkv_part, 1)

    heads_sum = sums_heads[0] + sums_heads[1]
    sums_feed = sums_own + sums_other
    qk_sum = heads_sum[2].reshape(2, heads, HEAD).sum(axis=1)
    small = jnp.concatenate(
        [
            jnp.stack(
                [heads_sum[0], heads_sum[1], sums_mix[0], sums_feed[0], sums_feed[1], sums_feed[2]]
            ).reshape(6, packs, share).swapaxes(0, 1).reshape(packs, 6 * share),
            qk_sum.reshape(2, packs, HEAD // packs).swapaxes(0, 1).reshape(packs, -1),
        ],
        axis=1,
    )
    small = small + swap(small, "hidden", 1)
    small = small + swap(small, "seq", 1)
    small = small + swap(small, "seq", 2)
    small = lax.psum_scatter(small, "dp", scatter_dimension=0, tiled=True)[0]
    vec = small[: 6 * share].reshape(6, share)
    qk_owned = small[6 * share :].reshape(2, HEAD // packs)

    back = gather_rows(here, mode, homes, returned)
    back_own, back_other = unsort_rows(place_own, place_other, back)
    back_got = swap(back_other, "hidden", 1)
    input_grad = norm_back(tokens, back_own, back_got, grad_mixed, vectors)
    return (
        output,
        input_grad,
        vec[0],
        vec[1],
        qkv_owned,
        qk_owned,
        out_owned,
        vec[2],
        vec[3],
        vec[4],
        fc1_owned,
        fc2_owned,
        vec[5],
    )


def solution(mesh):
    rows = P(("dp", "seq", "hidden"), None)
    in_specs = (
        rows,
        P("dp"),
        rows,
        P("dp"),
        P("dp"),
        P(None, "dp", "hidden"),
        P(None, "dp"),
        P("hidden", "dp"),
        P("dp"),
        P("dp"),
        P("dp"),
        P("dp", "hidden"),
        P("hidden", "dp"),
        P("dp"),
    )
    out_specs = (
        rows,
        rows,
        P("dp"),
        P("dp"),
        P(None, "dp", "hidden"),
        P(None, "dp"),
        P("hidden", "dp"),
        P("dp"),
        P("dp"),
        P("dp"),
        P("dp", "hidden"),
        P("hidden", "dp"),
        P("dp"),
    )
    return jax.shard_map(local, mesh=mesh, in_specs=in_specs, out_specs=out_specs, check_vma=False)
```

```python
import functools

import jax
import jax.numpy as jnp
from jax import lax
from jax.experimental import pallas as pl
from jax.experimental.pallas import tpu as pltpu
from jax.sharding import PartitionSpec as P

HEAD = 64
LONG = 576
IMAGE = 64
LABELS = 128
EPSILON = 1e-06
SCALE = HEAD ** (-0.5)
F32 = jnp.float32
BF16 = jnp.bfloat16

VMEM = pl.BlockSpec(memory_space=pltpu.VMEM)
SMEM = pl.BlockSpec(memory_space=pltpu.SMEM)
HERE = pl.BlockSpec(memory_space=pl.ANY)
LN1_GAIN, LN1_BIAS, OUT_BIAS, LN2_GAIN, LN2_BIAS, FC2_BIAS, QK_GAIN = range(7)


def params(limit=56 << 20, **more):
    return pltpu.CompilerParams(vmem_limit_bytes=limit, **more)


def shape(dims, dtype=BF16):
    return jax.ShapeDtypeStruct(dims, dtype)


def dot(left, right):
    return jnp.dot(left, right, preferred_element_type=F32)


def dot_nt(left, right):
    return lax.dot_general(left, right, (((1,), (1,)), ((), ())), preferred_element_type=F32)


def dot_tn(left, right):
    return lax.dot_general(left, right, (((0,), (0,)), ((), ())), preferred_element_type=F32)


def iota(dims, dim):
    return lax.broadcasted_iota(jnp.int32, dims, dim)


def one_hot(test):
    return jnp.where(test, 1.0, 0.0).astype(BF16)


def two_part(values, matrix):
    high = values.astype(BF16)
    rest = (values - high.astype(F32)).astype(BF16)
    return dot(high, matrix) + dot(rest, matrix)


def head_mean_matrix(width):
    return jnp.where(
        iota((width, width), 0) // HEAD == iota((width, width), 1) // HEAD, 1.0 / HEAD, 0.0
    ).astype(BF16)


def row_norm(values):
    mean = jnp.mean(values, axis=-1, keepdims=True)
    centred = values - mean
    spread = jnp.mean(centred * centred, axis=-1, keepdims=True)
    scale = lax.rsqrt(spread + EPSILON)
    return centred * scale, scale


def row_norm_back(grad_unit, unit, scale):
    first = jnp.mean(grad_unit, axis=-1, keepdims=True)
    second = jnp.mean(grad_unit * unit, axis=-1, keepdims=True)
    return scale * (grad_unit - first - unit * second)


def normal_cdf(values):
    size = jnp.abs(values) * (2.0 ** -0.5)
    bell = jnp.exp(-0.5 * values * values)
    t = 1.0 / (1.0 + 0.3275911 * size)
    poly = 1.061405429 * t - 1.453152027
    poly = poly * t + 1.421413741
    poly = poly * t - 0.284496736
    poly = poly * t + 0.254829592
    tail = 0.5 * (poly * t) * bell
    return jnp.where(values < 0, tail, 1.0 - tail), bell * 0.3989422804014327


def other_of(value, step):
    return lax.bitwise_xor(value, jnp.int32(step))


def rows_at(start, size):
    return pl.ds(pl.multiple_of(start, 16), size)


class Copies:
    def __init__(self, send_sem, recv_sem):
        self.send_sem, self.recv_sem = send_sem, recv_sem
        self.made = []

    def start(self, source, target, device):
        index = len(self.made)
        copy = pltpu.make_async_remote_copy(
            src_ref=source,
            dst_ref=target,
            send_sem=self.send_sem.at[index],
            recv_sem=self.recv_sem.at[index],
            device_id=device,
            device_id_type=pl.DeviceIdType.MESH,
        )
        copy.start()
        self.made.append(copy)
        return copy

    def finish(self):
        for copy in self.made:
            copy.wait_send()


class Locals:
    def __init__(self, sem):
        self.sem, self.made = sem, []

    def start(self, source, target):
        copy = pltpu.make_async_copy(source, target, self.sem.at[len(self.made)])
        copy.start()
        self.made.append(copy)
        return copy

    def finish(self):
        for copy in self.made:
            copy.wait()


def greet(devices):
    barrier = pltpu.get_barrier_semaphore()
    for device in devices:
        pl.semaphore_signal(barrier, inc=1, device_id=device, device_id_type=pl.DeviceIdType.MESH)
    pl.semaphore_wait(barrier, len(devices))


def place_rows(row_ref, col_ref, place_row_ref, place_col_ref, mode_ref):
    rows = row_ref.shape[1]
    half = rows // 2
    chunk = LONG // 4
    by_row = one_hot(row_ref[...] == iota((LABELS, rows), 0))
    by_col = one_hot(col_ref[...] == iota((rows, LABELS), 1))
    count_col = jnp.sum(by_row.astype(F32), axis=1, keepdims=True)
    count_row = jnp.sum(by_col.astype(F32), axis=0, keepdims=True)
    cut = 0.5 * (chunk + IMAGE)
    long_col = jnp.where(count_col > cut, count_col, 0.0)
    long_row = jnp.where(count_row > cut, count_row, 0.0)
    small_col = count_col - long_col
    small_row = count_row - long_row
    total = jnp.sum(long_row, axis=1, keepdims=True)
    left = iota((LABELS, LABELS), 0)
    right = iota((LABELS, LABELS), 1)

    def before_col(counts):
        return jnp.sum(jnp.where(right < left, counts, 0.0), axis=1, keepdims=True)

    def before_row(counts):
        return jnp.sum(jnp.where(left < right, counts, 0.0), axis=0, keepdims=True)

    base_col = jnp.where(long_col > 0, before_col(long_row), total + before_col(small_row))
    base_row = jnp.where(long_row > 0, before_row(long_col), total + before_row(small_col))
    earlier = one_hot(iota((rows, rows), 0) < iota((rows, rows), 1))
    later = one_hot(iota((rows, rows), 1) < iota((rows, rows), 0))
    rank_row = dot(by_row, earlier)
    rank_col = dot(later, by_col)
    place_row = jnp.sum(by_row.astype(F32) * (rank_row + base_col), axis=0, keepdims=True)
    place_col = jnp.sum(by_col.astype(F32) * (rank_col + base_row), axis=1, keepdims=True)
    place_row = place_row.astype(jnp.int32)
    place_row_ref[0:1, :] = place_row[:, :half]
    place_row_ref[1:2, :] = place_row[:, half:]
    place_col_ref[...] = place_col.astype(jnp.int32)
    mode_ref[...] = jnp.broadcast_to(jnp.where(total > rows - IMAGE, 1.0, 0.0), mode_ref.shape)


def sort_into(place_ref, side, own_ref, other_ref, sorted_ref, cols):
    half = own_ref.shape[0]
    first = side == 0
    place_own = jnp.where(first, place_ref[0:1, :], place_ref[1:2, :])
    place_other = jnp.where(first, place_ref[1:2, :], place_ref[0:1, :])
    for part in range(2):
        target = iota((half, half), 0) + part * half
        rows = dot(one_hot(target == place_own), own_ref[:, cols])
        rows = rows + dot(one_hot(target == place_other), other_ref[:, cols])
        sorted_ref[part * half : (part + 1) * half, cols] = rows.astype(BF16)


def fill_sequence(part, seq, mode_ref, sorted_ref, got_ref, rows_ref):
    half = rows_ref.shape[0]
    chunk = half // 4
    home = sorted_ref[rows_at(part * half + seq * chunk, chunk), :]
    for step in range(4):
        rows = home if step == 0 else got_ref[part, step * chunk : (step + 1) * chunk, :]
        if part == 1:
            local = sorted_ref[half + step * chunk : half + (step + 1) * chunk, :]
            rows = jnp.where(mode_ref[0:1, 0:1] > 0, rows.astype(F32), local.astype(F32))
        rows_ref[step * chunk : (step + 1) * chunk, :] = rows.astype(BF16)


def image_mask(mode_ref, rows):
    same = lax.shift_right_logical(iota((rows, rows), 0), 6) == lax.shift_right_logical(
        iota((rows, rows), 1), 6
    )
    return jnp.where(same, 1.0, mode_ref[0:1, 0:1])


def project(part, rows_ref, weight_ref, vec_ref, kept, raw_ref):
    normed_ref, unit_ref, low_ref, value_ref, head_unit_ref, head_scale_ref = (
        ref.at[part] for ref in kept
    )
    half, width = rows_ref.shape
    inner = value_ref.shape[1]
    chunk = half // 4
    for step in range(4):
        rows = slice(step * chunk, (step + 1) * chunk)
        unit, _ = row_norm(rows_ref[rows, :].astype(F32))
        unit_ref[rows, :] = unit.astype(BF16)
        normed = unit * vec_ref[LN1_GAIN : LN1_GAIN + 1, :] + vec_ref[LN1_BIAS : LN1_BIAS + 1, :]
        normed_ref[rows, :] = normed.astype(BF16)
    raw_ref[:, :inner] = dot(normed_ref[...], weight_ref[0])
    raw_ref[:, inner:] = dot(normed_ref[...], weight_ref[1])
    value_ref[...] = dot(normed_ref[...], weight_ref[2]).astype(BF16)
    group = 4 * HEAD
    means = head_mean_matrix(group)
    for first in range(0, 2 * inner, group):
        cols = slice(first, first + group)
        raw = raw_ref[:, cols]
        centred = raw - two_part(raw, means)
        scale = lax.rsqrt(two_part(centred * centred, means) + EPSILON)
        unit = centred * scale
        head_unit_ref[:, cols] = unit
        head_scale_ref[:, cols] = scale
        low_ref[:, cols] = (unit * vec_ref[QK_GAIN : QK_GAIN + 1, cols]).astype(BF16)


def attend(part, kept, mask_ref, attended_ref):
    low_ref, value_ref = kept[2].at[part], kept[3].at[part]
    half, inner = value_ref.shape
    pair = 2 * HEAD
    lane = iota((half, pair), 1)

    def one_pair(index, carry):
        cols = pl.ds(pl.multiple_of(index * pair, pair), pair)
        key_cols = pl.ds(pl.multiple_of(inner + index * pair, pair), pair)
        query = low_ref[:, cols] * SCALE
        key = low_ref[:, key_cols]
        value = jnp.concatenate([value_ref[:, cols], jnp.ones((half, pair), BF16)], axis=1)
        found = []
        for head in range(2):
            mine = lane < HEAD if head == 0 else lane >= HEAD
            scores = dot_nt(jnp.where(mine, query, jnp.zeros_like(query)), key)
            weights = jnp.exp(scores).astype(BF16)
            if part == 1:
                weights = weights * mask_ref[...]
            both = dot(weights, value)
            found.append(both[:, :pair] / both[:, pair:])
        attended_ref[part, :, cols] = jnp.where(lane < HEAD, found[0], found[1]).astype(BF16)
        return carry

    lax.fori_loop(0, inner // pair, one_pair, 0)


KEPT = 6


def front_kernel(gathers, *refs):
    (tok_ref, cot_ref, row_ref, col_ref, vec_part_ref, qkv_ref, out_ref, fc1_ref, fc2_ref) = refs[:9]
    (
        tok_other_ref,
        cot_other_ref,
        place_row_ref,
        place_col_ref,
        mode_ref,
        vec_ref,
        mine_ref,
        theirs_ref,
        qkv_all_ref,
        out_all_ref,
        out_theirs_ref,
        fc1_all_ref,
        fc2_all_ref,
        out_pair_ref,
    ) = refs[9:23]
    kept_out = refs[23 : 23 + KEPT]
    (
        sorted_ref,
        got_ref,
        rows_ref,
        raw_ref,
        mask_ref,
        attended_ref,
        back_ref,
        vec_got_ref,
    ) = refs[23 + KEPT : 31 + KEPT]
    kept = refs[31 + KEPT : 31 + 2 * KEPT]
    send_sem, recv_sem, local_sem = refs[31 + 2 * KEPT :]
    pack, seq, side = lax.axis_index("dp"), lax.axis_index("seq"), lax.axis_index("hidden")
    core = lax.bitwise_and(seq, 1)
    half, width = tok_ref.shape
    chunk = half // 4
    steps = range(1, 4)
    across = {"hidden": 1 - side}
    seq_mate = [{"seq": other_of(seq, step)} for step in range(4)]
    pack_mate = [{"dp": other_of(pack, step)} for step in range(4)]
    greet([across] + seq_mate[1:] + (pack_mate[1:] if gathers else []))
    copies, locals_ = Copies(send_sem, recv_sem), Locals(local_sem)

    wide = width // 2
    pieces = [slice(0, wide), slice(wide, width)]
    tokens = [copies.start(tok_ref.at[:, c], tok_other_ref.at[:, c], across) for c in pieces]
    whole = fc1_ref.shape[0]
    in_flight = []

    def rows_of(ref, index, piece, size):
        rows = rows_at(index * whole + piece * size, size)
        return ref.at[:, rows, :] if len(ref.shape) == 3 else ref.at[rows, :]

    class Half:
        def __init__(self, source, target):
            self.target, self.size = target, whole // 2
            self.first = [
                copies.start(
                    rows_of(source, 0, core, self.size),
                    rows_of(target, pack, core, self.size),
                    pack_mate[k],
                )
                for k in steps
            ]

        def share(self):
            for k in steps:
                self.first[k - 1].wait_recv()
                there = rows_of(self.target, other_of(pack, k), core, self.size)
                in_flight.append(copies.start(there, there, seq_mate[1]))

    class Quarter:
        def __init__(self, source, target):
            self.target, self.size = target, whole // 4
            self.first = [
                copies.start(
                    rows_of(source, 0, seq, self.size),
                    rows_of(target, pack, seq, self.size),
                    pack_mate[k],
                )
                for k in steps
            ]
            self.second = []

        def there(self, k, piece):
            return rows_of(self.target, other_of(pack, k), piece, self.size)

        def pass_on(self):
            for k in steps:
                self.first[k - 1].wait_recv()
                there = self.there(k, seq)
                self.second.append(copies.start(there, there, seq_mate[2]))
            for k in steps:
                there = self.there(k, seq)
                in_flight.append(copies.start(there, there, seq_mate[1]))

        def share(self):
            for k in steps:
                self.second[k - 1].wait_recv()
                there = self.there(k, other_of(seq, 2))
                in_flight.append(copies.start(there, there, seq_mate[1]))

    if gathers:
        gather_vec = [copies.start(vec_part_ref, vec_got_ref.at[k - 1], pack_mate[k]) for k in steps]
        gather_qkv = Quarter(qkv_ref, qkv_all_ref)
        pair_out = copies.start(out_ref, out_pair_ref, across)
        gather_out = Half(out_ref, out_all_ref)
        gather_fc2 = Quarter(fc2_ref, fc2_all_ref)
        keep = [
            locals_.start(qkv_ref, qkv_all_ref.at[:, rows_at(pack * whole, whole), :]),
            locals_.start(out_ref, out_all_ref.at[rows_at(pack * whole, whole), :]),
            locals_.start(fc1_ref, fc1_all_ref.at[rows_at(pack * whole, whole), :]),
            locals_.start(fc2_ref, fc2_all_ref.at[rows_at(pack * whole, whole), :]),
        ]
    else:
        keep = [locals_.start(qkv_ref, qkv_all_ref)]
    place_rows(row_ref, col_ref, place_row_ref, place_col_ref, mode_ref)
    mask_ref[...] = image_mask(mode_ref, half).astype(BF16)

    if gathers:
        gather_qkv.pass_on()
    moved = [[], []]
    for piece, cols in enumerate(pieces):
        tokens[piece].wait_recv()
        sort_into(place_row_ref, side, tok_ref, tok_other_ref, sorted_ref, cols)
        for part in range(2):
            for k in steps:
                start = part * half + other_of(seq, k) * chunk
                moved[part].append(
                    copies.start(
                        sorted_ref.at[rows_at(start, chunk), cols],
                        got_ref.at[part, k * chunk : (k + 1) * chunk, cols],
                        seq_mate[k],
                    )
                )
    cots = copies.start(cot_ref, cot_other_ref, across)
    if gathers:
        pair_out.wait_recv()
        keep.append(locals_.start(out_pair_ref, out_theirs_ref.at[rows_at(pack * whole, whole), :]))
        gather_theirs = Half(out_pair_ref, out_theirs_ref)
        gather_fc1 = Half(fc1_ref, fc1_all_ref)
        gather_qkv.share()
        needed = list(in_flight)
        total = vec_part_ref[...]
        for k in steps:
            gather_vec[k - 1].wait_recv()
        vec_ref[...] = (total + vec_got_ref[0]) + (vec_got_ref[1] + vec_got_ref[2])
        for copy in needed:
            copy.wait_recv()
            in_flight.remove(copy)
    else:
        vec_ref[...] = vec_part_ref[...]
    keep[0].wait()

    def begin(part):
        for copy in moved[part]:
            copy.wait_recv()
        fill_sequence(part, seq, mode_ref, sorted_ref, got_ref, rows_ref)
        project(part, rows_ref, qkv_all_ref, vec_ref, kept, raw_ref)

    def give_back(part, target_ref):
        target_ref[rows_at(seq * chunk, chunk), :] = attended_ref[part, 0:chunk, :]
        given = [
            copies.start(
                attended_ref.at[part, k * chunk : (k + 1) * chunk, :],
                target_ref.at[rows_at(seq * chunk, chunk), :],
                seq_mate[k],
            )
            for k in steps
        ]
        for ref, out in zip(kept, kept_out):
            locals_.start(ref.at[part], out.at[part])
        return given

    begin(0)
    if gathers:
        gather_out.share()
        gather_fc2.pass_on()
    attend(0, kept, mask_ref, attended_ref)
    given = give_back(0, mine_ref)
    begin(1)
    for copy in given:
        copy.wait_recv()
    first = copies.start(mine_ref.at[0:half, :], theirs_ref.at[0:half, :], across)
    attend(1, kept, mask_ref, attended_ref)
    for copy in give_back(1, back_ref):
        copy.wait_recv()
    mine_ref[half:, :] = jnp.where(
        mode_ref[0:1, 0:1] > 0, back_ref[...].astype(F32), attended_ref[1].astype(F32)
    ).astype(BF16)
    second = copies.start(mine_ref.at[half : 2 * half, :], theirs_ref.at[half : 2 * half, :], across)
    if gathers:
        gather_theirs.share()
        gather_fc2.share()
        gather_fc1.share()
        for copy in in_flight:
            copy.wait_recv()
    cots.wait_recv()
    first.wait_recv()
    second.wait_recv()
    copies.finish()
    for copy in locals_.made[1:]:
        copy.wait()


def front(gathers, tokens, cotangent, labels, vectors, qkv, out, fc1, fc2, packs):
    half, width = tokens.shape
    rows = labels.shape[0]
    share, inner = out.shape
    units = fc1.shape[1]
    kept = [
        ((2, half, width), BF16),
        ((2, half, width), BF16),
        ((2, half, 2 * inner), BF16),
        ((2, half, inner), BF16),
        ((2, half, 2 * inner), F32),
        ((2, half, 2 * inner), F32),
    ]
    whole = width if gathers else share
    outs = [
        (shape((half, width)), VMEM),
        (shape((half, width)), HERE),
        (shape((2, half), jnp.int32), VMEM),
        (shape((rows, 1), jnp.int32), VMEM),
        (shape((8, 128), F32), VMEM),
        (shape((8, width), F32), VMEM),
        (shape((rows, inner)), VMEM),
        (shape((rows, inner)), VMEM),
        (shape((3, width, inner)), VMEM),
        (shape((whole, inner)), HERE),
        (shape((whole, inner)), HERE),
        (shape((whole, units)), HERE),
        (shape((whole, units)), HERE),
        (shape((share, inner)), HERE),
    ] + [(shape(dims, kind), HERE) for dims, kind in kept]
    copies = 2 + 12 + 1 + 6 + 2 + (3 + 1 + 2 * 12 + 3 * 6 if gathers else 0)
    return pl.pallas_call(
        functools.partial(front_kernel, gathers),
        out_shape=[o[0] for o in outs],
        in_specs=[VMEM, HERE, VMEM, VMEM, VMEM] + [HERE] * 4,
        out_specs=[o[1] for o in outs],
        scratch_shapes=[
            pltpu.VMEM((rows, width), BF16),
            pltpu.VMEM((2, half, width), BF16),
            pltpu.VMEM((half, width), BF16),
            pltpu.VMEM((half, 2 * inner), F32),
            pltpu.VMEM((half, half), BF16),
            pltpu.VMEM((2, half, inner), BF16),
            pltpu.VMEM((half, inner), BF16),
            pltpu.VMEM((3, 8, width), F32),
        ]
        + [pltpu.VMEM(dims, kind) for dims, kind in kept]
        + [
            pltpu.SemaphoreType.DMA((copies,)),
            pltpu.SemaphoreType.DMA((copies,)),
            pltpu.SemaphoreType.DMA((5 + 2 * KEPT,)),
        ],
        compiler_params=params(collective_id=0, has_side_effects=True),
        name="front",
    )(tokens, cotangent, labels.reshape(1, rows), labels.reshape(rows, 1), vectors, qkv, out, fc1, fc2)


def middle_kernel(*refs):
    (
        tok_ref,
        tok_other_ref,
        cot_ref,
        cot_other_ref,
        place_ref,
        mine_ref,
        theirs_ref,
        vec_ref,
        out_mine_ref,
        out_theirs_ref,
        fc1_all_ref,
        fc2_all_ref,
    ) = refs[:12]
    (
        grad_mixed_out,
        back_mine_ref,
        back_got_ref,
        result_out,
        result_other_out,
        fc1_out,
        fc2_out,
        out_out,
        sum_ref,
    ) = refs[12:21]
    (
        fc1_ref,
        fc2_ref,
        act_ref,
        hidden_ref,
        normed_ref,
        grad_other_ref,
        grad_got_ref,
        grad_own_ref,
        mixed_ref,
        attended_ref,
        back_theirs_ref,
        low_ref,
        turned_ref,
        grad_mixed_ref,
        result_ref,
        result_other_ref,
        fc1_part_ref,
        fc2_part_ref,
        out_part_ref,
        send_sem,
        recv_sem,
        local_sem,
    ) = refs[21:]
    half, width = tok_ref.shape
    rows, inner = mine_ref.shape
    units = fc1_ref.shape[1]
    side = lax.axis_index("hidden")
    across = {"hidden": 1 - side}
    copies, locals_ = Copies(send_sem, recv_sem), Locals(local_sem)
    load_fc1 = locals_.start(fc1_all_ref, fc1_ref)
    load_fc2 = locals_.start(fc2_all_ref, fc2_ref)
    greet([across])
    tiles = 2
    tile = half // tiles
    spans = [slice(index * tile, (index + 1) * tile) for index in range(tiles)]
    sum_ref[...] = jnp.zeros_like(sum_ref)

    def feed(own, index):
        block, span = (0 if own else 1), spans[index]
        start = (side if own else 1 - side) * half + index * tile
        place = place_ref[pl.ds(pl.multiple_of(start, 16), tile), :]
        back = one_hot(place == iota((tile, rows), 1))
        mine = dot(back, mine_ref[...]).astype(BF16)
        theirs = dot(back, theirs_ref[...]).astype(BF16)
        tok = (tok_ref if own else tok_other_ref)[span, :]
        cot = (cot_ref if own else cot_other_ref)[span, :]
        mixed = (
            tok.astype(F32)
            + (dot_nt(mine, out_mine_ref[...]) + dot_nt(theirs, out_theirs_ref[...]))
            + vec_ref[OUT_BIAS : OUT_BIAS + 1, :]
        )
        unit, _ = row_norm(mixed)
        normed = unit * vec_ref[LN2_GAIN : LN2_GAIN + 1, :] + vec_ref[LN2_BIAS : LN2_BIAS + 1, :]
        normed = normed.astype(BF16)
        normed_ref[block, span, :] = normed
        if own:
            mixed_ref[span, :] = mixed
            attended_ref[span, :inner] = mine
            attended_ref[span, inner:] = theirs
            sum_ref[FC2_BIAS : FC2_BIAS + 1, :] += jnp.sum(cot.astype(F32), axis=0, keepdims=True)
        elif index == 0:
            load_fc1.wait()
            load_fc2.wait()
        total = None
        step = 512
        for first in range(0, units, step):
            cols = slice(first, first + step)
            pre = dot(normed, fc1_ref[:, cols])
            grad_act = dot(cot, fc2_ref[:, cols])
            cdf, density = normal_cdf(pre)
            act_ref[block, span, cols] = (pre * cdf).astype(BF16)
            grad_hidden = (grad_act * (cdf + pre * density)).astype(BF16)
            hidden_ref[block, span, cols] = grad_hidden
            add = dot_nt(grad_hidden, fc1_ref[:, cols])
            total = add if total is None else total + add
        sum_ref[LN2_GAIN : LN2_GAIN + 1, :] += jnp.sum(total * unit, axis=0, keepdims=True)
        sum_ref[LN2_BIAS : LN2_BIAS + 1, :] += jnp.sum(total, axis=0, keepdims=True)
        if own:
            grad_own_ref[span, :] = total
        else:
            grad_other_ref[span, :] = total.astype(BF16)

    crossing = []
    for index, span in enumerate(spans):
        feed(False, index)
        crossing.append(copies.start(grad_other_ref.at[span, :], grad_got_ref.at[span, :], across))
    for index in range(tiles):
        feed(True, index)

    back = []
    for index, span in enumerate(spans):
        crossing[index].wait_recv()
        unit, scale = row_norm(mixed_ref[span, :])
        grad = grad_own_ref[span, :] + grad_got_ref[span, :].astype(F32)
        grad = row_norm_back(grad * vec_ref[LN2_GAIN : LN2_GAIN + 1, :], unit, scale)
        grad = grad + cot_ref[span, :].astype(F32)
        grad_mixed_ref[span, :] = grad
        low = grad.astype(BF16)
        low_ref[span, :] = low
        back_theirs_ref[span, :] = dot(low, out_theirs_ref[...]).astype(BF16)
        back.append(copies.start(back_theirs_ref.at[span, :], back_got_ref.at[span, :], across))
        back_mine_ref[span, :] = dot(low, out_mine_ref[...]).astype(BF16)
        sum_ref[OUT_BIAS : OUT_BIAS + 1, :] += jnp.sum(low.astype(F32), axis=0, keepdims=True)
    locals_.start(grad_mixed_ref, grad_mixed_out)

    result_other_ref[...] = dot_nt(act_ref[1], fc2_ref[...]).astype(BF16)
    locals_.start(result_other_ref, result_other_out)
    result_ref[...] = (
        dot_nt(act_ref[0], fc2_ref[...])
        + mixed_ref[...]
        + vec_ref[FC2_BIAS : FC2_BIAS + 1, :]
    )
    locals_.start(result_ref, result_out)

    def outer(first, second, right_ref, part_ref):
        turned_ref[0] = first.T
        turned_ref[1] = second.T
        step = 256

        def one(index, carry):
            cols = pl.ds(pl.multiple_of(index * step, step), step)
            part_ref[:, cols] = (
                dot(turned_ref[0], right_ref[0, :, cols]) + dot(turned_ref[1], right_ref[1, :, cols])
            ).astype(BF16)
            return carry

        lax.fori_loop(0, units // step, one, 0)

    outer(cot_ref[...], cot_other_ref[...], act_ref, fc2_part_ref)
    locals_.start(fc2_part_ref, fc2_out)
    outer(normed_ref[0], normed_ref[1], hidden_ref, fc1_part_ref)
    locals_.start(fc1_part_ref, fc1_out)
    turned_ref[0] = low_ref[...].T
    out_part_ref[...] = dot(turned_ref[0], attended_ref[...]).astype(BF16)
    locals_.start(out_part_ref, out_out)
    for copy in back:
        copy.wait_recv()
    copies.finish()
    for copy in locals_.made[2:]:
        copy.wait()


def middle(token, token_other, cot, cot_other, place, mine, theirs, vectors, out_mine, out_theirs, fc1, fc2):
    half, width = token.shape
    rows, inner = mine.shape
    units = fc1.shape[1]
    block = lambda cols, kind=BF16: pltpu.VMEM((half, cols), kind)
    pair = lambda cols: pltpu.VMEM((2, half, cols), BF16)
    return pl.pallas_call(
        middle_kernel,
        out_shape=(
            shape((half, width), F32),
            shape((half, inner)),
            shape((half, inner)),
            shape((half, width), F32),
            shape((half, width)),
            shape((width, units)),
            shape((width, units)),
            shape((width, 2 * inner)),
            shape((8, width), F32),
        ),
        in_specs=[VMEM] * 10 + [HERE] * 2,
        out_specs=(HERE, VMEM, VMEM, HERE, HERE, HERE, HERE, HERE, VMEM),
        scratch_shapes=[
            pltpu.VMEM((width, units), BF16),
            pltpu.VMEM((width, units), BF16),
            pair(units),
            pair(units),
            pair(width),
            block(width),
            block(width),
            block(width, F32),
            block(width, F32),
            block(2 * inner),
            block(inner),
            block(width),
            pltpu.VMEM((2, width, half), BF16),
            block(width, F32),
            block(width, F32),
            block(width),
            pltpu.VMEM((width, units), BF16),
            pltpu.VMEM((width, units), BF16),
            pltpu.VMEM((width, 2 * inner), BF16),
            pltpu.SemaphoreType.DMA((4,)),
            pltpu.SemaphoreType.DMA((4,)),
            pltpu.SemaphoreType.DMA((8,)),
        ],
        compiler_params=params(60 << 20, collective_id=1, has_side_effects=True),
        name="middle",
    )(token, token_other, cot, cot_other, place, mine, theirs, vectors, out_mine, out_theirs, fc1, fc2)


def attend_back(rows_ref, low_ref, value_ref, mask_ref, raw_ref, grad_low_ref):
    half, inner = rows_ref.shape
    pair = 2 * HEAD
    lane = iota((half, pair), 1)

    def one_pair(index, carry):
        cols = pl.ds(pl.multiple_of(index * pair, pair), pair)
        key_cols = pl.ds(pl.multiple_of(inner + index * pair, pair), pair)
        value_cols = pl.ds(pl.multiple_of(2 * inner + index * pair, pair), pair)
        query = low_ref[:, cols] * SCALE
        key = low_ref[:, key_cols]
        value = value_ref[:, cols]
        grad = rows_ref[:, cols]
        key_turned = (key.astype(F32) * SCALE).T.astype(BF16)
        grad_values, grad_keys, grad_queries = [], [], []
        for head in range(2):
            mine = lane < HEAD if head == 0 else lane >= HEAD
            query_head = jnp.where(mine, query, jnp.zeros_like(query))
            grad_head = jnp.where(mine, grad, jnp.zeros_like(grad))
            weights = jnp.exp(dot_nt(key, query_head))
            if mask_ref is not None:
                weights = weights * mask_ref[...]
            weights = weights * (1.0 / jnp.sum(weights, axis=0, keepdims=True))
            grad_weights = dot_nt(value, grad_head)
            shared = jnp.sum(weights * grad_weights, axis=0, keepdims=True)
            grad_scores = (weights * (grad_weights - shared)).astype(BF16)
            grad_values.append(dot(weights.astype(BF16), grad))
            grad_keys.append(dot(grad_scores, query))
            grad_queries.append(dot(key_turned[head * HEAD : (head + 1) * HEAD, :], grad_scores))
        raw_ref[:, cols] = jnp.concatenate(grad_queries, axis=0).T
        raw_ref[:, key_cols] = jnp.where(lane < HEAD, grad_keys[0], grad_keys[1])
        grad_low_ref[:, value_cols] = jnp.where(lane < HEAD, grad_values[0], grad_values[1]).astype(BF16)
        return carry

    lax.fori_loop(0, inner // pair, one_pair, 0)


def head_norm_back(raw_ref, unit_ref, scale_ref, vec_ref, grad_low_ref, sum_ref):
    group = 4 * HEAD
    means = head_mean_matrix(group)
    for first in range(0, raw_ref.shape[1], group):
        cols = slice(first, first + group)
        grad = raw_ref[:, cols]
        unit = unit_ref[:, cols]
        sum_ref[QK_GAIN : QK_GAIN + 1, cols] += jnp.sum(grad * unit, axis=0, keepdims=True)
        grad = grad * vec_ref[QK_GAIN : QK_GAIN + 1, cols]
        grad = scale_ref[:, cols] * (
            grad - two_part(grad, means) - unit * two_part(grad * unit, means)
        )
        grad_low_ref[:, cols] = grad.astype(BF16)


class Reduce:
    def __init__(self, place, copies, part_ref, scratch, out_refs):
        self.place, self.copies, self.out_refs = place, copies, out_refs
        self.got_ref, self.low_ref, self.near_ref, self.far_ref, self.last_ref = scratch
        pack, seq, core, seq_mate, pack_mate = place
        self.cross = copies.start(part_ref.at[:, 1 - core], self.got_ref, seq_mate[1])

    def add(self, own_ref, locals_wait):
        core = self.place[2]
        locals_wait()
        self.cross.wait_recv()
        for index in range(4):
            self.low_ref[index] = (
                own_ref[index].astype(F32) + self.got_ref[index].astype(F32)
            ).astype(BF16)

    def near(self):
        pack, seq, core, seq_mate, pack_mate = self.place
        odd = lax.bitwise_and(pack, 1)
        self.first = [
            self.copies.start(
                self.low_ref.at[(1 - odd) + 2 * index], self.near_ref.at[index], pack_mate[1]
            )
            for index in range(2)
        ]

    def far(self):
        pack, seq, core, seq_mate, pack_mate = self.place
        odd, high = lax.bitwise_and(pack, 1), lax.shift_right_logical(pack, 1)
        for index in range(2):
            self.first[index].wait_recv()
            self.near_ref[index] = (
                self.low_ref[odd + 2 * index].astype(F32) + self.near_ref[index].astype(F32)
            ).astype(BF16)
        self.second = self.copies.start(self.near_ref.at[1 - high], self.far_ref.at[0], pack_mate[2])

    def along(self):
        pack, seq, core, seq_mate, pack_mate = self.place
        high = lax.shift_right_logical(pack, 1)
        self.second.wait_recv()
        self.far_ref[1] = (
            self.near_ref[high].astype(F32) + self.far_ref[0].astype(F32)
        ).astype(BF16)
        self.third = self.copies.start(self.far_ref.at[1], self.last_ref, seq_mate[2])

    def own(self):
        pack, seq, core, seq_mate, pack_mate = self.place
        self.third.wait_recv()
        total = self.far_ref[1].astype(F32) + self.last_ref[...].astype(F32)
        rows, width = total.shape
        share = width // len(self.out_refs)
        self.fourth = []
        for index, out_ref in enumerate(self.out_refs):
            here = out_ref.at[pl.ds(pl.multiple_of(core * rows, 16), rows), :]
            here[...] = total[:, index * share : (index + 1) * share]
            self.fourth.append(self.copies.start(here, here, seq_mate[1]))

    def finish(self):
        for copy in self.fourth:
            copy.wait_recv()


def back_kernel(reduces, *refs):
    (
        place_row_ref,
        place_col_ref,
        mode_ref,
        vec_ref,
        back_mine_ref,
        back_other_ref,
        weight_ref,
        tok_ref,
        sum_in_ref,
        low_all,
        value_all,
        normed_all,
        unit_all,
        head_unit_all,
        head_scale_all,
        grad_mixed_all,
        result_all,
        result_other_all,
        fc1_all,
        fc2_all,
        out_all,
    ) = refs[:21]
    (
        output_ref,
        input_grad_ref,
        qkv_out_ref,
        out_out_ref,
        fc1_out_ref,
        fc2_out_ref,
        sum_ref,
    ) = refs[21:28]
    (
        low_ref,
        value_ref,
        normed_ref,
        unit_ref,
        head_unit_ref,
        head_scale_ref,
        grad_mixed_ref,
        result_ref,
        result_got_ref,
        sorted_ref,
        got_ref,
        rows_ref,
        raw_ref,
        mask_ref,
        grad_low_ref,
        grad_normed_ref,
        ordered_ref,
        long_ref,
        own_ref,
        other_ref,
        other_got_ref,
        turned_ref,
        qkv_part_ref,
        sum_got_ref,
    ) = refs[28:52]
    reduce_refs = refs[52:-3]
    send_sem, recv_sem, local_sem = refs[-3:]
    half, width = tok_ref.shape
    inner = back_mine_ref.shape[1]
    rows = 2 * half
    chunk = half // 4
    steps = range(1, 4)
    pack, seq, side = lax.axis_index("dp"), lax.axis_index("seq"), lax.axis_index("hidden")
    core = lax.bitwise_and(seq, 1)
    across = {"hidden": 1 - side}
    seq_mate = [{"seq": other_of(seq, step)} for step in range(4)]
    pack_mate = [{"dp": other_of(pack, step)} for step in range(4)]
    copies, locals_ = Copies(send_sem, recv_sem), Locals(local_sem)
    place = (pack, seq, core, seq_mate, pack_mate)

    def load(part):
        return [
            locals_.start(source.at[part], target)
            for source, target in (
                (low_all, low_ref),
                (value_all, value_ref),
                (head_unit_all, head_unit_ref),
                (head_scale_all, head_scale_ref),
                (unit_all, unit_ref),
            )
        ]

    load_normed = locals_.start(normed_all, normed_ref)
    loading = load(0)
    greet([across] + seq_mate[1:] + (pack_mate[1:] if reduces else []))

    first = side == 0
    place_own = jnp.where(first, place_row_ref[0:1, :], place_row_ref[1:2, :])
    place_other = jnp.where(first, place_row_ref[1:2, :], place_row_ref[0:1, :])
    moved = []
    for part in range(2):
        target = iota((half, half), 0) + part * half
        found = dot(one_hot(target == place_own), back_mine_ref[...])
        found = found + dot(one_hot(target == place_other), back_other_ref[...])
        sorted_ref[part * half : (part + 1) * half, :] = found.astype(BF16)
        moved.append(
            [
                copies.start(
                    sorted_ref.at[rows_at(part * half + other_of(seq, k) * chunk, chunk), :],
                    got_ref.at[part, k * chunk : (k + 1) * chunk, :],
                    seq_mate[k],
                )
                for k in steps
            ]
        )
    result_cross = copies.start(result_other_all, result_got_ref, across)
    if reduces:
        scratch = [reduce_refs[index * 6 : (index + 1) * 6] for index in range(4)]
        parts = []
        for index, (source, outs) in enumerate(
            ((fc2_all, [fc2_out_ref]), (fc1_all, [fc1_out_ref]), (out_all, [out_out_ref]))
        ):
            mine = locals_.start(source.at[:, core], scratch[index][0])
            parts.append((Reduce(place, copies, source, scratch[index][1:], outs), mine))
        (fc2_sum, fc2_mine), (fc1_sum, fc1_mine), (out_sum, out_mine) = parts
        out_wide_ref, out_got_ref = reduce_refs[24:26]
    load_normed.wait()
    for part in range(2):
        turned_ref[part] = normed_ref[part].T
    mask_ref[...] = image_mask(mode_ref, half)
    work_ref = sum_got_ref.at[9]
    work_ref[...] = sum_in_ref[...]
    if reduces:
        fc2_sum.add(scratch[0][0], fc2_mine.wait)
        fc2_sum.near()
        out_mine.wait()
        out_sum.cross.wait_recv()
        for index in range(4):
            both = scratch[2][0][index].astype(F32) + scratch[2][1][index].astype(F32)
            scratch[2][2][index] = both[:, :inner].astype(BF16)
            out_wide_ref[index] = both[:, inner:].astype(BF16)
        out_cross = copies.start(out_wide_ref, out_got_ref, across)
        fc1_sum.add(scratch[1][0], fc1_mine.wait)
        fc1_sum.near()

    def attention(part):
        for copy in moved[part]:
            copy.wait_recv()
        fill_sequence(part, seq, mode_ref, sorted_ref, got_ref, rows_ref)
        for copy in loading:
            copy.wait()
        grad_low = grad_low_ref.at[part]
        attend_back(rows_ref, low_ref, value_ref, mask_ref if part else None, raw_ref, grad_low)
        head_norm_back(raw_ref, head_unit_ref, head_scale_ref, vec_ref, grad_low, work_ref)
        total = dot_nt(grad_low[:, :inner], weight_ref[0])
        total = total + dot_nt(grad_low[:, inner : 2 * inner], weight_ref[1])
        total = total + dot_nt(grad_low[:, 2 * inner :], weight_ref[2])
        work_ref[LN1_GAIN : LN1_GAIN + 1, :] += jnp.sum(
            total * unit_ref[...].astype(F32), axis=0, keepdims=True
        )
        work_ref[LN1_BIAS : LN1_BIAS + 1, :] += jnp.sum(total, axis=0, keepdims=True)
        grad_normed_ref[part] = total.astype(BF16)
        target_ref = ordered_ref if part == 0 else long_ref
        target_ref[rows_at(seq * chunk, chunk), :] = grad_normed_ref[part, 0:chunk, :]
        return [
            copies.start(
                grad_normed_ref.at[part, k * chunk : (k + 1) * chunk, :],
                target_ref.at[rows_at(seq * chunk, chunk), :],
                seq_mate[k],
            )
            for k in steps
        ]

    returned = attention(0)
    loading = load(1)
    load_mixed = locals_.start(grad_mixed_all, grad_mixed_ref)
    load_result = locals_.start(result_all, result_ref)
    if reduces:
        fc2_sum.far()
        out_cross.wait_recv()
        for index in range(4):
            out_sum.low_ref[index] = (
                out_sum.low_ref[index].astype(F32) + out_got_ref[index].astype(F32)
            ).astype(BF16)
        out_sum.near()
    returned += attention(1)

    sums = [copies.start(work_ref, sum_got_ref.at[0], across)]
    for index in range(8):
        share = width // 8
        span = slice(index * share, (index + 1) * share)
        qkv_part_ref[index // 2, index % 2] = (
            dot(turned_ref[0, span, :], grad_low_ref[0]) + dot(turned_ref[1, span, :], grad_low_ref[1])
        ).astype(BF16)
    if reduces:
        qkv_sum = Reduce(
            place, copies, qkv_part_ref, scratch[3][1:], [qkv_out_ref.at[k] for k in range(3)]
        )
        fc1_sum.far()
        fc2_sum.along()
        out_sum.far()
    else:
        qkv_out_ref[...] = qkv_part_ref[...]
    for copy in returned:
        copy.wait_recv()
    ordered_ref[half:, :] = jnp.where(
        mode_ref[0:1, 0:1] > 0, long_ref[...].astype(F32), grad_normed_ref[1].astype(F32)
    ).astype(BF16)

    def unsort(target_ref, which, cols):
        start = pl.multiple_of(which * half, 16)
        back = one_hot(place_col_ref[pl.ds(start, half), :] == iota((half, rows), 1))
        target_ref[:, cols] = dot(back, ordered_ref[:, cols]).astype(BF16)

    wide = width // 2
    crossing = []
    for cols in (slice(0, wide), slice(wide, width)):
        unsort(other_ref, 1 - side, cols)
        crossing.append(copies.start(other_ref.at[:, cols], other_got_ref.at[:, cols], across))
    unsort(own_ref, side, slice(0, width))
    if reduces:
        qkv_sum.cross.wait_recv()
        for index in range(4):
            qkv_sum.low_ref[index] = (
                qkv_part_ref[index, core].astype(F32) + qkv_sum.got_ref[index].astype(F32)
            ).astype(BF16)
        qkv_sum.near()

    sums[0].wait_recv()
    sum_got_ref[1] = work_ref[...] + sum_got_ref[0]
    around = [copies.start(sum_got_ref.at[1], sum_got_ref.at[1 + k], seq_mate[k]) for k in steps]
    load_result.wait()
    result_cross.wait_recv()
    output_ref[...] = (result_ref[...] + result_got_ref[...].astype(F32)).astype(BF16)
    for copy in around:
        copy.wait_recv()
    sum_got_ref[5] = (sum_got_ref[1] + sum_got_ref[2]) + (sum_got_ref[3] + sum_got_ref[4])
    if reduces:
        through = [copies.start(sum_got_ref.at[5], sum_got_ref.at[5 + k], pack_mate[k]) for k in steps]
        fc1_sum.along()
        out_sum.along()
        fc2_sum.own()
        qkv_sum.far()
    load_mixed.wait()
    for copy in crossing:
        copy.wait_recv()
    for step in range(4):
        span = slice(step * chunk, (step + 1) * chunk)
        unit, scale = row_norm(tok_ref[span, :].astype(F32))
        grad = own_ref[span, :].astype(F32) + other_got_ref[span, :].astype(F32)
        grad = row_norm_back(grad * vec_ref[LN1_GAIN : LN1_GAIN + 1, :], unit, scale)
        input_grad_ref[span, :] = (grad_mixed_ref[span, :] + grad).astype(BF16)
    if reduces:
        fc1_sum.own()
        out_sum.own()
        for copy in through:
            copy.wait_recv()
        sum_ref[...] = (sum_got_ref[5] + sum_got_ref[6]) + (sum_got_ref[7] + sum_got_ref[8])
        qkv_sum.along()
        qkv_sum.own()
        for each in (fc1_sum, fc2_sum, out_sum, qkv_sum):
            each.finish()
    else:
        sum_ref[...] = sum_got_ref[5]
    copies.finish()


def back(reduces, place_row, place_col, mode, vectors, back_mine, back_other, weight, token, sums, kept, grad_mixed, result, result_other, fc1_part, fc2_part, out_part, packs):
    normed, unit, low, value, head_unit, head_scale = kept
    half, width = token.shape
    inner = back_mine.shape[1]
    units = fc1_part.shape[1]
    share = width // packs
    rows = 2 * half
    block = lambda cols, kind=BF16: pltpu.VMEM((half, cols), kind)
    pair = lambda cols: pltpu.VMEM((2, half, cols), BF16)
    cut = (4, 2, width // 8)
    piece = width // 8

    def summing(columns, wide, owns):
        return [
            pltpu.VMEM((4, piece, wide) if owns else (8, 128), BF16),
            pltpu.VMEM((4, piece, wide), BF16),
            pltpu.VMEM((4, piece, columns), BF16),
            pltpu.VMEM((2, piece, columns), BF16),
            pltpu.VMEM((2, piece, columns), BF16),
            pltpu.VMEM((piece, columns), BF16),
        ]

    reduce_scratch = []
    if reduces:
        reduce_scratch = (
            summing(units, units, True)
            + summing(units, units, True)
            + summing(inner, 2 * inner, True)
            + summing(3 * inner, 3 * inner, False)
            + [pltpu.VMEM((4, piece, inner), BF16)] * 2
        )
    copies = 6 + 1 + 6 + 1 + 3 + 2 + (3 + 3 * 6 + 1 + 8 if reduces else 0)
    return pl.pallas_call(
        functools.partial(back_kernel, reduces),
        out_shape=(
            shape((half, width)),
            shape((half, width)),
            shape((3, share, inner), F32) if reduces else shape((*cut, 3 * inner)),
            shape((share, inner), F32),
            shape((share, units), F32),
            shape((share, units), F32),
            shape((8, width), F32),
        ),
        in_specs=[VMEM] * 9 + [HERE] * 12,
        out_specs=(VMEM,) * 7,
        scratch_shapes=[
            block(2 * inner),
            block(inner),
            pair(width),
            block(width),
            block(2 * inner, F32),
            block(2 * inner, F32),
            block(width, F32),
            block(width, F32),
            block(width),
            pltpu.VMEM((rows, inner), BF16),
            pair(inner),
            block(inner),
            block(2 * inner, F32),
            pltpu.VMEM((half, half), F32),
            pair(3 * inner),
            pair(width),
            pltpu.VMEM((rows, width), BF16),
            block(width),
            block(width),
            block(width),
            block(width),
            pltpu.VMEM((2, width, half), BF16),
            pltpu.VMEM((*cut, 3 * inner), BF16),
            pltpu.VMEM((10, 8, width), F32),
        ]
        + reduce_scratch
        + [
            pltpu.SemaphoreType.DMA((copies,)),
            pltpu.SemaphoreType.DMA((copies,)),
            pltpu.SemaphoreType.DMA((16,)),
        ],
        compiler_params=params(63 << 20, collective_id=2, has_side_effects=True),
        name="back",
    )(
        place_row,
        place_col,
        mode,
        vectors,
        back_mine,
        back_other,
        weight,
        token,
        sums,
        low,
        value,
        normed,
        unit,
        head_unit,
        head_scale,
        grad_mixed,
        result,
        result_other,
        fc1_part.reshape(*cut, -1),
        fc2_part.reshape(*cut, -1),
        out_part.reshape(*cut, -1),
    )


def swap(array, axis, step):
    pairs = [(index, index ^ step) for index in range(lax.axis_size(axis))]
    return lax.ppermute(array, axis, pairs)


def owned_sum(part, dim):
    total = lax.psum_scatter(part.astype(BF16), "dp", scatter_dimension=dim, tiled=True)
    total = (total.astype(F32) + swap(total, "seq", 1).astype(F32)).astype(BF16)
    return total.astype(F32) + swap(total, "seq", 2).astype(F32)


def local(
    tokens,
    segment,
    cotangent,
    ln1_gain,
    ln1_bias,
    qkv_weight,
    qk_gain,
    out_weight,
    out_bias,
    ln2_gain,
    ln2_bias,
    fc1_weight,
    fc2_weight,
    fc2_bias,
):
    half, width = tokens.shape
    quarter = half * lax.axis_size("hidden")
    packs = lax.axis_size("dp")
    inner = qkv_weight.shape[2]
    heads = inner // HEAD
    seq = lax.axis_index("seq")
    share = ln1_gain.shape[0]
    gathers = packs == 4
    lanes = jnp.arange(width)
    pieces = jnp.stack([ln1_gain, ln1_bias, out_bias, ln2_gain, ln2_bias, fc2_bias]).astype(F32)
    pack = lax.axis_index("dp")
    vectors = jnp.where(lanes // share == pack, jnp.tile(pieces, (1, packs)), 0.0)
    gains = jnp.tile(qk_gain.astype(F32), (1, width // (2 * qk_gain.shape[1]))).reshape(1, width)
    gains = jnp.where(lanes % HEAD // qk_gain.shape[1] == pack, gains, 0.0)
    vectors = jnp.concatenate([vectors, gains, jnp.zeros((1, width), F32)], axis=0)
    if not gathers:
        vectors = lax.psum(vectors, "dp")
        qkv_weight = lax.all_gather(qkv_weight, "dp", axis=1, tiled=True)
    labels = lax.dynamic_slice_in_dim(segment, seq * quarter, quarter, 0)
    (
        tokens_other,
        cot_other,
        place_row,
        place_col,
        mode,
        vectors,
        mine,
        theirs,
        qkv_full,
        out_mine,
        out_theirs,
        fc1_full,
        fc2_full,
        _,
        *kept,
    ) = front(
        gathers, tokens, cotangent, labels, vectors, qkv_weight, out_weight.T, fc1_weight,
        fc2_weight.T, packs,
    )
    if not gathers:
        out_mine = lax.all_gather(out_weight.T, "dp", axis=0, tiled=True)
        out_theirs = swap(out_mine, "hidden", 1)
        fc1_full = lax.all_gather(fc1_weight, "dp", axis=0, tiled=True)
        fc2_full = lax.all_gather(fc2_weight.T, "dp", axis=0, tiled=True)
    (
        grad_mixed,
        back_mine,
        back_other,
        result,
        result_other,
        fc1_part,
        fc2_part,
        out_part,
        sums,
    ) = middle(
        tokens, tokens_other, cotangent, cot_other, place_col, mine, theirs, vectors, out_mine,
        out_theirs, fc1_full, fc2_full,
    )
    output, input_grad, qkv_owned, out_owned, fc1_owned, fc2_owned, sums = back(
        gathers, place_row, place_col, mode, vectors, back_mine, back_other, qkv_full, tokens, sums,
        kept, grad_mixed, result, result_other, fc1_part, fc2_part, out_part, packs,
    )
    if not gathers:
        sums = lax.psum(sums, "dp")
        qkv_part = jnp.moveaxis(qkv_owned.reshape(width, 3, inner), 1, 0)
        qkv_owned = owned_sum(qkv_part, 1)
        out_part = out_part[:, :inner].astype(F32) + swap(out_part[:, inner:], "hidden", 1).astype(F32)
        out_owned = owned_sum(out_part, 0)
        fc1_owned = owned_sum(fc1_part, 0)
        fc2_owned = owned_sum(fc2_part, 0)
    out_owned, fc2_owned = out_owned.T, fc2_owned.T
    vec = lax.dynamic_slice_in_dim(sums[:QK_GAIN], pack * share, share, 1)
    qk_share = qk_gain.shape[1]
    qk_owned = sums[QK_GAIN].reshape(2, heads, HEAD).sum(axis=1)
    qk_owned = lax.dynamic_slice_in_dim(qk_owned, pack * qk_share, qk_share, 1)
    return (
        output,
        input_grad,
        vec[LN1_GAIN],
        vec[LN1_BIAS],
        qkv_owned,
        qk_owned,
        out_owned,
        vec[OUT_BIAS],
        vec[LN2_GAIN],
        vec[LN2_BIAS],
        fc1_owned,
        fc2_owned,
        vec[FC2_BIAS],
    )


def solution(mesh):
    rows = P(("dp", "seq", "hidden"), None)
    in_specs = (
        rows,
        P("dp"),
        rows,
        P("dp"),
        P("dp"),
        P(None, "dp", "hidden"),
        P(None, "dp"),
        P("hidden", "dp"),
        P("dp"),
        P("dp"),
        P("dp"),
        P("dp", "hidden"),
        P("hidden", "dp"),
        P("dp"),
    )
    out_specs = (
        rows,
        rows,
        P("dp"),
        P("dp"),
        P(None, "dp", "hidden"),
        P(None, "dp"),
        P("hidden", "dp"),
        P("dp"),
        P("dp"),
        P("dp"),
        P("dp", "hidden"),
        P("hidden", "dp"),
        P("dp"),
    )
    return jax.shard_map(local, mesh=mesh, in_specs=in_specs, out_specs=out_specs, check_vma=False)
```

```python
import functools

import jax
import jax.numpy as jnp
from jax import lax
from jax.experimental import pallas as pl
from jax.experimental.pallas import tpu as pltpu
from jax.sharding import PartitionSpec as P

HEAD = 64
LONG = 576
IMAGE = 64
LABELS = 128
EPSILON = 1e-06
SCALE = HEAD ** (-0.5)
F32 = jnp.float32
BF16 = jnp.bfloat16

VMEM = pl.BlockSpec(memory_space=pltpu.VMEM)
SMEM = pl.BlockSpec(memory_space=pltpu.SMEM)
HERE = pl.BlockSpec(memory_space=pl.ANY)
LN1_GAIN, LN1_BIAS, OUT_BIAS, LN2_GAIN, LN2_BIAS, FC2_BIAS, QK_GAIN = range(7)


def params(limit=56 << 20, **more):
    return pltpu.CompilerParams(vmem_limit_bytes=limit, **more)


def shape(dims, dtype=BF16):
    return jax.ShapeDtypeStruct(dims, dtype)


def dot(left, right):
    return jnp.dot(left, right, preferred_element_type=F32)


def dot_nt(left, right):
    return lax.dot_general(left, right, (((1,), (1,)), ((), ())), preferred_element_type=F32)


def dot_tn(left, right):
    return lax.dot_general(left, right, (((0,), (0,)), ((), ())), preferred_element_type=F32)


def iota(dims, dim):
    return lax.broadcasted_iota(jnp.int32, dims, dim)


def one_hot(test):
    return jnp.where(test, 1.0, 0.0).astype(BF16)


def two_part(values, matrix):
    high = values.astype(BF16)
    rest = (values - high.astype(F32)).astype(BF16)
    return dot(high, matrix) + dot(rest, matrix)


def head_mean_matrix(width):
    return jnp.where(
        iota((width, width), 0) // HEAD == iota((width, width), 1) // HEAD, 1.0 / HEAD, 0.0
    ).astype(BF16)


def row_norm(values):
    mean = jnp.mean(values, axis=-1, keepdims=True)
    centred = values - mean
    spread = jnp.mean(centred * centred, axis=-1, keepdims=True)
    scale = lax.rsqrt(spread + EPSILON)
    return centred * scale, scale


def row_norm_back(grad_unit, unit, scale):
    first = jnp.mean(grad_unit, axis=-1, keepdims=True)
    second = jnp.mean(grad_unit * unit, axis=-1, keepdims=True)
    return scale * (grad_unit - first - unit * second)


def normal_cdf(values):
    size = jnp.abs(values) * (2.0 ** -0.5)
    bell = jnp.exp(-0.5 * values * values)
    t = 1.0 / (1.0 + 0.3275911 * size)
    poly = 1.061405429 * t - 1.453152027
    poly = poly * t + 1.421413741
    poly = poly * t - 0.284496736
    poly = poly * t + 0.254829592
    tail = 0.5 * (poly * t) * bell
    return jnp.where(values < 0, tail, 1.0 - tail), bell * 0.3989422804014327


def other_of(value, step):
    return lax.bitwise_xor(value, jnp.int32(step))


def rows_at(start, size):
    return pl.ds(pl.multiple_of(start, 16), size)


class Copies:
    def __init__(self, send_sem, recv_sem):
        self.send_sem, self.recv_sem = send_sem, recv_sem
        self.made = []

    def start(self, source, target, device):
        index = len(self.made)
        copy = pltpu.make_async_remote_copy(
            src_ref=source,
            dst_ref=target,
            send_sem=self.send_sem.at[index],
            recv_sem=self.recv_sem.at[index],
            device_id=device,
            device_id_type=pl.DeviceIdType.MESH,
        )
        copy.start()
        self.made.append(copy)
        return copy

    def finish(self):
        for copy in self.made:
            copy.wait_send()


class Locals:
    def __init__(self, sem):
        self.sem, self.made = sem, []

    def start(self, source, target):
        copy = pltpu.make_async_copy(source, target, self.sem.at[len(self.made)])
        copy.start()
        self.made.append(copy)
        return copy

    def finish(self):
        for copy in self.made:
            copy.wait()


def greet(devices):
    barrier = pltpu.get_barrier_semaphore()
    for device in devices:
        pl.semaphore_signal(barrier, inc=1, device_id=device, device_id_type=pl.DeviceIdType.MESH)
    pl.semaphore_wait(barrier, len(devices))


def place_rows(labels, place_row_ref, place_col_ref, mode_ref, places_ref):
    rows = labels.shape[1]
    half = rows // 2
    chunk = LONG // 4
    by_row = jnp.where(labels == iota((LABELS, rows), 0), 1.0, 0.0)
    count = jnp.sum(by_row, axis=1, keepdims=True)
    cut = 0.5 * (chunk + IMAGE)
    long = jnp.where(count > cut, count, 0.0)
    small = count - long
    total = jnp.sum(long, axis=0, keepdims=True)
    left = iota((LABELS, LABELS), 0)
    right = iota((LABELS, LABELS), 1)

    def before(counts):
        turned = jnp.broadcast_to(counts, (LABELS, LABELS)).T
        return jnp.sum(jnp.where(right < left, turned, 0.0), axis=1, keepdims=True)

    base = jnp.where(long > 0, before(long), total + before(small))
    earlier = one_hot(left < right)
    for first in range(0, rows, LABELS):
        cols = slice(first, first + LABELS)
        block = by_row[:, cols]
        place = base + dot(block.astype(BF16), earlier)
        base = base + jnp.sum(block, axis=1, keepdims=True)
        place = jnp.sum(block * place, axis=0, keepdims=True)
        places_ref[0:1, cols] = place.astype(jnp.int32)
        turned = jnp.broadcast_to(place, (LABELS, LABELS)).T
        place_col_ref[cols, :] = turned[:, 0:1].astype(jnp.int32)
    place_row_ref[0:1, :] = places_ref[0:1, :half]
    place_row_ref[1:2, :] = places_ref[0:1, half:]
    mode_ref[...] = jnp.broadcast_to(jnp.where(total > rows - IMAGE, 1.0, 0.0), mode_ref.shape)


def sorting(place_ref, side, hot_ref):
    half = place_ref.shape[1]
    first = side == 0
    place_own = jnp.where(first, place_ref[0:1, :], place_ref[1:2, :])
    place_other = jnp.where(first, place_ref[1:2, :], place_ref[0:1, :])
    for part in range(2):
        target = iota((half, half), 0) + part * half
        hot_ref[0, part * half : (part + 1) * half, :] = one_hot(target == place_own)
        hot_ref[1, part * half : (part + 1) * half, :] = one_hot(target == place_other)


def put_vectors(pieces, gain_ref, pack, vec_ref):
    share, width = pieces[0].shape[0], vec_ref.shape[1]
    at = one_hot(iota((share, width), 1) == iota((share, width), 0) + pack * share)
    vec_ref[...] = jnp.zeros_like(vec_ref)
    for index, piece in enumerate(pieces):
        row = piece[...].astype(F32).reshape(1, share)
        row = jnp.broadcast_to(row, (8, share)).astype(BF16)
        vec_ref[index : index + 1, :] = dot(row, at)[0:1, :]
    few, half = gain_ref.shape[1], width // 2
    at = one_hot(lax.bitwise_and(iota((few, half), 1), HEAD - 1) == iota((few, half), 0) + pack * few)
    gains = dot(gain_ref[...], at)
    vec_ref[QK_GAIN : QK_GAIN + 1, :half] = gains[0:1, :]
    vec_ref[QK_GAIN : QK_GAIN + 1, half:] = gains[1:2, :]


def fill_sequence(part, seq, mode_ref, sorted_ref, got_ref, rows_ref):
    half = rows_ref.shape[0]
    chunk = half // 4
    home = sorted_ref[rows_at(part * half + seq * chunk, chunk), :]
    for step in range(4):
        rows = home if step == 0 else got_ref[part, step * chunk : (step + 1) * chunk, :]
        if part == 1:
            local = sorted_ref[half + step * chunk : half + (step + 1) * chunk, :]
            rows = jnp.where(mode_ref[0:1, 0:1] > 0, rows.astype(F32), local.astype(F32))
        rows_ref[step * chunk : (step + 1) * chunk, :] = rows.astype(BF16)


def image_mask(mode_ref, rows):
    same = lax.shift_right_logical(iota((rows, rows), 0), 6) == lax.shift_right_logical(
        iota((rows, rows), 1), 6
    )
    return jnp.where(same, 1.0, mode_ref[0:1, 0:1])


def project(part, rows_ref, weight_ref, vec_ref, kept, raw_ref):
    normed_ref, unit_ref, low_ref, value_ref, head_unit_ref, head_scale_ref = (
        ref.at[part] for ref in kept
    )
    half, width = rows_ref.shape
    inner = value_ref.shape[1]
    chunk = half // 4
    for step in range(4):
        rows = slice(step * chunk, (step + 1) * chunk)
        unit, _ = row_norm(rows_ref[rows, :].astype(F32))
        unit_ref[rows, :] = unit.astype(BF16)
        normed = unit * vec_ref[LN1_GAIN : LN1_GAIN + 1, :] + vec_ref[LN1_BIAS : LN1_BIAS + 1, :]
        normed_ref[rows, :] = normed.astype(BF16)
    raw_ref[:, :inner] = dot(normed_ref[...], weight_ref[0])
    raw_ref[:, inner:] = dot(normed_ref[...], weight_ref[1])
    value_ref[...] = dot(normed_ref[...], weight_ref[2]).astype(BF16)
    group = 4 * HEAD
    means = head_mean_matrix(group)
    for first in range(0, 2 * inner, group):
        cols = slice(first, first + group)
        raw = raw_ref[:, cols]
        centred = raw - two_part(raw, means)
        scale = lax.rsqrt(two_part(centred * centred, means) + EPSILON)
        unit = centred * scale
        head_unit_ref[:, cols] = unit
        head_scale_ref[:, cols] = scale
        low_ref[:, cols] = (unit * vec_ref[QK_GAIN : QK_GAIN + 1, cols]).astype(BF16)


def attend(part, kept, mask_ref, attended_ref):
    low_ref, value_ref = kept[2].at[part], kept[3].at[part]
    half, inner = value_ref.shape
    pair = 2 * HEAD
    lane = iota((half, pair), 1)

    def one_pair(index, carry):
        cols = pl.ds(pl.multiple_of(index * pair, pair), pair)
        key_cols = pl.ds(pl.multiple_of(inner + index * pair, pair), pair)
        query = low_ref[:, cols] * SCALE
        key = low_ref[:, key_cols]
        value = jnp.concatenate([value_ref[:, cols], jnp.ones((half, pair), BF16)], axis=1)
        found = []
        for head in range(2):
            mine = lane < HEAD if head == 0 else lane >= HEAD
            scores = dot_nt(jnp.where(mine, query, jnp.zeros_like(query)), key)
            weights = jnp.exp(scores).astype(BF16)
            if part == 1:
                weights = weights * mask_ref[...]
            both = dot(weights, value)
            found.append(both[:, :pair] / both[:, pair:])
        attended_ref[part, :, cols] = jnp.where(lane < HEAD, found[0], found[1]).astype(BF16)
        return carry

    lax.fori_loop(0, inner // pair, one_pair, 0)


KEPT = 6


def front_kernel(gathers, *refs):
    tok_ref, cot_ref, seg_ref, qkv_ref, out_ref, fc1_ref, fc2_ref = refs[:7]
    vec_in_refs, refs = (refs[7:14], refs[14:]) if gathers else (refs[7:8], refs[8:])
    (
        tok_other_ref,
        cot_other_ref,
        place_row_ref,
        place_col_ref,
        mode_ref,
        vec_ref,
        mine_ref,
        theirs_ref,
        qkv_all_ref,
        out_all_ref,
        out_theirs_ref,
        fc1_all_ref,
        fc2_all_ref,
    ) = refs[:13]
    kept_out = refs[13 : 13 + KEPT]
    (
        sorted_ref,
        got_ref,
        rows_ref,
        raw_ref,
        mask_ref,
        attended_ref,
        back_ref,
        vec_got_ref,
        hot_ref,
        places_ref,
        out_pair_ref,
    ) = refs[13 + KEPT : 24 + KEPT]
    share_refs = refs[24 + KEPT : 27 + KEPT]
    kept = refs[27 + KEPT : 27 + 2 * KEPT]
    send_sem, recv_sem, local_sem = refs[27 + 2 * KEPT :]
    pack, seq, side = lax.axis_index("dp"), lax.axis_index("seq"), lax.axis_index("hidden")
    core = lax.bitwise_and(seq, 1)
    half, width = tok_ref.shape
    chunk = half // 4
    steps = range(1, 4)
    across = {"hidden": 1 - side}
    seq_mate = [{"seq": other_of(seq, step)} for step in range(4)]
    pack_mate = [{"dp": other_of(pack, step)} for step in range(4)]
    greet([across] + seq_mate[1:] + (pack_mate[1:] if gathers else []))
    copies, locals_ = Copies(send_sem, recv_sem), Locals(local_sem)

    wide = width // 3
    pieces = [slice(first, first + wide) for first in range(0, width, wide)]
    tokens = [copies.start(tok_ref.at[:, c], tok_other_ref.at[:, c], across) for c in pieces]
    whole = fc1_ref.shape[0]
    in_flight = []

    def rows_of(ref, index, piece, size):
        rows = rows_at(index * whole + piece * size, size)
        return ref.at[:, rows, :] if len(ref.shape) == 3 else ref.at[rows, :]

    class Half:
        def __init__(self, source, target):
            self.target, self.size = target, whole // 2
            self.first = [
                copies.start(
                    rows_of(source, 0, core, self.size),
                    rows_of(target, pack, core, self.size),
                    pack_mate[k],
                )
                for k in steps
            ]

        def share(self):
            for k in steps:
                self.first[k - 1].wait_recv()
                there = rows_of(self.target, other_of(pack, k), core, self.size)
                in_flight.append(copies.start(there, there, seq_mate[1]))

    class Quarter:
        def __init__(self, source, target):
            self.target, self.size = target, whole // 4
            self.first = [
                copies.start(
                    rows_of(source, 0, seq, self.size),
                    rows_of(target, pack, seq, self.size),
                    pack_mate[k],
                )
                for k in steps
            ]
            self.second = []

        def there(self, k, piece):
            return rows_of(self.target, other_of(pack, k), piece, self.size)

        def pass_on(self):
            for k in steps:
                self.first[k - 1].wait_recv()
                there = self.there(k, seq)
                self.second.append(copies.start(there, there, seq_mate[2]))
            for k in steps:
                there = self.there(k, seq)
                in_flight.append(copies.start(there, there, seq_mate[1]))

        def share(self):
            for k in steps:
                self.second[k - 1].wait_recv()
                there = self.there(k, other_of(seq, 2))
                in_flight.append(copies.start(there, there, seq_mate[1]))

    if gathers:
        gather_qkv = Quarter(qkv_ref, qkv_all_ref)
        put_vectors(vec_in_refs[:6], vec_in_refs[6], pack, vec_got_ref.at[3])
        gather_vec = [
            copies.start(vec_got_ref.at[3], vec_got_ref.at[k - 1], pack_mate[k]) for k in steps
        ]
        pair_out = copies.start(out_ref, out_pair_ref, across)
        gather_out = Half(out_ref, out_all_ref)
        gather_fc2 = Quarter(fc2_ref, fc2_all_ref)
        keep = [locals_.start(qkv_ref, qkv_all_ref.at[:, rows_at(pack * whole, whole), :])] + [
            locals_.start(source, target)
            for source, target in zip((out_ref, fc1_ref, fc2_ref), share_refs)
        ]
    else:
        keep = [locals_.start(qkv_ref, qkv_all_ref)]
    rows = 2 * half
    labels = seg_ref[...]
    place_rows(
        sum(
            jnp.where(seq == index, labels[index * rows : (index + 1) * rows].reshape(1, rows), 0)
            for index in range(4)
        ),
        place_row_ref,
        place_col_ref,
        mode_ref,
        places_ref,
    )
    sorting(place_row_ref, side, hot_ref)
    mask_ref[...] = image_mask(mode_ref, half).astype(BF16)

    if gathers:
        gather_qkv.pass_on()
    moved = [[], []]
    for piece, cols in enumerate(pieces):
        tokens[piece].wait_recv()
        for part in range(2):
            span = slice(part * half, (part + 1) * half)
            found = dot(hot_ref[0, span, :], tok_ref[:, cols])
            found = found + dot(hot_ref[1, span, :], tok_other_ref[:, cols])
            sorted_ref[span, cols] = found.astype(BF16)
            for k in steps:
                start = part * half + other_of(seq, k) * chunk
                moved[part].append(
                    copies.start(
                        sorted_ref.at[rows_at(start, chunk), cols],
                        got_ref.at[part, k * chunk : (k + 1) * chunk, cols],
                        seq_mate[k],
                    )
                )
    cots = copies.start(cot_ref, cot_other_ref, across)
    if gathers:
        pair_out.wait_recv()
        for copy in keep[1:]:
            copy.wait()
        for source, target in zip(
            (*share_refs, out_pair_ref), (out_all_ref, fc1_all_ref, fc2_all_ref, out_theirs_ref)
        ):
            locals_.start(source, target.at[rows_at(pack * whole, whole), :])
        gather_theirs = Half(out_pair_ref, out_theirs_ref)
        gather_fc1 = Half(fc1_ref, fc1_all_ref)
        gather_qkv.share()
        needed = list(in_flight)
        for k in steps:
            gather_vec[k - 1].wait_recv()
        vec_ref[...] = (vec_got_ref[3] + vec_got_ref[0]) + (vec_got_ref[1] + vec_got_ref[2])
        for copy in needed:
            copy.wait_recv()
            in_flight.remove(copy)
    else:
        vec_ref[...] = vec_in_refs[0][...]
    keep[0].wait()

    def begin(part):
        for copy in moved[part]:
            copy.wait_recv()
        fill_sequence(part, seq, mode_ref, sorted_ref, got_ref, rows_ref)
        project(part, rows_ref, qkv_all_ref, vec_ref, kept, raw_ref)

    def give_back(part, target_ref):
        target_ref[rows_at(seq * chunk, chunk), :] = attended_ref[part, 0:chunk, :]
        given = [
            copies.start(
                attended_ref.at[part, k * chunk : (k + 1) * chunk, :],
                target_ref.at[rows_at(seq * chunk, chunk), :],
                seq_mate[k],
            )
            for k in steps
        ]
        for ref, out in zip(kept, kept_out):
            locals_.start(ref.at[part], out.at[part])
        return given

    begin(0)
    if gathers:
        gather_out.share()
        gather_fc2.pass_on()
    attend(0, kept, mask_ref, attended_ref)
    given = give_back(0, mine_ref)
    begin(1)
    for copy in given:
        copy.wait_recv()
    first = copies.start(mine_ref.at[0:half, :], theirs_ref.at[0:half, :], across)
    attend(1, kept, mask_ref, attended_ref)
    for copy in give_back(1, back_ref):
        copy.wait_recv()
    mine_ref[half:, :] = jnp.where(
        mode_ref[0:1, 0:1] > 0, back_ref[...].astype(F32), attended_ref[1].astype(F32)
    ).astype(BF16)
    second = copies.start(mine_ref.at[half : 2 * half, :], theirs_ref.at[half : 2 * half, :], across)
    if gathers:
        gather_theirs.share()
        gather_fc2.share()
        gather_fc1.share()
        for copy in in_flight:
            copy.wait_recv()
    cots.wait_recv()
    first.wait_recv()
    second.wait_recv()
    copies.finish()
    for copy in locals_.made[4 if gathers else 1 :]:
        copy.wait()


def front(gathers, tokens, cotangent, segment, vectors, qkv, out, fc1, fc2):
    half, width = tokens.shape
    rows = 2 * half
    share, inner = out.shape
    units = fc1.shape[1]
    kept = [
        ((2, half, width), BF16),
        ((2, half, width), BF16),
        ((2, half, 2 * inner), BF16),
        ((2, half, inner), BF16),
        ((2, half, 2 * inner), F32),
        ((2, half, 2 * inner), F32),
    ]
    whole = width if gathers else share
    outs = [
        (shape((half, width)), VMEM),
        (shape((half, width)), HERE),
        (shape((2, half), jnp.int32), VMEM),
        (shape((rows, 1), jnp.int32), VMEM),
        (shape((8, 128), F32), VMEM),
        (shape((8, width), F32), VMEM),
        (shape((rows, inner)), VMEM),
        (shape((rows, inner)), VMEM),
        (shape((3, width, inner)), VMEM),
        (shape((whole, inner)), HERE),
        (shape((whole, inner)), HERE),
        (shape((whole, units)), HERE),
        (shape((whole, units)), HERE),
    ] + [(shape(dims, kind), HERE) for dims, kind in kept]
    copies = 3 + 18 + 1 + 6 + 2 + (3 + 1 + 2 * 12 + 3 * 6 if gathers else 0)
    return pl.pallas_call(
        functools.partial(front_kernel, gathers),
        out_shape=[o[0] for o in outs],
        in_specs=[VMEM, HERE, VMEM] + [HERE] * 4 + [VMEM] * len(vectors),
        out_specs=[o[1] for o in outs],
        scratch_shapes=[
            pltpu.VMEM((rows, width), BF16),
            pltpu.VMEM((2, half, width), BF16),
            pltpu.VMEM((half, width), BF16),
            pltpu.VMEM((half, 2 * inner), F32),
            pltpu.VMEM((half, half), BF16),
            pltpu.VMEM((2, half, inner), BF16),
            pltpu.VMEM((half, inner), BF16),
            pltpu.VMEM((4, 8, width), F32),
            pltpu.VMEM((2, rows, half), BF16),
            pltpu.VMEM((8, rows), jnp.int32),
            pltpu.VMEM((share, inner), BF16),
            pltpu.VMEM((share, inner), BF16),
            pltpu.VMEM((share, units), BF16),
            pltpu.VMEM((share, units), BF16),
        ]
        + [pltpu.VMEM(dims, kind) for dims, kind in kept]
        + [
            pltpu.SemaphoreType.DMA((copies,)),
            pltpu.SemaphoreType.DMA((copies,)),
            pltpu.SemaphoreType.DMA((8 + 2 * KEPT,)),
        ],
        compiler_params=params(collective_id=0, has_side_effects=True),
        name="front",
    )(tokens, cotangent, segment, qkv, out, fc1, fc2, *vectors)


def middle_kernel(*refs):
    (
        tok_ref,
        tok_other_ref,
        cot_ref,
        cot_other_ref,
        place_ref,
        mine_ref,
        theirs_ref,
        vec_ref,
        out_mine_ref,
        out_theirs_ref,
        fc1_all_ref,
        fc2_all_ref,
    ) = refs[:12]
    (
        grad_mixed_out,
        back_mine_ref,
        back_got_ref,
        result_out,
        result_other_out,
        fc1_out,
        fc2_out,
        out_out,
        sum_ref,
    ) = refs[12:21]
    (
        fc1_ref,
        fc2_ref,
        act_ref,
        hidden_ref,
        normed_ref,
        grad_other_ref,
        grad_got_ref,
        grad_own_ref,
        mixed_ref,
        attended_ref,
        back_theirs_ref,
        low_ref,
        turned_ref,
        grad_mixed_ref,
        result_ref,
        result_other_ref,
        fc1_part_ref,
        fc2_part_ref,
        out_part_ref,
        send_sem,
        recv_sem,
        local_sem,
    ) = refs[21:]
    half, width = tok_ref.shape
    rows, inner = mine_ref.shape
    units = fc1_ref.shape[1]
    side = lax.axis_index("hidden")
    across = {"hidden": 1 - side}
    copies, locals_ = Copies(send_sem, recv_sem), Locals(local_sem)
    load_fc1 = locals_.start(fc1_all_ref, fc1_ref)
    load_fc2 = locals_.start(fc2_all_ref, fc2_ref)
    greet([across])
    tiles = 2
    tile = half // tiles
    spans = [slice(index * tile, (index + 1) * tile) for index in range(tiles)]
    sum_ref[...] = jnp.zeros_like(sum_ref)

    def feed(own, index):
        block, span = (0 if own else 1), spans[index]
        start = (side if own else 1 - side) * half + index * tile
        place = place_ref[pl.ds(pl.multiple_of(start, 16), tile), :]
        back = one_hot(place == iota((tile, rows), 1))
        mine = dot(back, mine_ref[...]).astype(BF16)
        theirs = dot(back, theirs_ref[...]).astype(BF16)
        tok = (tok_ref if own else tok_other_ref)[span, :]
        cot = (cot_ref if own else cot_other_ref)[span, :]
        mixed = (
            tok.astype(F32)
            + (dot_nt(mine, out_mine_ref[...]) + dot_nt(theirs, out_theirs_ref[...]))
            + vec_ref[OUT_BIAS : OUT_BIAS + 1, :]
        )
        unit, _ = row_norm(mixed)
        normed = unit * vec_ref[LN2_GAIN : LN2_GAIN + 1, :] + vec_ref[LN2_BIAS : LN2_BIAS + 1, :]
        normed = normed.astype(BF16)
        normed_ref[block, span, :] = normed
        if own:
            mixed_ref[span, :] = mixed
            attended_ref[span, :inner] = mine
            attended_ref[span, inner:] = theirs
            sum_ref[FC2_BIAS : FC2_BIAS + 1, :] += jnp.sum(cot.astype(F32), axis=0, keepdims=True)
        elif index == 0:
            load_fc1.wait()
            load_fc2.wait()
        total = None
        step = 512
        for first in range(0, units, step):
            cols = slice(first, first + step)
            pre = dot(normed, fc1_ref[:, cols])
            grad_act = dot(cot, fc2_ref[:, cols])
            cdf, density = normal_cdf(pre)
            act_ref[block, span, cols] = (pre * cdf).astype(BF16)
            grad_hidden = (grad_act * (cdf + pre * density)).astype(BF16)
            hidden_ref[block, span, cols] = grad_hidden
            add = dot_nt(grad_hidden, fc1_ref[:, cols])
            total = add if total is None else total + add
        sum_ref[LN2_GAIN : LN2_GAIN + 1, :] += jnp.sum(total * unit, axis=0, keepdims=True)
        sum_ref[LN2_BIAS : LN2_BIAS + 1, :] += jnp.sum(total, axis=0, keepdims=True)
        if own:
            grad_own_ref[span, :] = total
        else:
            grad_other_ref[span, :] = total.astype(BF16)

    crossing = []
    for index, span in enumerate(spans):
        feed(False, index)
        crossing.append(copies.start(grad_other_ref.at[span, :], grad_got_ref.at[span, :], across))
    for index in range(tiles):
        feed(True, index)

    back = []
    for index, span in enumerate(spans):
        crossing[index].wait_recv()
        unit, scale = row_norm(mixed_ref[span, :])
        grad = grad_own_ref[span, :] + grad_got_ref[span, :].astype(F32)
        grad = row_norm_back(grad * vec_ref[LN2_GAIN : LN2_GAIN + 1, :], unit, scale)
        grad = grad + cot_ref[span, :].astype(F32)
        grad_mixed_ref[span, :] = grad
        low = grad.astype(BF16)
        low_ref[span, :] = low
        back_theirs_ref[span, :] = dot(low, out_theirs_ref[...]).astype(BF16)
        back.append(copies.start(back_theirs_ref.at[span, :], back_got_ref.at[span, :], across))
        back_mine_ref[span, :] = dot(low, out_mine_ref[...]).astype(BF16)
        sum_ref[OUT_BIAS : OUT_BIAS + 1, :] += jnp.sum(low.astype(F32), axis=0, keepdims=True)
    locals_.start(grad_mixed_ref, grad_mixed_out)

    result_other_ref[...] = dot_nt(act_ref[1], fc2_ref[...]).astype(BF16)
    locals_.start(result_other_ref, result_other_out)
    result_ref[...] = (
        dot_nt(act_ref[0], fc2_ref[...])
        + mixed_ref[...]
        + vec_ref[FC2_BIAS : FC2_BIAS + 1, :]
    )
    locals_.start(result_ref, result_out)

    def outer(first, second, right_ref, part_ref):
        turned_ref[0] = first.T
        turned_ref[1] = second.T
        step = 256

        def one(index, carry):
            cols = pl.ds(pl.multiple_of(index * step, step), step)
            part_ref[:, cols] = (
                dot(turned_ref[0], right_ref[0, :, cols]) + dot(turned_ref[1], right_ref[1, :, cols])
            ).astype(BF16)
            return carry

        lax.fori_loop(0, units // step, one, 0)

    outer(cot_ref[...], cot_other_ref[...], act_ref, fc2_part_ref)
    locals_.start(fc2_part_ref, fc2_out)
    outer(normed_ref[0], normed_ref[1], hidden_ref, fc1_part_ref)
    locals_.start(fc1_part_ref, fc1_out)
    turned_ref[0] = low_ref[...].T
    out_part_ref[...] = dot(turned_ref[0], attended_ref[...]).astype(BF16)
    locals_.start(out_part_ref, out_out)
    for copy in back:
        copy.wait_recv()
    copies.finish()
    for copy in locals_.made[2:]:
        copy.wait()


def middle(token, token_other, cot, cot_other, place, mine, theirs, vectors, out_mine, out_theirs, fc1, fc2):
    half, width = token.shape
    rows, inner = mine.shape
    units = fc1.shape[1]
    block = lambda cols, kind=BF16: pltpu.VMEM((half, cols), kind)
    pair = lambda cols: pltpu.VMEM((2, half, cols), BF16)
    return pl.pallas_call(
        middle_kernel,
        out_shape=(
            shape((half, width), F32),
            shape((half, inner)),
            shape((half, inner)),
            shape((half, width), F32),
            shape((half, width)),
            shape((width, units)),
            shape((width, units)),
            shape((width, 2 * inner)),
            shape((8, width), F32),
        ),
        in_specs=[VMEM] * 10 + [HERE] * 2,
        out_specs=(HERE, VMEM, VMEM, HERE, HERE, HERE, HERE, HERE, VMEM),
        scratch_shapes=[
            pltpu.VMEM((width, units), BF16),
            pltpu.VMEM((width, units), BF16),
            pair(units),
            pair(units),
            pair(width),
            block(width),
            block(width),
            block(width, F32),
            block(width, F32),
            block(2 * inner),
            block(inner),
            block(width),
            pltpu.VMEM((2, width, half), BF16),
            block(width, F32),
            block(width, F32),
            block(width),
            pltpu.VMEM((width, units), BF16),
            pltpu.VMEM((width, units), BF16),
            pltpu.VMEM((width, 2 * inner), BF16),
            pltpu.SemaphoreType.DMA((4,)),
            pltpu.SemaphoreType.DMA((4,)),
            pltpu.SemaphoreType.DMA((8,)),
        ],
        compiler_params=params(60 << 20, collective_id=1, has_side_effects=True),
        name="middle",
    )(token, token_other, cot, cot_other, place, mine, theirs, vectors, out_mine, out_theirs, fc1, fc2)


def attend_back(rows_ref, low_ref, value_ref, mask_ref, raw_ref, grad_low_ref):
    half, inner = rows_ref.shape
    pair = 2 * HEAD
    lane = iota((half, pair), 1)

    def one_pair(index, carry):
        cols = pl.ds(pl.multiple_of(index * pair, pair), pair)
        key_cols = pl.ds(pl.multiple_of(inner + index * pair, pair), pair)
        value_cols = pl.ds(pl.multiple_of(2 * inner + index * pair, pair), pair)
        query = low_ref[:, cols] * SCALE
        key = low_ref[:, key_cols]
        value = value_ref[:, cols]
        grad = rows_ref[:, cols]
        key_turned = (key.astype(F32) * SCALE).T.astype(BF16)
        grad_values, grad_keys, grad_queries = [], [], []
        for head in range(2):
            mine = lane < HEAD if head == 0 else lane >= HEAD
            query_head = jnp.where(mine, query, jnp.zeros_like(query))
            grad_head = jnp.where(mine, grad, jnp.zeros_like(grad))
            weights = jnp.exp(dot_nt(key, query_head))
            if mask_ref is not None:
                weights = weights * mask_ref[...]
            weights = weights * (1.0 / jnp.sum(weights, axis=0, keepdims=True))
            grad_weights = dot_nt(value, grad_head)
            shared = jnp.sum(weights * grad_weights, axis=0, keepdims=True)
            grad_scores = (weights * (grad_weights - shared)).astype(BF16)
            grad_values.append(dot(weights.astype(BF16), grad))
            grad_keys.append(dot(grad_scores, query))
            grad_queries.append(dot(key_turned[head * HEAD : (head + 1) * HEAD, :], grad_scores))
        raw_ref[:, cols] = jnp.concatenate(grad_queries, axis=0).T
        raw_ref[:, key_cols] = jnp.where(lane < HEAD, grad_keys[0], grad_keys[1])
        grad_low_ref[:, value_cols] = jnp.where(lane < HEAD, grad_values[0], grad_values[1]).astype(BF16)
        return carry

    lax.fori_loop(0, inner // pair, one_pair, 0)


def head_norm_back(raw_ref, unit_ref, scale_ref, vec_ref, grad_low_ref, sum_ref):
    group = 4 * HEAD
    means = head_mean_matrix(group)
    for first in range(0, raw_ref.shape[1], group):
        cols = slice(first, first + group)
        grad = raw_ref[:, cols]
        unit = unit_ref[:, cols]
        sum_ref[QK_GAIN : QK_GAIN + 1, cols] += jnp.sum(grad * unit, axis=0, keepdims=True)
        grad = grad * vec_ref[QK_GAIN : QK_GAIN + 1, cols]
        grad = scale_ref[:, cols] * (
            grad - two_part(grad, means) - unit * two_part(grad * unit, means)
        )
        grad_low_ref[:, cols] = grad.astype(BF16)


class Reduce:
    def __init__(self, place, copies, part_ref, scratch, out_refs):
        self.place, self.copies, self.out_refs = place, copies, out_refs
        (
            self.got_ref,
            self.low_ref,
            self.near_ref,
            self.far_ref,
            self.last_ref,
            self.total_ref,
        ) = scratch
        pack, seq, core, seq_mate, pack_mate = place
        self.cross = copies.start(part_ref.at[:, 1 - core], self.got_ref, seq_mate[1])

    def add(self, own_ref, locals_wait):
        core = self.place[2]
        locals_wait()
        self.cross.wait_recv()
        for index in range(4):
            self.low_ref[index] = (
                own_ref[index].astype(F32) + self.got_ref[index].astype(F32)
            ).astype(BF16)

    def near(self):
        pack, seq, core, seq_mate, pack_mate = self.place
        odd = lax.bitwise_and(pack, 1)
        self.first = [
            self.copies.start(
                self.low_ref.at[(1 - odd) + 2 * index], self.near_ref.at[index], pack_mate[1]
            )
            for index in range(2)
        ]

    def far(self):
        pack, seq, core, seq_mate, pack_mate = self.place
        odd, high = lax.bitwise_and(pack, 1), lax.shift_right_logical(pack, 1)
        for index in range(2):
            self.first[index].wait_recv()
            self.near_ref[index] = (
                self.low_ref[odd + 2 * index].astype(F32) + self.near_ref[index].astype(F32)
            ).astype(BF16)
        self.second = self.copies.start(self.near_ref.at[1 - high], self.far_ref.at[0], pack_mate[2])

    def along(self):
        pack, seq, core, seq_mate, pack_mate = self.place
        high = lax.shift_right_logical(pack, 1)
        self.second.wait_recv()
        self.far_ref[1] = (
            self.near_ref[high].astype(F32) + self.far_ref[0].astype(F32)
        ).astype(BF16)
        self.third = self.copies.start(self.far_ref.at[1], self.last_ref, seq_mate[2])

    def straight(self):
        pack, seq, core, seq_mate, pack_mate = self.place
        self.first = [
            self.copies.start(
                self.low_ref.at[other_of(pack, k)], self.near_ref.at[k - 1], pack_mate[k]
            )
            for k in range(1, 4)
        ]

    def straight_along(self):
        pack, seq, core, seq_mate, pack_mate = self.place
        for copy in self.first:
            copy.wait_recv()
        mine, near = self.low_ref[pack].astype(F32), self.near_ref
        self.far_ref[1] = (
            (mine + near[0].astype(F32)) + (near[1].astype(F32) + near[2].astype(F32))
        ).astype(BF16)
        self.third = self.copies.start(self.far_ref.at[1], self.last_ref, seq_mate[2])

    def own(self, locals_):
        pack, seq, core, seq_mate, pack_mate = self.place
        self.third.wait_recv()
        self.total_ref[...] = self.far_ref[1].astype(F32) + self.last_ref[...].astype(F32)
        rows, width = self.total_ref.shape
        share = width // len(self.out_refs)
        self.fourth = []
        for index, out_ref in enumerate(self.out_refs):
            here = out_ref.at[pl.ds(pl.multiple_of(core * rows, 16), rows), :]
            source = self.total_ref.at[:, index * share : (index + 1) * share]
            self.fourth.append(self.copies.start(source, here, seq_mate[1]))
            locals_.start(source, here)

    def finish(self):
        for copy in self.fourth:
            copy.wait_recv()


def back_kernel(reduces, *refs):
    (
        place_row_ref,
        place_col_ref,
        mode_ref,
        vec_ref,
        back_mine_ref,
        back_other_ref,
        weight_ref,
        sum_in_ref,
        low_all,
        value_all,
        normed_all,
        unit_all,
        head_unit_all,
        head_scale_all,
        result_other_all,
        fc1_all,
        fc2_all,
        out_all,
    ) = refs[:18]
    (
        own_out,
        other_got_ref,
        result_got_ref,
        qkv_out_ref,
        out_out_ref,
        fc1_out_ref,
        fc2_out_ref,
        sum_ref,
    ) = refs[18:26]
    (
        low_ref,
        value_ref,
        normed_ref,
        unit_ref,
        head_unit_ref,
        head_scale_ref,
        sorted_ref,
        got_ref,
        rows_ref,
        raw_ref,
        mask_ref,
        grad_low_ref,
        grad_normed_ref,
        ordered_ref,
        long_ref,
        own_ref,
        other_ref,
        turned_ref,
        qkv_part_ref,
        sum_got_ref,
    ) = refs[26:46]
    reduce_refs = refs[46:-3]
    send_sem, recv_sem, local_sem = refs[-3:]
    half, width = own_ref.shape
    inner = back_mine_ref.shape[1]
    rows = 2 * half
    chunk = half // 4
    steps = range(1, 4)
    pack, seq, side = lax.axis_index("dp"), lax.axis_index("seq"), lax.axis_index("hidden")
    core = lax.bitwise_and(seq, 1)
    across = {"hidden": 1 - side}
    seq_mate = [{"seq": other_of(seq, step)} for step in range(4)]
    pack_mate = [{"dp": other_of(pack, step)} for step in range(4)]
    copies, locals_ = Copies(send_sem, recv_sem), Locals(local_sem)
    place = (pack, seq, core, seq_mate, pack_mate)

    def load(part):
        return [
            locals_.start(source.at[part], target)
            for source, target in (
                (low_all, low_ref),
                (value_all, value_ref),
                (head_unit_all, head_unit_ref),
                (head_scale_all, head_scale_ref),
                (unit_all, unit_ref),
            )
        ]

    load_normed = locals_.start(normed_all, normed_ref)
    loading = load(0)
    greet([across] + seq_mate[1:] + (pack_mate[1:] if reduces else []))

    first = side == 0
    place_own = jnp.where(first, place_row_ref[0:1, :], place_row_ref[1:2, :])
    place_other = jnp.where(first, place_row_ref[1:2, :], place_row_ref[0:1, :])
    moved = []
    for part in range(2):
        target = iota((half, half), 0) + part * half
        found = dot(one_hot(target == place_own), back_mine_ref[...])
        found = found + dot(one_hot(target == place_other), back_other_ref[...])
        sorted_ref[part * half : (part + 1) * half, :] = found.astype(BF16)
        moved.append(
            [
                copies.start(
                    sorted_ref.at[rows_at(part * half + other_of(seq, k) * chunk, chunk), :],
                    got_ref.at[part, k * chunk : (k + 1) * chunk, :],
                    seq_mate[k],
                )
                for k in steps
            ]
        )
    result_cross = copies.start(result_other_all, result_got_ref, across)
    if reduces:
        scratch = [reduce_refs[index * 7 : (index + 1) * 7] for index in range(4)]
        parts = []
        for index, (source, outs) in enumerate(
            ((fc2_all, [fc2_out_ref]), (fc1_all, [fc1_out_ref]), (out_all, [out_out_ref]))
        ):
            mine = locals_.start(source.at[:, core], scratch[index][0])
            parts.append((Reduce(place, copies, source, scratch[index][1:], outs), mine))
        (fc2_sum, fc2_mine), (fc1_sum, fc1_mine), (out_sum, out_mine) = parts
        out_wide_ref, out_got_ref = reduce_refs[28:30]
    load_normed.wait()
    for part in range(2):
        turned_ref[part] = normed_ref[part].T
    mask_ref[...] = image_mask(mode_ref, half)
    work_ref = sum_got_ref.at[9]
    work_ref[...] = sum_in_ref[...]
    if reduces:
        fc2_sum.add(scratch[0][0], fc2_mine.wait)
        fc2_sum.near()
        out_mine.wait()
        out_sum.cross.wait_recv()
        for index in range(4):
            both = scratch[2][0][index].astype(F32) + scratch[2][1][index].astype(F32)
            scratch[2][2][index] = both[:, :inner].astype(BF16)
            out_wide_ref[index] = both[:, inner:].astype(BF16)
        out_cross = copies.start(out_wide_ref, out_got_ref, across)
        fc1_sum.add(scratch[1][0], fc1_mine.wait)
        fc1_sum.near()

    wide = width // 2
    pieces = [slice(0, wide), slice(wide, width)]

    def attention(part):
        for copy in moved[part]:
            copy.wait_recv()
        fill_sequence(part, seq, mode_ref, sorted_ref, got_ref, rows_ref)
        for copy in loading:
            copy.wait()
        grad_low = grad_low_ref.at[part]
        attend_back(rows_ref, low_ref, value_ref, mask_ref if part else None, raw_ref, grad_low)
        head_norm_back(raw_ref, head_unit_ref, head_scale_ref, vec_ref, grad_low, work_ref)
        total = dot_nt(grad_low[:, :inner], weight_ref[0])
        total = total + dot_nt(grad_low[:, inner : 2 * inner], weight_ref[1])
        total = total + dot_nt(grad_low[:, 2 * inner :], weight_ref[2])
        work_ref[LN1_GAIN : LN1_GAIN + 1, :] += jnp.sum(
            total * unit_ref[...].astype(F32), axis=0, keepdims=True
        )
        work_ref[LN1_BIAS : LN1_BIAS + 1, :] += jnp.sum(total, axis=0, keepdims=True)
        grad_normed_ref[part] = total.astype(BF16)
        target_ref = ordered_ref if part == 0 else long_ref
        target_ref[rows_at(seq * chunk, chunk), :] = grad_normed_ref[part, 0:chunk, :]
        return [
            [
                copies.start(
                    grad_normed_ref.at[part, k * chunk : (k + 1) * chunk, cols],
                    target_ref.at[rows_at(seq * chunk, chunk), cols],
                    seq_mate[k],
                )
                for k in steps
            ]
            for cols in ([slice(0, width)] if part == 0 else pieces)
        ]

    returned = attention(0)
    loading = load(1)
    if reduces:
        fc2_sum.far()
        out_cross.wait_recv()
        for index in range(4):
            out_sum.low_ref[index] = (
                out_sum.low_ref[index].astype(F32) + out_got_ref[index].astype(F32)
            ).astype(BF16)
        out_sum.near()
    returned += attention(1)

    sums = copies.start(work_ref, sum_got_ref.at[0], across)
    for index in range(8):
        share = width // 8
        span = slice(index * share, (index + 1) * share)
        qkv_part_ref[index // 2, index % 2] = (
            dot(turned_ref[0, span, :], grad_low_ref[0]) + dot(turned_ref[1, span, :], grad_low_ref[1])
        ).astype(BF16)
    if reduces:
        qkv_sum = Reduce(
            place, copies, qkv_part_ref, scratch[3][1:], [qkv_out_ref.at[k] for k in range(3)]
        )
        fc1_sum.far()
        out_sum.far()
        fc2_sum.along()
        qkv_sum.cross.wait_recv()
        for index in range(4):
            qkv_sum.low_ref[index] = (
                qkv_part_ref[index, core].astype(F32) + qkv_sum.got_ref[index].astype(F32)
            ).astype(BF16)
        qkv_sum.straight()
    else:
        keep = locals_.start(qkv_part_ref, qkv_out_ref)

    def unsort(target_ref, which, cols):
        start = pl.multiple_of(which * half, 16)
        back = one_hot(place_col_ref[pl.ds(start, half), :] == iota((half, rows), 1))
        target_ref[:, cols] = dot(back, ordered_ref[:, cols]).astype(BF16)

    for copy in returned[0]:
        copy.wait_recv()
    crossing = []
    for cols, coming in zip(pieces, returned[1:]):
        for copy in coming:
            copy.wait_recv()
        ordered_ref[half:, cols] = jnp.where(
            mode_ref[0:1, 0:1] > 0,
            long_ref[:, cols].astype(F32),
            grad_normed_ref[1, :, cols].astype(F32),
        ).astype(BF16)
        unsort(other_ref, 1 - side, cols)
        crossing.append(copies.start(other_ref.at[:, cols], other_got_ref.at[:, cols], across))
    sums.wait_recv()
    sum_got_ref[1] = work_ref[...] + sum_got_ref[0]
    around = [copies.start(sum_got_ref.at[1], sum_got_ref.at[1 + k], seq_mate[k]) for k in steps]
    unsort(own_ref, side, slice(0, width))
    own_copy = locals_.start(own_ref, own_out)
    for copy in around:
        copy.wait_recv()
    sum_got_ref[5] = (sum_got_ref[1] + sum_got_ref[2]) + (sum_got_ref[3] + sum_got_ref[4])
    if reduces:
        through = [copies.start(sum_got_ref.at[5], sum_got_ref.at[5 + k], pack_mate[k]) for k in steps]
        fc1_sum.along()
        out_sum.along()
        fc2_sum.own(locals_)
        qkv_sum.straight_along()
        fc1_sum.own(locals_)
        out_sum.own(locals_)
        for copy in through:
            copy.wait_recv()
        sum_ref[...] = (sum_got_ref[5] + sum_got_ref[6]) + (sum_got_ref[7] + sum_got_ref[8])
        qkv_sum.own(locals_)
        for each in (fc1_sum, fc2_sum, out_sum, qkv_sum):
            each.finish()
    else:
        sum_ref[...] = sum_got_ref[5]
        keep.wait()
    for copy in crossing:
        copy.wait_recv()
    result_cross.wait_recv()
    copies.finish()
    own_copy.wait()
    if reduces:
        for copy in locals_.made[-6:]:
            copy.wait()


def back(reduces, place_row, place_col, mode, vectors, back_mine, back_other, weight, sums, kept, result_other, fc1_part, fc2_part, out_part, packs):
    normed, unit, low, value, head_unit, head_scale = kept
    half, width = result_other.shape
    inner = back_mine.shape[1]
    units = fc1_part.shape[1]
    share = width // packs
    rows = 2 * half
    block = lambda cols, kind=BF16: pltpu.VMEM((half, cols), kind)
    pair = lambda cols: pltpu.VMEM((2, half, cols), BF16)
    cut = (4, 2, width // 8)
    piece = width // 8

    def summing(columns, wide, owns, near):
        return [
            pltpu.VMEM((4, piece, wide) if owns else (8, 128), BF16),
            pltpu.VMEM((4, piece, wide), BF16),
            pltpu.VMEM((4, piece, columns), BF16),
            pltpu.VMEM((near, piece, columns), BF16),
            pltpu.VMEM((2, piece, columns), BF16),
            pltpu.VMEM((piece, columns), BF16),
            pltpu.VMEM((piece, columns), F32),
        ]

    reduce_scratch = []
    if reduces:
        reduce_scratch = (
            summing(units, units, True, 2)
            + summing(units, units, True, 2)
            + summing(inner, 2 * inner, True, 2)
            + summing(3 * inner, 3 * inner, False, 3)
            + [pltpu.VMEM((4, piece, inner), BF16)] * 2
        )
    copies = 6 + 1 + 9 + 1 + 3 + 2 + (3 + 3 * 6 + 1 + 8 if reduces else 0)
    return pl.pallas_call(
        functools.partial(back_kernel, reduces),
        out_shape=(
            shape((half, width)),
            shape((half, width)),
            shape((half, width)),
            shape((3, share, inner), F32) if reduces else shape((*cut, 3 * inner)),
            shape((share, inner), F32),
            shape((share, units), F32),
            shape((share, units), F32),
            shape((8, width), F32),
        ),
        in_specs=[VMEM] * 8 + [HERE] * 10,
        out_specs=(HERE,) * 7 + (VMEM,),
        scratch_shapes=[
            block(2 * inner),
            block(inner),
            pair(width),
            block(width),
            block(2 * inner, F32),
            block(2 * inner, F32),
            pltpu.VMEM((rows, inner), BF16),
            pair(inner),
            block(inner),
            block(2 * inner, F32),
            pltpu.VMEM((half, half), F32),
            pair(3 * inner),
            pair(width),
            pltpu.VMEM((rows, width), BF16),
            block(width),
            block(width),
            block(width),
            pltpu.VMEM((2, width, half), BF16),
            pltpu.VMEM((*cut, 3 * inner), BF16),
            pltpu.VMEM((10, 8, width), F32),
        ]
        + reduce_scratch
        + [
            pltpu.SemaphoreType.DMA((copies,)),
            pltpu.SemaphoreType.DMA((copies,)),
            pltpu.SemaphoreType.DMA((24,)),
        ],
        compiler_params=params(63 << 20, collective_id=2, has_side_effects=True),
        name="back",
    )(
        place_row,
        place_col,
        mode,
        vectors,
        back_mine,
        back_other,
        weight,
        sums,
        low,
        value,
        normed,
        unit,
        head_unit,
        head_scale,
        result_other,
        fc1_part.reshape(*cut, -1),
        fc2_part.reshape(*cut, -1),
        out_part.reshape(*cut, -1),
    )


def finish_kernel(*refs):
    tok_ref, own_ref, got_ref, grad_mixed_ref, result_ref, result_got_ref, vec_ref, sum_ref = refs[:8]
    sources, refs = refs[8:12], refs[12:]
    output_ref, input_grad_ref = refs[:2]
    vec_outs, gain_out, targets = refs[2:8], refs[8], refs[9:13]
    for source, target in zip(sources, targets):
        target[...] = source[...]

    @pl.when(pl.program_id(0) == 0)
    def _():
        pack = lax.axis_index("dp")
        share, width = vec_outs[0].shape[0], vec_ref.shape[1]
        sums = sum_ref[...]
        mine = sum(
            jnp.where(pack == index, sums[:, index * share : (index + 1) * share], 0.0)
            for index in range(width // share)
        )
        for index, out_ref in enumerate(vec_outs):
            out_ref[...] = mine[index : index + 1, :].reshape(share)
        few = gain_out.shape[1]
        for index in range(2):
            row = sums[QK_GAIN : QK_GAIN + 1, index * width // 2 : (index + 1) * width // 2]
            row = sum(row[:, first : first + HEAD] for first in range(0, width // 2, HEAD))
            gain_out[index : index + 1, :] = sum(
                jnp.where(pack == place, row[:, place * few : (place + 1) * few], 0.0)
                for place in range(HEAD // few)
            )

    output_ref[...] = (result_ref[...] + result_got_ref[...].astype(F32)).astype(BF16)
    unit, scale = row_norm(tok_ref[...].astype(F32))
    grad = own_ref[...].astype(F32) + got_ref[...].astype(F32)
    grad = row_norm_back(grad * vec_ref[LN1_GAIN : LN1_GAIN + 1, :], unit, scale)
    input_grad_ref[...] = (grad_mixed_ref[...] + grad).astype(BF16)


def finish(token, own, got, grad_mixed, result, result_got, vectors, sums, arrays, share, few):
    half, width = token.shape
    tile = half // 4
    by_row = pl.BlockSpec((tile, width), lambda i: (i, 0))
    whole = pl.BlockSpec((8, width), lambda i: (0, 0))
    parts = 4 if share % 32 == 0 else 1

    def block(array):
        lead = array.shape[:-2]
        dims = (*lead, share // parts, array.shape[-1])
        return pl.BlockSpec(dims, lambda i: (*(0,) * len(lead), i if parts > 1 else 0, 0))

    return pl.pallas_call(
        finish_kernel,
        out_shape=[shape((half, width))] * 2
        + [shape((share,), F32)] * 6
        + [shape((2, few), F32)]
        + [shape(array.shape, F32) for array in arrays],
        grid=(half // tile,),
        in_specs=[by_row] * 6 + [whole] * 2 + [block(array) for array in arrays],
        out_specs=[by_row] * 2
        + [pl.BlockSpec((share,), lambda i: (0,))] * 6
        + [pl.BlockSpec((2, few), lambda i: (0, 0))]
        + [block(array) for array in arrays],
        compiler_params=params(60 << 20, dimension_semantics=("arbitrary",)),
        name="finish",
    )(token, own, got, grad_mixed, result, result_got, vectors, sums, *arrays)


def swap(array, axis, step):
    pairs = [(index, index ^ step) for index in range(lax.axis_size(axis))]
    return lax.ppermute(array, axis, pairs)


def owned_sum(part, dim):
    total = lax.psum_scatter(part.astype(BF16), "dp", scatter_dimension=dim, tiled=True)
    total = (total.astype(F32) + swap(total, "seq", 1).astype(F32)).astype(BF16)
    return total.astype(F32) + swap(total, "seq", 2).astype(F32)


def local(
    tokens,
    segment,
    cotangent,
    ln1_gain,
    ln1_bias,
    qkv_weight,
    qk_gain,
    out_weight,
    out_bias,
    ln2_gain,
    ln2_bias,
    fc1_weight,
    fc2_weight,
    fc2_bias,
):
    half, width = tokens.shape
    packs = lax.axis_size("dp")
    inner = qkv_weight.shape[2]
    share = ln1_gain.shape[0]
    gathers = packs == 4
    pack = lax.axis_index("dp")
    pieces = [ln1_gain, ln1_bias, out_bias, ln2_gain, ln2_bias, fc2_bias]
    if gathers:
        vectors = [*pieces, qk_gain]
    else:
        few = qk_gain.shape[1]
        lanes = jnp.arange(width)
        wide = jnp.where(lanes // share == pack, jnp.tile(jnp.stack(pieces).astype(F32), (1, packs)), 0.0)
        gains = jnp.tile(qk_gain.astype(F32), (1, width // (2 * few))).reshape(1, width)
        gains = jnp.where(lanes % HEAD // few == pack, gains, 0.0)
        vectors = jnp.concatenate([wide, gains, jnp.zeros((1, width), F32)], axis=0)
        vectors = [lax.psum(vectors, "dp")]
        qkv_weight = lax.all_gather(qkv_weight, "dp", axis=1, tiled=True)
    (
        tokens_other,
        cot_other,
        place_row,
        place_col,
        mode,
        vectors,
        mine,
        theirs,
        qkv_full,
        out_mine,
        out_theirs,
        fc1_full,
        fc2_full,
        *kept,
    ) = front(
        gathers, tokens, cotangent, segment, vectors, qkv_weight, out_weight.T, fc1_weight,
        fc2_weight.T,
    )
    if not gathers:
        out_mine = lax.all_gather(out_weight.T, "dp", axis=0, tiled=True)
        out_theirs = swap(out_mine, "hidden", 1)
        fc1_full = lax.all_gather(fc1_weight, "dp", axis=0, tiled=True)
        fc2_full = lax.all_gather(fc2_weight.T, "dp", axis=0, tiled=True)
    (
        grad_mixed,
        back_mine,
        back_other,
        result,
        result_other,
        fc1_part,
        fc2_part,
        out_part,
        sums,
    ) = middle(
        tokens, tokens_other, cotangent, cot_other, place_col, mine, theirs, vectors, out_mine,
        out_theirs, fc1_full, fc2_full,
    )
    own, got, result_got, qkv_owned, out_owned, fc1_owned, fc2_owned, sums = back(
        gathers, place_row, place_col, mode, vectors, back_mine, back_other, qkv_full, sums, kept,
        result_other, fc1_part, fc2_part, out_part, packs,
    )
    if not gathers:
        sums = lax.psum(sums, "dp")
        qkv_part = jnp.moveaxis(qkv_owned.reshape(width, 3, inner), 1, 0)
        qkv_owned = owned_sum(qkv_part, 1)
        out_part = out_part[:, :inner].astype(F32) + swap(out_part[:, inner:], "hidden", 1).astype(F32)
        out_owned = owned_sum(out_part, 0)
        fc1_owned = owned_sum(fc1_part, 0)
        fc2_owned = owned_sum(fc2_part, 0)
    output, input_grad, *sums, qk_owned, qkv_owned, out_owned, fc1_owned, fc2_owned = finish(
        tokens, own, got, grad_mixed, result, result_got, vectors, sums,
        [qkv_owned, out_owned, fc1_owned, fc2_owned], share, qk_gain.shape[1],
    )
    return (
        output,
        input_grad,
        sums[LN1_GAIN],
        sums[LN1_BIAS],
        qkv_owned,
        qk_owned,
        out_owned.T,
        sums[OUT_BIAS],
        sums[LN2_GAIN],
        sums[LN2_BIAS],
        fc1_owned,
        fc2_owned.T,
        sums[FC2_BIAS],
    )


def solution(mesh):
    rows = P(("dp", "seq", "hidden"), None)
    in_specs = (
        rows,
        P("dp"),
        rows,
        P("dp"),
        P("dp"),
        P(None, "dp", "hidden"),
        P(None, "dp"),
        P("hidden", "dp"),
        P("dp"),
        P("dp"),
        P("dp"),
        P("dp", "hidden"),
        P("hidden", "dp"),
        P("dp"),
    )
    out_specs = (
        rows,
        rows,
        P("dp"),
        P("dp"),
        P(None, "dp", "hidden"),
        P(None, "dp"),
        P("hidden", "dp"),
        P("dp"),
        P("dp"),
        P("dp"),
        P("dp", "hidden"),
        P("hidden", "dp"),
        P("dp"),
    )
    return jax.shard_map(local, mesh=mesh, in_specs=in_specs, out_specs=out_specs, check_vma=False)
```

```python
import functools

import jax
import jax.numpy as jnp
from jax import lax
from jax.experimental import pallas as pl
from jax.experimental.pallas import tpu as pltpu
from jax.sharding import PartitionSpec as P

HEAD = 64
LONG = 576
IMAGE = 64
LABELS = 128
EPSILON = 1e-06
SCALE = HEAD ** (-0.5)
F32 = jnp.float32
BF16 = jnp.bfloat16

VMEM = pl.BlockSpec(memory_space=pltpu.VMEM)
SMEM = pl.BlockSpec(memory_space=pltpu.SMEM)
HERE = pl.BlockSpec(memory_space=pl.ANY)
LN1_GAIN, LN1_BIAS, OUT_BIAS, LN2_GAIN, LN2_BIAS, FC2_BIAS, QK_GAIN = range(7)


def params(limit=56 << 20, **more):
    return pltpu.CompilerParams(vmem_limit_bytes=limit, **more)


def shape(dims, dtype=BF16):
    return jax.ShapeDtypeStruct(dims, dtype)


def dot(left, right):
    return jnp.dot(left, right, preferred_element_type=F32)


def dot_nt(left, right):
    return lax.dot_general(left, right, (((1,), (1,)), ((), ())), preferred_element_type=F32)


def dot_tn(left, right):
    return lax.dot_general(left, right, (((0,), (0,)), ((), ())), preferred_element_type=F32)


def iota(dims, dim):
    return lax.broadcasted_iota(jnp.int32, dims, dim)


def one_hot(test):
    return jnp.where(test, 1.0, 0.0).astype(BF16)


def two_part(values, matrix):
    high = values.astype(BF16)
    rest = (values - high.astype(F32)).astype(BF16)
    return dot(high, matrix) + dot(rest, matrix)


def head_mean_matrix(width):
    return jnp.where(
        iota((width, width), 0) // HEAD == iota((width, width), 1) // HEAD, 1.0 / HEAD, 0.0
    ).astype(BF16)


def row_norm(values):
    mean = jnp.mean(values, axis=-1, keepdims=True)
    centred = values - mean
    spread = jnp.mean(centred * centred, axis=-1, keepdims=True)
    scale = lax.rsqrt(spread + EPSILON)
    return centred * scale, scale


def row_norm_back(grad_unit, unit, scale):
    first = jnp.mean(grad_unit, axis=-1, keepdims=True)
    second = jnp.mean(grad_unit * unit, axis=-1, keepdims=True)
    return scale * (grad_unit - first - unit * second)


def normal_cdf(values):
    size = jnp.abs(values) * (2.0 ** -0.5)
    bell = jnp.exp(-0.5 * values * values)
    t = 1.0 / (1.0 + 0.3275911 * size)
    poly = 1.061405429 * t - 1.453152027
    poly = poly * t + 1.421413741
    poly = poly * t - 0.284496736
    poly = poly * t + 0.254829592
    tail = 0.5 * (poly * t) * bell
    return jnp.where(values < 0, tail, 1.0 - tail), bell * 0.3989422804014327


def other_of(value, step):
    return lax.bitwise_xor(value, jnp.int32(step))


def rows_at(start, size):
    return pl.ds(pl.multiple_of(start, 16), size)


class Copies:
    def __init__(self, send_sem, recv_sem):
        self.send_sem, self.recv_sem = send_sem, recv_sem
        self.made = []

    def start(self, source, target, device):
        index = len(self.made)
        copy = pltpu.make_async_remote_copy(
            src_ref=source,
            dst_ref=target,
            send_sem=self.send_sem.at[index],
            recv_sem=self.recv_sem.at[index],
            device_id=device,
            device_id_type=pl.DeviceIdType.MESH,
        )
        copy.start()
        self.made.append(copy)
        return copy

    def finish(self):
        for copy in self.made:
            copy.wait_send()


class Locals:
    def __init__(self, sem):
        self.sem, self.made = sem, []

    def start(self, source, target):
        copy = pltpu.make_async_copy(source, target, self.sem.at[len(self.made)])
        copy.start()
        self.made.append(copy)
        return copy

    def finish(self):
        for copy in self.made:
            copy.wait()


def greet(devices):
    barrier = pltpu.get_barrier_semaphore()
    for device in devices:
        pl.semaphore_signal(barrier, inc=1, device_id=device, device_id_type=pl.DeviceIdType.MESH)
    pl.semaphore_wait(barrier, len(devices))


def place_rows(labels, place_row_ref, place_col_ref, mode_ref, places_ref):
    rows = labels.shape[1]
    half = rows // 2
    chunk = LONG // 4
    by_row = jnp.where(labels == iota((LABELS, rows), 0), 1.0, 0.0)
    count = jnp.sum(by_row, axis=1, keepdims=True)
    cut = 0.5 * (chunk + IMAGE)
    long = jnp.where(count > cut, count, 0.0)
    small = count - long
    total = jnp.sum(long, axis=0, keepdims=True)
    left = iota((LABELS, LABELS), 0)
    right = iota((LABELS, LABELS), 1)

    def before(counts):
        turned = jnp.broadcast_to(counts, (LABELS, LABELS)).T
        return jnp.sum(jnp.where(right < left, turned, 0.0), axis=1, keepdims=True)

    base = jnp.where(long > 0, before(long), total + before(small))
    earlier = one_hot(left < right)
    for first in range(0, rows, LABELS):
        cols = slice(first, first + LABELS)
        block = by_row[:, cols]
        place = base + dot(block.astype(BF16), earlier)
        base = base + jnp.sum(block, axis=1, keepdims=True)
        place = jnp.sum(block * place, axis=0, keepdims=True)
        places_ref[0:1, cols] = place.astype(jnp.int32)
        turned = jnp.broadcast_to(place, (LABELS, LABELS)).T
        place_col_ref[cols, :] = turned[:, 0:1].astype(jnp.int32)
    place_row_ref[0:1, :] = places_ref[0:1, :half]
    place_row_ref[1:2, :] = places_ref[0:1, half:]
    mode_ref[...] = jnp.broadcast_to(jnp.where(total > rows - IMAGE, 1.0, 0.0), mode_ref.shape)


def sorting(place_ref, side, hot_ref):
    half = place_ref.shape[1]
    first = side == 0
    place_own = jnp.where(first, place_ref[0:1, :], place_ref[1:2, :])
    place_other = jnp.where(first, place_ref[1:2, :], place_ref[0:1, :])
    for part in range(2):
        target = iota((half, half), 0) + part * half
        hot_ref[0, part * half : (part + 1) * half, :] = one_hot(target == place_own)
        hot_ref[1, part * half : (part + 1) * half, :] = one_hot(target == place_other)


def put_vectors(pieces, gain_ref, pack, vec_ref):
    share, width = pieces[0].shape[0], vec_ref.shape[1]
    at = one_hot(iota((share, width), 1) == iota((share, width), 0) + pack * share)
    vec_ref[...] = jnp.zeros_like(vec_ref)
    for index, piece in enumerate(pieces):
        row = piece[...].astype(F32).reshape(1, share)
        row = jnp.broadcast_to(row, (8, share)).astype(BF16)
        vec_ref[index : index + 1, :] = dot(row, at)[0:1, :]
    few, half = gain_ref.shape[1], width // 2
    at = one_hot(lax.bitwise_and(iota((few, half), 1), HEAD - 1) == iota((few, half), 0) + pack * few)
    gains = dot(gain_ref[...], at)
    vec_ref[QK_GAIN : QK_GAIN + 1, :half] = gains[0:1, :]
    vec_ref[QK_GAIN : QK_GAIN + 1, half:] = gains[1:2, :]


def fill_sequence(part, seq, mode_ref, sorted_ref, got_ref, rows_ref):
    half = rows_ref.shape[0]
    chunk = half // 4
    home = sorted_ref[rows_at(part * half + seq * chunk, chunk), :]
    for step in range(4):
        rows = home if step == 0 else got_ref[part, step * chunk : (step + 1) * chunk, :]
        if part == 1:
            local = sorted_ref[half + step * chunk : half + (step + 1) * chunk, :]
            rows = jnp.where(mode_ref[0:1, 0:1] > 0, rows.astype(F32), local.astype(F32))
        rows_ref[step * chunk : (step + 1) * chunk, :] = rows.astype(BF16)


def image_mask(mode_ref, rows):
    same = lax.shift_right_logical(iota((rows, rows), 0), 6) == lax.shift_right_logical(
        iota((rows, rows), 1), 6
    )
    return jnp.where(same, 1.0, mode_ref[0:1, 0:1])


def project(part, rows_ref, weight_ref, vec_ref, kept, raw_ref):
    normed_ref, unit_ref, low_ref, value_ref, head_unit_ref, head_scale_ref = (
        ref.at[part] for ref in kept
    )
    half, width = rows_ref.shape
    inner = value_ref.shape[1]
    chunk = half // 4
    for step in range(4):
        rows = slice(step * chunk, (step + 1) * chunk)
        unit, _ = row_norm(rows_ref[rows, :].astype(F32))
        unit_ref[rows, :] = unit.astype(BF16)
        normed = unit * vec_ref[LN1_GAIN : LN1_GAIN + 1, :] + vec_ref[LN1_BIAS : LN1_BIAS + 1, :]
        normed_ref[rows, :] = normed.astype(BF16)
    raw_ref[:, :inner] = dot(normed_ref[...], weight_ref[0])
    raw_ref[:, inner:] = dot(normed_ref[...], weight_ref[1])
    value_ref[...] = dot(normed_ref[...], weight_ref[2]).astype(BF16)
    group = 4 * HEAD
    means = head_mean_matrix(group)
    for first in range(0, 2 * inner, group):
        cols = slice(first, first + group)
        raw = raw_ref[:, cols]
        centred = raw - two_part(raw, means)
        scale = lax.rsqrt(two_part(centred * centred, means) + EPSILON)
        unit = centred * scale
        head_unit_ref[:, cols] = unit
        head_scale_ref[:, cols] = scale
        low_ref[:, cols] = (unit * vec_ref[QK_GAIN : QK_GAIN + 1, cols]).astype(BF16)


def attend(part, kept, mask_ref, attended_ref):
    low_ref, value_ref = kept[2].at[part], kept[3].at[part]
    half, inner = value_ref.shape
    pair = 2 * HEAD
    lane = iota((half, pair), 1)

    def one_pair(index, carry):
        cols = pl.ds(pl.multiple_of(index * pair, pair), pair)
        key_cols = pl.ds(pl.multiple_of(inner + index * pair, pair), pair)
        query = low_ref[:, cols] * SCALE
        key = low_ref[:, key_cols]
        value = jnp.concatenate([value_ref[:, cols], jnp.ones((half, pair), BF16)], axis=1)
        found = []
        for head in range(2):
            mine = lane < HEAD if head == 0 else lane >= HEAD
            scores = dot_nt(jnp.where(mine, query, jnp.zeros_like(query)), key)
            weights = jnp.exp(scores).astype(BF16)
            if part == 1:
                weights = weights * mask_ref[...]
            both = dot(weights, value)
            found.append(both[:, :pair] / both[:, pair:])
        attended_ref[part, :, cols] = jnp.where(lane < HEAD, found[0], found[1]).astype(BF16)
        return carry

    lax.fori_loop(0, inner // pair, one_pair, 0)


KEPT = 6


def front_kernel(gathers, *refs):
    tok_ref, cot_ref, seg_ref, qkv_ref, out_ref, fc1_ref, fc2_ref = refs[:7]
    vec_in_refs, refs = (refs[7:14], refs[14:]) if gathers else (refs[7:8], refs[8:])
    (
        tok_other_ref,
        cot_other_ref,
        place_row_ref,
        place_col_ref,
        mode_ref,
        vec_ref,
        mine_ref,
        theirs_ref,
        qkv_all_ref,
        out_all_ref,
        out_theirs_ref,
        fc1_all_ref,
        fc2_all_ref,
    ) = refs[:13]
    kept_out = refs[13 : 13 + KEPT]
    (
        sorted_ref,
        got_ref,
        rows_ref,
        raw_ref,
        mask_ref,
        attended_ref,
        back_ref,
        vec_got_ref,
        hot_ref,
        places_ref,
        out_pair_ref,
    ) = refs[13 + KEPT : 24 + KEPT]
    share_refs = refs[24 + KEPT : 27 + KEPT]
    kept = refs[27 + KEPT : 27 + 2 * KEPT]
    send_sem, recv_sem, local_sem = refs[27 + 2 * KEPT :]
    pack, seq, side = lax.axis_index("dp"), lax.axis_index("seq"), lax.axis_index("hidden")
    core = lax.bitwise_and(seq, 1)
    half, width = tok_ref.shape
    chunk = half // 4
    steps = range(1, 4)
    across = {"hidden": 1 - side}
    seq_mate = [{"seq": other_of(seq, step)} for step in range(4)]
    pack_mate = [{"dp": other_of(pack, step)} for step in range(4)]
    greet([across] + seq_mate[1:] + (pack_mate[1:] if gathers else []))
    copies, locals_ = Copies(send_sem, recv_sem), Locals(local_sem)

    wide = width // 3
    pieces = [slice(first, first + wide) for first in range(0, width, wide)]
    tokens = [copies.start(tok_ref.at[:, c], tok_other_ref.at[:, c], across) for c in pieces]
    whole = fc1_ref.shape[0]
    in_flight = []

    def rows_of(ref, index, piece, size):
        rows = rows_at(index * whole + piece * size, size)
        return ref.at[:, rows, :] if len(ref.shape) == 3 else ref.at[rows, :]

    class Half:
        def __init__(self, source, target):
            self.target, self.size = target, whole // 2
            self.first = [
                copies.start(
                    rows_of(source, 0, core, self.size),
                    rows_of(target, pack, core, self.size),
                    pack_mate[k],
                )
                for k in steps
            ]

        def share(self):
            for k in steps:
                self.first[k - 1].wait_recv()
                there = rows_of(self.target, other_of(pack, k), core, self.size)
                in_flight.append(copies.start(there, there, seq_mate[1]))

    class Quarter:
        def __init__(self, source, target):
            self.target, self.size = target, whole // 4
            self.first = [
                copies.start(
                    rows_of(source, 0, seq, self.size),
                    rows_of(target, pack, seq, self.size),
                    pack_mate[k],
                )
                for k in steps
            ]
            self.second = []

        def there(self, k, piece):
            return rows_of(self.target, other_of(pack, k), piece, self.size)

        def pass_on(self):
            for k in steps:
                self.first[k - 1].wait_recv()
                there = self.there(k, seq)
                self.second.append(copies.start(there, there, seq_mate[2]))
            for k in steps:
                there = self.there(k, seq)
                in_flight.append(copies.start(there, there, seq_mate[1]))

        def share(self):
            for k in steps:
                self.second[k - 1].wait_recv()
                there = self.there(k, other_of(seq, 2))
                in_flight.append(copies.start(there, there, seq_mate[1]))

    if gathers:
        gather_qkv = Quarter(qkv_ref, qkv_all_ref)
        put_vectors(vec_in_refs[:6], vec_in_refs[6], pack, vec_got_ref.at[3])
        gather_vec = [
            copies.start(vec_got_ref.at[3], vec_got_ref.at[k - 1], pack_mate[k]) for k in steps
        ]
        pair_out = copies.start(out_ref, out_pair_ref, across)
        gather_out = Half(out_ref, out_all_ref)
        gather_fc2 = Quarter(fc2_ref, fc2_all_ref)
        keep = [locals_.start(qkv_ref, qkv_all_ref.at[:, rows_at(pack * whole, whole), :])] + [
            locals_.start(source, target)
            for source, target in zip((out_ref, fc1_ref, fc2_ref), share_refs)
        ]
    else:
        keep = [locals_.start(qkv_ref, qkv_all_ref)]
    rows = 2 * half
    labels = seg_ref[...]
    place_rows(
        sum(
            jnp.where(seq == index, labels[index * rows : (index + 1) * rows].reshape(1, rows), 0)
            for index in range(4)
        ),
        place_row_ref,
        place_col_ref,
        mode_ref,
        places_ref,
    )
    sorting(place_row_ref, side, hot_ref)
    mask_ref[...] = image_mask(mode_ref, half).astype(BF16)

    if gathers:
        gather_qkv.pass_on()
    moved = [[], []]
    for piece, cols in enumerate(pieces):
        tokens[piece].wait_recv()
        for part in range(2):
            span = slice(part * half, (part + 1) * half)
            found = dot(hot_ref[0, span, :], tok_ref[:, cols])
            found = found + dot(hot_ref[1, span, :], tok_other_ref[:, cols])
            sorted_ref[span, cols] = found.astype(BF16)
            for k in steps:
                start = part * half + other_of(seq, k) * chunk
                moved[part].append(
                    copies.start(
                        sorted_ref.at[rows_at(start, chunk), cols],
                        got_ref.at[part, k * chunk : (k + 1) * chunk, cols],
                        seq_mate[k],
                    )
                )
    cots = copies.start(cot_ref, cot_other_ref, across)
    if gathers:
        pair_out.wait_recv()
        for copy in keep[1:]:
            copy.wait()
        for source, target in zip(
            (*share_refs, out_pair_ref), (out_all_ref, fc1_all_ref, fc2_all_ref, out_theirs_ref)
        ):
            locals_.start(source, target.at[rows_at(pack * whole, whole), :])
        gather_theirs = Half(out_pair_ref, out_theirs_ref)
        gather_fc1 = Half(fc1_ref, fc1_all_ref)
        gather_qkv.share()
        needed = list(in_flight)
        for k in steps:
            gather_vec[k - 1].wait_recv()
        vec_ref[...] = (vec_got_ref[3] + vec_got_ref[0]) + (vec_got_ref[1] + vec_got_ref[2])
        for copy in needed:
            copy.wait_recv()
            in_flight.remove(copy)
    else:
        vec_ref[...] = vec_in_refs[0][...]
    keep[0].wait()

    def begin(part):
        for copy in moved[part]:
            copy.wait_recv()
        fill_sequence(part, seq, mode_ref, sorted_ref, got_ref, rows_ref)
        project(part, rows_ref, qkv_all_ref, vec_ref, kept, raw_ref)

    def give_back(part, target_ref):
        target_ref[rows_at(seq * chunk, chunk), :] = attended_ref[part, 0:chunk, :]
        given = [
            copies.start(
                attended_ref.at[part, k * chunk : (k + 1) * chunk, :],
                target_ref.at[rows_at(seq * chunk, chunk), :],
                seq_mate[k],
            )
            for k in steps
        ]
        for ref, out in zip(kept, kept_out):
            locals_.start(ref.at[part], out.at[part])
        return given

    begin(0)
    attend(0, kept, mask_ref, attended_ref)
    given = give_back(0, mine_ref)
    begin(1)
    attend(1, kept, mask_ref, attended_ref)
    given_long = give_back(1, back_ref)
    if gathers:
        gather_fc2.pass_on()
        gather_out.share()
    for copy in given:
        copy.wait_recv()
    first = copies.start(mine_ref.at[0:half, :], theirs_ref.at[0:half, :], across)
    for copy in given_long:
        copy.wait_recv()
    mine_ref[half:, :] = jnp.where(
        mode_ref[0:1, 0:1] > 0, back_ref[...].astype(F32), attended_ref[1].astype(F32)
    ).astype(BF16)
    second = copies.start(mine_ref.at[half : 2 * half, :], theirs_ref.at[half : 2 * half, :], across)
    if gathers:
        gather_theirs.share()
        gather_fc2.share()
        gather_fc1.share()
        for copy in in_flight:
            copy.wait_recv()
    cots.wait_recv()
    first.wait_recv()
    second.wait_recv()
    copies.finish()
    for copy in locals_.made[4 if gathers else 1 :]:
        copy.wait()


def front(gathers, tokens, cotangent, segment, vectors, qkv, out, fc1, fc2):
    half, width = tokens.shape
    rows = 2 * half
    share, inner = out.shape
    units = fc1.shape[1]
    kept = [
        ((2, half, width), BF16),
        ((2, half, width), BF16),
        ((2, half, 2 * inner), BF16),
        ((2, half, inner), BF16),
        ((2, half, 2 * inner), F32),
        ((2, half, 2 * inner), F32),
    ]
    whole = width if gathers else share
    outs = [
        (shape((half, width)), VMEM),
        (shape((half, width)), HERE),
        (shape((2, half), jnp.int32), VMEM),
        (shape((rows, 1), jnp.int32), VMEM),
        (shape((8, 128), F32), VMEM),
        (shape((8, width), F32), VMEM),
        (shape((rows, inner)), VMEM),
        (shape((rows, inner)), VMEM),
        (shape((3, width, inner)), VMEM),
        (shape((whole, inner)), HERE),
        (shape((whole, inner)), HERE),
        (shape((whole, units)), HERE),
        (shape((whole, units)), HERE),
    ] + [(shape(dims, kind), HERE) for dims, kind in kept]
    copies = 3 + 18 + 1 + 6 + 2 + (3 + 1 + 2 * 12 + 3 * 6 if gathers else 0)
    return pl.pallas_call(
        functools.partial(front_kernel, gathers),
        out_shape=[o[0] for o in outs],
        in_specs=[VMEM, HERE, VMEM] + [HERE] * 4 + [VMEM] * len(vectors),
        out_specs=[o[1] for o in outs],
        scratch_shapes=[
            pltpu.VMEM((rows, width), BF16),
            pltpu.VMEM((2, half, width), BF16),
            pltpu.VMEM((half, width), BF16),
            pltpu.VMEM((half, 2 * inner), F32),
            pltpu.VMEM((half, half), BF16),
            pltpu.VMEM((2, half, inner), BF16),
            pltpu.VMEM((half, inner), BF16),
            pltpu.VMEM((4, 8, width), F32),
            pltpu.VMEM((2, rows, half), BF16),
            pltpu.VMEM((8, rows), jnp.int32),
            pltpu.VMEM((share, inner), BF16),
            pltpu.VMEM((share, inner), BF16),
            pltpu.VMEM((share, units), BF16),
            pltpu.VMEM((share, units), BF16),
        ]
        + [pltpu.VMEM(dims, kind) for dims, kind in kept]
        + [
            pltpu.SemaphoreType.DMA((copies,)),
            pltpu.SemaphoreType.DMA((copies,)),
            pltpu.SemaphoreType.DMA((8 + 2 * KEPT,)),
        ],
        compiler_params=params(collective_id=0, has_side_effects=True),
        name="front",
    )(tokens, cotangent, segment, qkv, out, fc1, fc2, *vectors)


def middle_kernel(*refs):
    (
        tok_ref,
        tok_other_ref,
        cot_ref,
        cot_other_ref,
        place_ref,
        mine_ref,
        theirs_ref,
        vec_ref,
        out_mine_ref,
        out_theirs_ref,
        fc1_all_ref,
        fc2_all_ref,
    ) = refs[:12]
    (
        grad_mixed_out,
        back_mine_ref,
        back_got_ref,
        result_out,
        result_other_out,
        fc1_out,
        fc2_out,
        out_out,
        sum_ref,
    ) = refs[12:21]
    (
        fc1_ref,
        fc2_ref,
        act_ref,
        hidden_ref,
        normed_ref,
        grad_other_ref,
        grad_got_ref,
        grad_own_ref,
        mixed_ref,
        attended_ref,
        back_theirs_ref,
        low_ref,
        turned_ref,
        grad_mixed_ref,
        result_ref,
        result_other_ref,
        fc1_part_ref,
        fc2_part_ref,
        out_part_ref,
        send_sem,
        recv_sem,
        local_sem,
    ) = refs[21:]
    half, width = tok_ref.shape
    rows, inner = mine_ref.shape
    units = fc1_ref.shape[1]
    side = lax.axis_index("hidden")
    across = {"hidden": 1 - side}
    copies, locals_ = Copies(send_sem, recv_sem), Locals(local_sem)
    load_fc1 = locals_.start(fc1_all_ref, fc1_ref)
    load_fc2 = locals_.start(fc2_all_ref, fc2_ref)
    greet([across])
    tiles = 3
    tile = half // tiles
    spans = [slice(index * tile, (index + 1) * tile) for index in range(tiles)]
    sum_ref[...] = jnp.zeros_like(sum_ref)

    def feed(own, index):
        block, span = (0 if own else 1), spans[index]
        start = (side if own else 1 - side) * half + index * tile
        place = place_ref[pl.ds(pl.multiple_of(start, 16), tile), :]
        back = one_hot(place == iota((tile, rows), 1))
        mine = dot(back, mine_ref[...]).astype(BF16)
        theirs = dot(back, theirs_ref[...]).astype(BF16)
        tok = (tok_ref if own else tok_other_ref)[span, :]
        cot = (cot_ref if own else cot_other_ref)[span, :]
        mixed = (
            tok.astype(F32)
            + (dot_nt(mine, out_mine_ref[...]) + dot_nt(theirs, out_theirs_ref[...]))
            + vec_ref[OUT_BIAS : OUT_BIAS + 1, :]
        )
        unit, _ = row_norm(mixed)
        normed = unit * vec_ref[LN2_GAIN : LN2_GAIN + 1, :] + vec_ref[LN2_BIAS : LN2_BIAS + 1, :]
        normed = normed.astype(BF16)
        normed_ref[block, span, :] = normed
        if own:
            mixed_ref[span, :] = mixed
            attended_ref[span, :inner] = mine
            attended_ref[span, inner:] = theirs
            sum_ref[FC2_BIAS : FC2_BIAS + 1, :] += jnp.sum(cot.astype(F32), axis=0, keepdims=True)
        elif index == 0:
            load_fc1.wait()
            load_fc2.wait()
        total = None
        step = 512
        for first in range(0, units, step):
            cols = slice(first, first + step)
            pre = dot(normed, fc1_ref[:, cols])
            grad_act = dot(cot, fc2_ref[:, cols])
            cdf, density = normal_cdf(pre)
            act_ref[block, span, cols] = (pre * cdf).astype(BF16)
            grad_hidden = (grad_act * (cdf + pre * density)).astype(BF16)
            hidden_ref[block, span, cols] = grad_hidden
            add = dot_nt(grad_hidden, fc1_ref[:, cols])
            total = add if total is None else total + add
        sum_ref[LN2_GAIN : LN2_GAIN + 1, :] += jnp.sum(total * unit, axis=0, keepdims=True)
        sum_ref[LN2_BIAS : LN2_BIAS + 1, :] += jnp.sum(total, axis=0, keepdims=True)
        if own:
            grad_own_ref[span, :] = total
        else:
            grad_other_ref[span, :] = total.astype(BF16)

    crossing = []
    for index, span in enumerate(spans):
        feed(False, index)
        crossing.append(copies.start(grad_other_ref.at[span, :], grad_got_ref.at[span, :], across))
    for index in range(tiles):
        feed(True, index)

    back = []
    for index, span in enumerate(spans):
        crossing[index].wait_recv()
        unit, scale = row_norm(mixed_ref[span, :])
        grad = grad_own_ref[span, :] + grad_got_ref[span, :].astype(F32)
        grad = row_norm_back(grad * vec_ref[LN2_GAIN : LN2_GAIN + 1, :], unit, scale)
        grad = grad + cot_ref[span, :].astype(F32)
        grad_mixed_ref[span, :] = grad
        low = grad.astype(BF16)
        low_ref[span, :] = low
        back_theirs_ref[span, :] = dot(low, out_theirs_ref[...]).astype(BF16)
        back.append(copies.start(back_theirs_ref.at[span, :], back_got_ref.at[span, :], across))
        back_mine_ref[span, :] = dot(low, out_mine_ref[...]).astype(BF16)
        sum_ref[OUT_BIAS : OUT_BIAS + 1, :] += jnp.sum(low.astype(F32), axis=0, keepdims=True)
    locals_.start(grad_mixed_ref, grad_mixed_out)

    result_other_ref[...] = dot_nt(act_ref[1], fc2_ref[...]).astype(BF16)
    locals_.start(result_other_ref, result_other_out)
    result_ref[...] = (
        dot_nt(act_ref[0], fc2_ref[...])
        + mixed_ref[...]
        + vec_ref[FC2_BIAS : FC2_BIAS + 1, :]
    )
    locals_.start(result_ref, result_out)

    def outer(first, second, right_ref, part_ref):
        turned_ref[0] = first.T
        turned_ref[1] = second.T
        step = 256

        def one(index, carry):
            cols = pl.ds(pl.multiple_of(index * step, step), step)
            part_ref[:, cols] = (
                dot(turned_ref[0], right_ref[0, :, cols]) + dot(turned_ref[1], right_ref[1, :, cols])
            ).astype(BF16)
            return carry

        lax.fori_loop(0, units // step, one, 0)

    outer(cot_ref[...], cot_other_ref[...], act_ref, fc2_part_ref)
    locals_.start(fc2_part_ref, fc2_out)
    outer(normed_ref[0], normed_ref[1], hidden_ref, fc1_part_ref)
    locals_.start(fc1_part_ref, fc1_out)
    turned_ref[0] = low_ref[...].T
    out_part_ref[...] = dot(turned_ref[0], attended_ref[...]).astype(BF16)
    locals_.start(out_part_ref, out_out)
    for copy in back:
        copy.wait_recv()
    copies.finish()
    for copy in locals_.made[2:]:
        copy.wait()


def middle(token, token_other, cot, cot_other, place, mine, theirs, vectors, out_mine, out_theirs, fc1, fc2):
    half, width = token.shape
    rows, inner = mine.shape
    units = fc1.shape[1]
    block = lambda cols, kind=BF16: pltpu.VMEM((half, cols), kind)
    pair = lambda cols: pltpu.VMEM((2, half, cols), BF16)
    return pl.pallas_call(
        middle_kernel,
        out_shape=(
            shape((half, width), F32),
            shape((half, inner)),
            shape((half, inner)),
            shape((half, width), F32),
            shape((half, width)),
            shape((width, units)),
            shape((width, units)),
            shape((width, 2 * inner)),
            shape((8, width), F32),
        ),
        in_specs=[VMEM] * 10 + [HERE] * 2,
        out_specs=(HERE, VMEM, VMEM, HERE, HERE, HERE, HERE, HERE, VMEM),
        scratch_shapes=[
            pltpu.VMEM((width, units), BF16),
            pltpu.VMEM((width, units), BF16),
            pair(units),
            pair(units),
            pair(width),
            block(width),
            block(width),
            block(width, F32),
            block(width, F32),
            block(2 * inner),
            block(inner),
            block(width),
            pltpu.VMEM((2, width, half), BF16),
            block(width, F32),
            block(width, F32),
            block(width),
            pltpu.VMEM((width, units), BF16),
            pltpu.VMEM((width, units), BF16),
            pltpu.VMEM((width, 2 * inner), BF16),
            pltpu.SemaphoreType.DMA((6,)),
            pltpu.SemaphoreType.DMA((6,)),
            pltpu.SemaphoreType.DMA((8,)),
        ],
        compiler_params=params(60 << 20, collective_id=1, has_side_effects=True),
        name="middle",
    )(token, token_other, cot, cot_other, place, mine, theirs, vectors, out_mine, out_theirs, fc1, fc2)


def attend_back(rows_ref, low_ref, value_ref, mask_ref, raw_ref, grad_low_ref):
    half, inner = rows_ref.shape
    pair = 2 * HEAD
    lane = iota((half, pair), 1)

    def one_pair(index, carry):
        cols = pl.ds(pl.multiple_of(index * pair, pair), pair)
        key_cols = pl.ds(pl.multiple_of(inner + index * pair, pair), pair)
        value_cols = pl.ds(pl.multiple_of(2 * inner + index * pair, pair), pair)
        query = low_ref[:, cols] * SCALE
        key = low_ref[:, key_cols]
        value = value_ref[:, cols]
        grad = rows_ref[:, cols]
        key_turned = (key.astype(F32) * SCALE).T.astype(BF16)
        grad_values, grad_keys, grad_queries = [], [], []
        for head in range(2):
            mine = lane < HEAD if head == 0 else lane >= HEAD
            query_head = jnp.where(mine, query, jnp.zeros_like(query))
            grad_head = jnp.where(mine, grad, jnp.zeros_like(grad))
            weights = jnp.exp(dot_nt(key, query_head))
            if mask_ref is not None:
                weights = weights * mask_ref[...]
            weights = weights * (1.0 / jnp.sum(weights, axis=0, keepdims=True))
            grad_weights = dot_nt(value, grad_head)
            shared = jnp.sum(weights * grad_weights, axis=0, keepdims=True)
            grad_scores = (weights * (grad_weights - shared)).astype(BF16)
            grad_values.append(dot(weights.astype(BF16), grad))
            grad_keys.append(dot(grad_scores, query))
            grad_queries.append(dot(key_turned[head * HEAD : (head + 1) * HEAD, :], grad_scores))
        raw_ref[:, cols] = jnp.concatenate(grad_queries, axis=0).T
        raw_ref[:, key_cols] = jnp.where(lane < HEAD, grad_keys[0], grad_keys[1])
        grad_low_ref[:, value_cols] = jnp.where(lane < HEAD, grad_values[0], grad_values[1]).astype(BF16)
        return carry

    lax.fori_loop(0, inner // pair, one_pair, 0)


def head_norm_back(raw_ref, unit_ref, scale_ref, vec_ref, grad_low_ref, sum_ref):
    group = 4 * HEAD
    means = head_mean_matrix(group)
    for first in range(0, raw_ref.shape[1], group):
        cols = slice(first, first + group)
        grad = raw_ref[:, cols]
        unit = unit_ref[:, cols]
        sum_ref[QK_GAIN : QK_GAIN + 1, cols] += jnp.sum(grad * unit, axis=0, keepdims=True)
        grad = grad * vec_ref[QK_GAIN : QK_GAIN + 1, cols]
        grad = scale_ref[:, cols] * (
            grad - two_part(grad, means) - unit * two_part(grad * unit, means)
        )
        grad_low_ref[:, cols] = grad.astype(BF16)


class Reduce:
    def __init__(self, place, copies, part_ref, scratch, out_ref):
        self.place, self.copies, self.out_ref = place, copies, out_ref
        (
            self.got_ref,
            self.low_ref,
            self.near_ref,
            self.far_ref,
            self.last_ref,
            self.total_ref,
        ) = scratch
        self.less_ref = None
        pack, seq, core, seq_mate, pack_mate = place
        self.cross = copies.start(part_ref.at[:, 1 - core], self.got_ref, seq_mate[1])

    def add(self, own_ref, locals_wait):
        core = self.place[2]
        locals_wait()
        self.cross.wait_recv()
        for index in range(4):
            self.low_ref[index] = (
                own_ref[index].astype(F32) + self.got_ref[index].astype(F32)
            ).astype(BF16)

    def near(self):
        pack, seq, core, seq_mate, pack_mate = self.place
        odd = lax.bitwise_and(pack, 1)
        self.first = [
            self.copies.start(
                self.low_ref.at[(1 - odd) + 2 * index], self.near_ref.at[index], pack_mate[1]
            )
            for index in range(2)
        ]

    def far(self):
        pack, seq, core, seq_mate, pack_mate = self.place
        odd, high = lax.bitwise_and(pack, 1), lax.shift_right_logical(pack, 1)
        for index in range(2):
            self.first[index].wait_recv()
            self.near_ref[index] = (
                self.low_ref[odd + 2 * index].astype(F32) + self.near_ref[index].astype(F32)
            ).astype(BF16)
        self.second = self.copies.start(self.near_ref.at[1 - high], self.far_ref.at[0], pack_mate[2])

    def along(self):
        pack, seq, core, seq_mate, pack_mate = self.place
        high = lax.shift_right_logical(pack, 1)
        self.second.wait_recv()
        self.far_ref[1] = (
            self.near_ref[high].astype(F32) + self.far_ref[0].astype(F32)
        ).astype(BF16)
        self.third = self.copies.start(self.far_ref.at[1], self.last_ref, seq_mate[2])

    def piece(self, mine):
        place = lax.shift_right_logical(self.place[1], 1)
        size = self.low_ref.shape[1] // 2
        return rows_at((place if mine else 1 - place) * size, size)

    def split(self, less_ref, from_ref):
        self.less_ref, self.from_ref = less_ref, from_ref
        source = self.low_ref.at[:, self.piece(False), :]
        self.zeroth = self.copies.start(source, from_ref, self.place[3][2])

    def straight(self):
        pack, seq, core, seq_mate, pack_mate = self.place
        self.zeroth.wait_recv()
        for index in range(4):
            self.less_ref[index] = (
                self.low_ref[index, self.piece(True), :].astype(F32)
                + self.from_ref[index].astype(F32)
            ).astype(BF16)
        self.first = [
            self.copies.start(
                self.less_ref.at[other_of(pack, k)], self.near_ref.at[k - 1], pack_mate[k]
            )
            for k in range(1, 4)
        ]

    def straight_along(self):
        pack, seq, core, seq_mate, pack_mate = self.place
        for copy in self.first:
            copy.wait_recv()
        mine, near = self.less_ref[pack].astype(F32), self.near_ref
        self.far_ref[0] = (
            (mine + near[0].astype(F32)) + (near[1].astype(F32) + near[2].astype(F32))
        ).astype(BF16)
        self.third = self.copies.start(self.far_ref.at[0], self.last_ref, seq_mate[2])

    def own(self, locals_):
        pack, seq, core, seq_mate, pack_mate = self.place
        self.third.wait_recv()
        if self.less_ref is None:
            self.total_ref[...] = (
                self.far_ref[1].astype(F32) + self.last_ref[...].astype(F32)
            ).astype(BF16)
        else:
            self.total_ref[self.piece(True), :] = self.far_ref[0]
            self.total_ref[self.piece(False), :] = self.last_ref[...]
        rows = self.total_ref.shape[0]
        here = self.out_ref.at[rows_at(core * rows, rows), :]
        self.fourth = self.copies.start(self.total_ref, here, seq_mate[1])
        locals_.start(self.total_ref, here)

    def finish(self):
        self.fourth.wait_recv()


def back_kernel(reduces, *refs):
    (
        place_row_ref,
        place_col_ref,
        mode_ref,
        vec_ref,
        back_mine_ref,
        back_other_ref,
        weight_ref,
        sum_in_ref,
        low_all,
        value_all,
        normed_all,
        unit_all,
        head_unit_all,
        head_scale_all,
        result_other_all,
        fc1_all,
        fc2_all,
        out_all,
    ) = refs[:18]
    (
        own_out,
        other_got_ref,
        result_got_ref,
        qkv_out_ref,
        out_out_ref,
        fc1_out_ref,
        fc2_out_ref,
        sum_ref,
    ) = refs[18:26]
    (
        low_ref,
        value_ref,
        normed_ref,
        unit_ref,
        head_unit_ref,
        head_scale_ref,
        sorted_ref,
        got_ref,
        rows_ref,
        raw_ref,
        mask_ref,
        grad_low_ref,
        grad_normed_ref,
        ordered_ref,
        long_ref,
        own_ref,
        other_ref,
        turned_ref,
        qkv_part_ref,
        sum_got_ref,
    ) = refs[26:46]
    reduce_refs = refs[46:-3]
    send_sem, recv_sem, local_sem = refs[-3:]
    half, width = own_ref.shape
    inner = back_mine_ref.shape[1]
    rows = 2 * half
    chunk = half // 4
    steps = range(1, 4)
    pack, seq, side = lax.axis_index("dp"), lax.axis_index("seq"), lax.axis_index("hidden")
    core = lax.bitwise_and(seq, 1)
    across = {"hidden": 1 - side}
    seq_mate = [{"seq": other_of(seq, step)} for step in range(4)]
    pack_mate = [{"dp": other_of(pack, step)} for step in range(4)]
    copies, locals_ = Copies(send_sem, recv_sem), Locals(local_sem)
    place = (pack, seq, core, seq_mate, pack_mate)

    def load(part):
        return [
            locals_.start(source.at[part], target)
            for source, target in (
                (low_all, low_ref),
                (value_all, value_ref),
                (head_unit_all, head_unit_ref),
                (head_scale_all, head_scale_ref),
                (unit_all, unit_ref),
            )
        ]

    load_normed = locals_.start(normed_all, normed_ref)
    loading = load(0)
    greet([across] + seq_mate[1:] + (pack_mate[1:] if reduces else []))

    first = side == 0
    place_own = jnp.where(first, place_row_ref[0:1, :], place_row_ref[1:2, :])
    place_other = jnp.where(first, place_row_ref[1:2, :], place_row_ref[0:1, :])
    moved = []
    for part in range(2):
        target = iota((half, half), 0) + part * half
        found = dot(one_hot(target == place_own), back_mine_ref[...])
        found = found + dot(one_hot(target == place_other), back_other_ref[...])
        sorted_ref[part * half : (part + 1) * half, :] = found.astype(BF16)
        moved.append(
            [
                copies.start(
                    sorted_ref.at[rows_at(part * half + other_of(seq, k) * chunk, chunk), :],
                    got_ref.at[part, k * chunk : (k + 1) * chunk, :],
                    seq_mate[k],
                )
                for k in steps
            ]
        )
    if reduces:
        scratch = [reduce_refs[index * 7 : (index + 1) * 7] for index in range(6)]
        parts = []
        for index, (source, target) in enumerate(
            ((fc2_all, fc2_out_ref), (fc1_all, fc1_out_ref), (out_all, out_out_ref))
        ):
            mine = locals_.start(source.at[:, core], scratch[index][0])
            parts.append((Reduce(place, copies, source, scratch[index][1:], target), mine))
        (fc2_sum, fc2_mine), (fc1_sum, fc1_mine), (out_sum, out_mine) = parts
        out_wide_ref, out_got_ref = reduce_refs[42:44]
    work_ref = sum_got_ref.at[9]
    work_ref[...] = sum_in_ref[...]
    if reduces:
        fc2_sum.add(scratch[0][0], fc2_mine.wait)
        fc2_sum.near()
        out_mine.wait()
        out_sum.cross.wait_recv()
        for index in range(4):
            both = scratch[2][0][index].astype(F32) + scratch[2][1][index].astype(F32)
            scratch[2][2][index] = both[:, :inner].astype(BF16)
            out_wide_ref[index] = both[:, inner:].astype(BF16)
        out_cross = copies.start(out_wide_ref, out_got_ref, across)
        fc1_sum.add(scratch[1][0], fc1_mine.wait)
        fc1_sum.near()
    result_cross = copies.start(result_other_all, result_got_ref, across)
    load_normed.wait()
    for part in range(2):
        turned_ref[part] = normed_ref[part].T
    mask_ref[...] = image_mask(mode_ref, half)

    wide = width // 2
    pieces = [slice(0, wide), slice(wide, width)]

    def attention(part):
        for copy in moved[part]:
            copy.wait_recv()
        fill_sequence(part, seq, mode_ref, sorted_ref, got_ref, rows_ref)
        for copy in loading:
            copy.wait()
        grad_low = grad_low_ref.at[part]
        attend_back(rows_ref, low_ref, value_ref, mask_ref if part else None, raw_ref, grad_low)
        head_norm_back(raw_ref, head_unit_ref, head_scale_ref, vec_ref, grad_low, work_ref)
        total = dot_nt(grad_low[:, :inner], weight_ref[0])
        total = total + dot_nt(grad_low[:, inner : 2 * inner], weight_ref[1])
        total = total + dot_nt(grad_low[:, 2 * inner :], weight_ref[2])
        work_ref[LN1_GAIN : LN1_GAIN + 1, :] += jnp.sum(
            total * unit_ref[...].astype(F32), axis=0, keepdims=True
        )
        work_ref[LN1_BIAS : LN1_BIAS + 1, :] += jnp.sum(total, axis=0, keepdims=True)
        grad_normed_ref[part] = total.astype(BF16)
        target_ref = ordered_ref if part == 0 else long_ref
        target_ref[rows_at(seq * chunk, chunk), :] = grad_normed_ref[part, 0:chunk, :]
        return [
            [
                copies.start(
                    grad_normed_ref.at[part, k * chunk : (k + 1) * chunk, cols],
                    target_ref.at[rows_at(seq * chunk, chunk), cols],
                    seq_mate[k],
                )
                for k in steps
            ]
            for cols in ([slice(0, width)] if part == 0 else pieces)
        ]

    returned = attention(0)
    loading = load(1)
    if reduces:
        fc2_sum.far()
        out_cross.wait_recv()
        for index in range(4):
            out_sum.low_ref[index] = (
                out_sum.low_ref[index].astype(F32) + out_got_ref[index].astype(F32)
            ).astype(BF16)
        out_sum.near()
    returned += attention(1)

    sums = copies.start(work_ref, sum_got_ref.at[0], across)
    def qkv_block(kind, index, which):
        share = width // 8
        span = rows_at((2 * index + which) * share, share)
        cols = slice(kind * inner, (kind + 1) * inner)
        qkv_part_ref[kind, index, which] = (
            dot(turned_ref[0, span, :], grad_low_ref[0, :, cols])
            + dot(turned_ref[1, span, :], grad_low_ref[1, :, cols])
        ).astype(BF16)

    qkv_sums = []
    for kind in (2, 1, 0):
        for index in range(4):
            qkv_block(kind, index, 1 - core)
        if reduces:
            qkv_sums.append(
                Reduce(
                    place, copies, qkv_part_ref.at[kind], scratch[3 + kind][1:], qkv_out_ref.at[kind]
                )
            )
        for index in range(4):
            qkv_block(kind, index, core)
    if reduces:
        fc1_sum.far()
        out_sum.far()
        for kind, each in zip((2, 1, 0), qkv_sums):
            each.cross.wait_recv()
            for index in range(4):
                each.low_ref[index] = (
                    qkv_part_ref[kind, index, core].astype(F32) + each.got_ref[index].astype(F32)
                ).astype(BF16)
            each.split(*reduce_refs[44 + 2 * kind : 46 + 2 * kind])
    else:
        keep = locals_.start(qkv_part_ref, qkv_out_ref)

    def unsort(target_ref, which, cols):
        start = pl.multiple_of(which * half, 16)
        back = one_hot(place_col_ref[pl.ds(start, half), :] == iota((half, rows), 1))
        target_ref[:, cols] = dot(back, ordered_ref[:, cols]).astype(BF16)

    for copy in returned[0]:
        copy.wait_recv()
    crossing = []
    for cols, coming in zip(pieces, returned[1:]):
        for copy in coming:
            copy.wait_recv()
        ordered_ref[half:, cols] = jnp.where(
            mode_ref[0:1, 0:1] > 0,
            long_ref[:, cols].astype(F32),
            grad_normed_ref[1, :, cols].astype(F32),
        ).astype(BF16)
        unsort(other_ref, 1 - side, cols)
        crossing.append(copies.start(other_ref.at[:, cols], other_got_ref.at[:, cols], across))
    if reduces:
        fc2_sum.along()
    sums.wait_recv()
    sum_got_ref[1] = work_ref[...] + sum_got_ref[0]
    around = [copies.start(sum_got_ref.at[1], sum_got_ref.at[1 + k], seq_mate[k]) for k in steps]
    if reduces:
        for each in qkv_sums:
            each.straight()
    unsort(own_ref, side, slice(0, width))
    own_copy = locals_.start(own_ref, own_out)
    for copy in around:
        copy.wait_recv()
    sum_got_ref[5] = (sum_got_ref[1] + sum_got_ref[2]) + (sum_got_ref[3] + sum_got_ref[4])
    if reduces:
        through = [copies.start(sum_got_ref.at[5], sum_got_ref.at[5 + k], pack_mate[k]) for k in steps]
        fc1_sum.along()
        out_sum.along()
        fc2_sum.own(locals_)
        for each in qkv_sums:
            each.straight_along()
        fc1_sum.own(locals_)
        out_sum.own(locals_)
        for copy in through:
            copy.wait_recv()
        sum_ref[...] = (sum_got_ref[5] + sum_got_ref[6]) + (sum_got_ref[7] + sum_got_ref[8])
        for each in qkv_sums:
            each.own(locals_)
        for each in (fc1_sum, fc2_sum, out_sum, *qkv_sums):
            each.finish()
    else:
        sum_ref[...] = sum_got_ref[5]
        keep.wait()
    for copy in crossing:
        copy.wait_recv()
    result_cross.wait_recv()
    copies.finish()
    own_copy.wait()
    if reduces:
        for copy in locals_.made[-6:]:
            copy.wait()


def back(reduces, place_row, place_col, mode, vectors, back_mine, back_other, weight, sums, kept, result_other, fc1_part, fc2_part, out_part, packs):
    normed, unit, low, value, head_unit, head_scale = kept
    half, width = result_other.shape
    inner = back_mine.shape[1]
    units = fc1_part.shape[1]
    share = width // packs
    rows = 2 * half
    block = lambda cols, kind=BF16: pltpu.VMEM((half, cols), kind)
    pair = lambda cols: pltpu.VMEM((2, half, cols), BF16)
    cut = (4, 2, width // 8)
    piece = width // 8

    def summing(columns, wide, owns, split):
        last = piece // 2 if split else piece
        return [
            pltpu.VMEM((4, piece, wide) if owns else (8, 128), BF16),
            pltpu.VMEM((4, piece, wide), BF16),
            pltpu.VMEM((4, piece, columns), BF16),
            pltpu.VMEM((3 if split else 2, last, columns), BF16),
            pltpu.VMEM((2, last, columns), BF16),
            pltpu.VMEM((last, columns), BF16),
            pltpu.VMEM((piece, columns), BF16),
        ]

    reduce_scratch = []
    if reduces:
        reduce_scratch = (
            summing(units, units, True, False)
            + summing(units, units, True, False)
            + summing(inner, 2 * inner, True, False)
            + summing(inner, inner, False, True) * 3
            + [pltpu.VMEM((4, piece, inner), BF16)] * 2
            + [pltpu.VMEM((4, piece // 2, inner), BF16)] * 6
        )
    copies = 6 + 1 + 9 + 1 + 3 + 2 + (3 + 3 * 6 + 1 + 3 * 7 if reduces else 0)
    return pl.pallas_call(
        functools.partial(back_kernel, reduces),
        out_shape=(
            shape((half, width)),
            shape((half, width)),
            shape((half, width)),
            shape((3, share, inner) if reduces else (3, *cut, inner)),
            shape((share, inner)),
            shape((share, units)),
            shape((share, units)),
            shape((8, width), F32),
        ),
        in_specs=[VMEM] * 8 + [HERE] * 10,
        out_specs=(HERE,) * 7 + (VMEM,),
        scratch_shapes=[
            block(2 * inner),
            block(inner),
            pair(width),
            block(width),
            block(2 * inner, F32),
            block(2 * inner, F32),
            pltpu.VMEM((rows, inner), BF16),
            pair(inner),
            block(inner),
            block(2 * inner, F32),
            pltpu.VMEM((half, half), F32),
            pair(3 * inner),
            pair(width),
            pltpu.VMEM((rows, width), BF16),
            block(width),
            block(width),
            block(width),
            pltpu.VMEM((2, width, half), BF16),
            pltpu.VMEM((3, *cut, inner), BF16),
            pltpu.VMEM((10, 8, width), F32),
        ]
        + reduce_scratch
        + [
            pltpu.SemaphoreType.DMA((copies,)),
            pltpu.SemaphoreType.DMA((copies,)),
            pltpu.SemaphoreType.DMA((24,)),
        ],
        compiler_params=params(63 << 20, collective_id=2, has_side_effects=True),
        name="back",
    )(
        place_row,
        place_col,
        mode,
        vectors,
        back_mine,
        back_other,
        weight,
        sums,
        low,
        value,
        normed,
        unit,
        head_unit,
        head_scale,
        result_other,
        fc1_part.reshape(*cut, -1),
        fc2_part.reshape(*cut, -1),
        out_part.reshape(*cut, -1),
    )


def finish_kernel(*refs):
    tok_ref, own_ref, got_ref, grad_mixed_ref, result_ref, result_got_ref, vec_ref, sum_ref = refs[:8]
    sources, refs = refs[8:12], refs[12:]
    output_ref, input_grad_ref = refs[:2]
    vec_outs, gain_out, targets = refs[2:8], refs[8], refs[9:13]
    for source, target in zip(sources, targets):
        target[...] = source[...].astype(F32)

    @pl.when(pl.program_id(0) == 0)
    def _():
        pack = lax.axis_index("dp")
        share, width = vec_outs[0].shape[0], vec_ref.shape[1]
        sums = sum_ref[...]
        mine = sum(
            jnp.where(pack == index, sums[:, index * share : (index + 1) * share], 0.0)
            for index in range(width // share)
        )
        for index, out_ref in enumerate(vec_outs):
            out_ref[...] = mine[index : index + 1, :].reshape(share)
        few = gain_out.shape[1]
        for index in range(2):
            row = sums[QK_GAIN : QK_GAIN + 1, index * width // 2 : (index + 1) * width // 2]
            row = sum(row[:, first : first + HEAD] for first in range(0, width // 2, HEAD))
            gain_out[index : index + 1, :] = sum(
                jnp.where(pack == place, row[:, place * few : (place + 1) * few], 0.0)
                for place in range(HEAD // few)
            )

    output_ref[...] = (result_ref[...] + result_got_ref[...].astype(F32)).astype(BF16)
    unit, scale = row_norm(tok_ref[...].astype(F32))
    grad = own_ref[...].astype(F32) + got_ref[...].astype(F32)
    grad = row_norm_back(grad * vec_ref[LN1_GAIN : LN1_GAIN + 1, :], unit, scale)
    input_grad_ref[...] = (grad_mixed_ref[...] + grad).astype(BF16)


def finish(token, own, got, grad_mixed, result, result_got, vectors, sums, arrays, share, few):
    half, width = token.shape
    tile = half // 4
    by_row = pl.BlockSpec((tile, width), lambda i: (i, 0))
    whole = pl.BlockSpec((8, width), lambda i: (0, 0))
    parts = 4 if share % 32 == 0 else 1

    def block(array):
        lead = array.shape[:-2]
        dims = (*lead, share // parts, array.shape[-1])
        return pl.BlockSpec(dims, lambda i: (*(0,) * len(lead), i if parts > 1 else 0, 0))

    return pl.pallas_call(
        finish_kernel,
        out_shape=[shape((half, width))] * 2
        + [shape((share,), F32)] * 6
        + [shape((2, few), F32)]
        + [shape(array.shape, F32) for array in arrays],
        grid=(half // tile,),
        in_specs=[by_row] * 6 + [whole] * 2 + [block(array) for array in arrays],
        out_specs=[by_row] * 2
        + [pl.BlockSpec((share,), lambda i: (0,))] * 6
        + [pl.BlockSpec((2, few), lambda i: (0, 0))]
        + [block(array) for array in arrays],
        compiler_params=params(60 << 20, dimension_semantics=("arbitrary",)),
        name="finish",
    )(token, own, got, grad_mixed, result, result_got, vectors, sums, *arrays)


def swap(array, axis, step):
    pairs = [(index, index ^ step) for index in range(lax.axis_size(axis))]
    return lax.ppermute(array, axis, pairs)


def owned_sum(part, dim):
    total = lax.psum_scatter(part.astype(BF16), "dp", scatter_dimension=dim, tiled=True)
    total = (total.astype(F32) + swap(total, "seq", 1).astype(F32)).astype(BF16)
    return total.astype(F32) + swap(total, "seq", 2).astype(F32)


def local(
    tokens,
    segment,
    cotangent,
    ln1_gain,
    ln1_bias,
    qkv_weight,
    qk_gain,
    out_weight,
    out_bias,
    ln2_gain,
    ln2_bias,
    fc1_weight,
    fc2_weight,
    fc2_bias,
):
    half, width = tokens.shape
    packs = lax.axis_size("dp")
    inner = qkv_weight.shape[2]
    share = ln1_gain.shape[0]
    gathers = packs == 4
    pack = lax.axis_index("dp")
    pieces = [ln1_gain, ln1_bias, out_bias, ln2_gain, ln2_bias, fc2_bias]
    if gathers:
        vectors = [*pieces, qk_gain]
    else:
        few = qk_gain.shape[1]
        lanes = jnp.arange(width)
        wide = jnp.where(lanes // share == pack, jnp.tile(jnp.stack(pieces).astype(F32), (1, packs)), 0.0)
        gains = jnp.tile(qk_gain.astype(F32), (1, width // (2 * few))).reshape(1, width)
        gains = jnp.where(lanes % HEAD // few == pack, gains, 0.0)
        vectors = jnp.concatenate([wide, gains, jnp.zeros((1, width), F32)], axis=0)
        vectors = [lax.psum(vectors, "dp")]
        qkv_weight = lax.all_gather(qkv_weight, "dp", axis=1, tiled=True)
    (
        tokens_other,
        cot_other,
        place_row,
        place_col,
        mode,
        vectors,
        mine,
        theirs,
        qkv_full,
        out_mine,
        out_theirs,
        fc1_full,
        fc2_full,
        *kept,
    ) = front(
        gathers, tokens, cotangent, segment, vectors, qkv_weight, out_weight.T, fc1_weight,
        fc2_weight.T,
    )
    if not gathers:
        out_mine = lax.all_gather(out_weight.T, "dp", axis=0, tiled=True)
        out_theirs = swap(out_mine, "hidden", 1)
        fc1_full = lax.all_gather(fc1_weight, "dp", axis=0, tiled=True)
        fc2_full = lax.all_gather(fc2_weight.T, "dp", axis=0, tiled=True)
    (
        grad_mixed,
        back_mine,
        back_other,
        result,
        result_other,
        fc1_part,
        fc2_part,
        out_part,
        sums,
    ) = middle(
        tokens, tokens_other, cotangent, cot_other, place_col, mine, theirs, vectors, out_mine,
        out_theirs, fc1_full, fc2_full,
    )
    own, got, result_got, qkv_owned, out_owned, fc1_owned, fc2_owned, sums = back(
        gathers, place_row, place_col, mode, vectors, back_mine, back_other, qkv_full, sums, kept,
        result_other, fc1_part, fc2_part, out_part, packs,
    )
    if not gathers:
        sums = lax.psum(sums, "dp")
        qkv_owned = owned_sum(qkv_owned.reshape(3, width, inner), 1)
        out_part = out_part[:, :inner].astype(F32) + swap(out_part[:, inner:], "hidden", 1).astype(F32)
        out_owned = owned_sum(out_part, 0)
        fc1_owned = owned_sum(fc1_part, 0)
        fc2_owned = owned_sum(fc2_part, 0)
    output, input_grad, *sums, qk_owned, qkv_owned, out_owned, fc1_owned, fc2_owned = finish(
        tokens, own, got, grad_mixed, result, result_got, vectors, sums,
        [qkv_owned, out_owned, fc1_owned, fc2_owned], share, qk_gain.shape[1],
    )
    return (
        output,
        input_grad,
        sums[LN1_GAIN],
        sums[LN1_BIAS],
        qkv_owned,
        qk_owned,
        out_owned.T,
        sums[OUT_BIAS],
        sums[LN2_GAIN],
        sums[LN2_BIAS],
        fc1_owned,
        fc2_owned.T,
        sums[FC2_BIAS],
    )


def solution(mesh):
    rows = P(("dp", "seq", "hidden"), None)
    in_specs = (
        rows,
        P("dp"),
        rows,
        P("dp"),
        P("dp"),
        P(None, "dp", "hidden"),
        P(None, "dp"),
        P("hidden", "dp"),
        P("dp"),
        P("dp"),
        P("dp"),
        P("dp", "hidden"),
        P("hidden", "dp"),
        P("dp"),
    )
    out_specs = (
        rows,
        rows,
        P("dp"),
        P("dp"),
        P(None, "dp", "hidden"),
        P(None, "dp"),
        P("hidden", "dp"),
        P("dp"),
        P("dp"),
        P("dp"),
        P("dp", "hidden"),
        P("hidden", "dp"),
        P("dp"),
    )
    return jax.shard_map(local, mesh=mesh, in_specs=in_specs, out_specs=out_specs, check_vma=False)
```

```python
import functools

import jax
import jax.numpy as jnp
from jax import lax
from jax.experimental import pallas as pl
from jax.experimental.pallas import tpu as pltpu
from jax.sharding import PartitionSpec as P

HEAD = 64
LONG = 576
IMAGE = 64
LABELS = 128
EPSILON = 1e-06
SCALE = HEAD ** (-0.5)
F32 = jnp.float32
BF16 = jnp.bfloat16

VMEM = pl.BlockSpec(memory_space=pltpu.VMEM)
SMEM = pl.BlockSpec(memory_space=pltpu.SMEM)
HERE = pl.BlockSpec(memory_space=pl.ANY)
LN1_GAIN, LN1_BIAS, OUT_BIAS, LN2_GAIN, LN2_BIAS, FC2_BIAS, QK_GAIN = range(7)


def params(limit=56 << 20, **more):
    return pltpu.CompilerParams(vmem_limit_bytes=limit, **more)


def shape(dims, dtype=BF16):
    return jax.ShapeDtypeStruct(dims, dtype)


def dot(left, right):
    return jnp.dot(left, right, preferred_element_type=F32)


def dot_nt(left, right):
    return lax.dot_general(left, right, (((1,), (1,)), ((), ())), preferred_element_type=F32)


def dot_tn(left, right):
    return lax.dot_general(left, right, (((0,), (0,)), ((), ())), preferred_element_type=F32)


def iota(dims, dim):
    return lax.broadcasted_iota(jnp.int32, dims, dim)


def one_hot(test):
    return jnp.where(test, 1.0, 0.0).astype(BF16)


def two_part(values, matrix):
    high = values.astype(BF16)
    rest = (values - high.astype(F32)).astype(BF16)
    return dot(high, matrix) + dot(rest, matrix)


def head_mean_matrix(width):
    return jnp.where(
        iota((width, width), 0) // HEAD == iota((width, width), 1) // HEAD, 1.0 / HEAD, 0.0
    ).astype(BF16)


def row_norm(values):
    mean = jnp.mean(values, axis=-1, keepdims=True)
    centred = values - mean
    spread = jnp.mean(centred * centred, axis=-1, keepdims=True)
    scale = lax.rsqrt(spread + EPSILON)
    return centred * scale, scale


def row_norm_back(grad_unit, unit, scale):
    first = jnp.mean(grad_unit, axis=-1, keepdims=True)
    second = jnp.mean(grad_unit * unit, axis=-1, keepdims=True)
    return scale * (grad_unit - first - unit * second)


def normal_cdf(values):
    size = jnp.abs(values) * (2.0 ** -0.5)
    bell = jnp.exp(-0.5 * values * values)
    t = 1.0 / (1.0 + 0.3275911 * size)
    poly = 1.061405429 * t - 1.453152027
    poly = poly * t + 1.421413741
    poly = poly * t - 0.284496736
    poly = poly * t + 0.254829592
    tail = 0.5 * (poly * t) * bell
    return jnp.where(values < 0, tail, 1.0 - tail), bell * 0.3989422804014327


def other_of(value, step):
    return lax.bitwise_xor(value, jnp.int32(step))


def rows_at(start, size):
    return pl.ds(pl.multiple_of(start, 16), size)


class Copies:
    def __init__(self, send_sem, recv_sem):
        self.send_sem, self.recv_sem = send_sem, recv_sem
        self.made = []

    def start(self, source, target, device):
        index = len(self.made)
        copy = pltpu.make_async_remote_copy(
            src_ref=source,
            dst_ref=target,
            send_sem=self.send_sem.at[index],
            recv_sem=self.recv_sem.at[index],
            device_id=device,
            device_id_type=pl.DeviceIdType.MESH,
        )
        copy.start()
        self.made.append(copy)
        return copy

    def finish(self):
        for copy in self.made:
            copy.wait_send()


class Locals:
    def __init__(self, sem):
        self.sem, self.made = sem, []

    def start(self, source, target):
        copy = pltpu.make_async_copy(source, target, self.sem.at[len(self.made)])
        copy.start()
        self.made.append(copy)
        return copy

    def finish(self):
        for copy in self.made:
            copy.wait()


def greet(devices):
    barrier = pltpu.get_barrier_semaphore()
    for device in devices:
        pl.semaphore_signal(barrier, inc=1, device_id=device, device_id_type=pl.DeviceIdType.MESH)
    pl.semaphore_wait(barrier, len(devices))


def place_rows(labels, place_row_ref, place_col_ref, mode_ref, places_ref):
    rows = labels.shape[1]
    half = rows // 2
    chunk = LONG // 4
    by_row = jnp.where(labels == iota((LABELS, rows), 0), 1.0, 0.0)
    count = jnp.sum(by_row, axis=1, keepdims=True)
    cut = 0.5 * (chunk + IMAGE)
    long = jnp.where(count > cut, count, 0.0)
    small = count - long
    total = jnp.sum(long, axis=0, keepdims=True)
    left = iota((LABELS, LABELS), 0)
    right = iota((LABELS, LABELS), 1)

    def before(counts):
        turned = jnp.broadcast_to(counts, (LABELS, LABELS)).T
        return jnp.sum(jnp.where(right < left, turned, 0.0), axis=1, keepdims=True)

    base = jnp.where(long > 0, before(long), total + before(small))
    earlier = one_hot(left < right)
    for first in range(0, rows, LABELS):
        cols = slice(first, first + LABELS)
        block = by_row[:, cols]
        place = base + dot(block.astype(BF16), earlier)
        base = base + jnp.sum(block, axis=1, keepdims=True)
        place = jnp.sum(block * place, axis=0, keepdims=True)
        places_ref[0:1, cols] = place.astype(jnp.int32)
        turned = jnp.broadcast_to(place, (LABELS, LABELS)).T
        place_col_ref[cols, :] = turned[:, 0:1].astype(jnp.int32)
    place_row_ref[0:1, :] = places_ref[0:1, :half]
    place_row_ref[1:2, :] = places_ref[0:1, half:]
    mode_ref[...] = jnp.broadcast_to(jnp.where(total > rows - IMAGE, 1.0, 0.0), mode_ref.shape)


def sorting(place_ref, side, hot_ref):
    half = place_ref.shape[1]
    first = side == 0
    place_own = jnp.where(first, place_ref[0:1, :], place_ref[1:2, :])
    place_other = jnp.where(first, place_ref[1:2, :], place_ref[0:1, :])
    for part in range(2):
        target = iota((half, half), 0) + part * half
        hot_ref[0, part * half : (part + 1) * half, :] = one_hot(target == place_own)
        hot_ref[1, part * half : (part + 1) * half, :] = one_hot(target == place_other)


def put_vectors(pieces, gain_ref, pack, vec_ref):
    share, width = pieces[0].shape[0], vec_ref.shape[1]
    at = one_hot(iota((share, width), 1) == iota((share, width), 0) + pack * share)
    vec_ref[...] = jnp.zeros_like(vec_ref)
    for index, piece in enumerate(pieces):
        row = piece[...].astype(F32).reshape(1, share)
        row = jnp.broadcast_to(row, (8, share)).astype(BF16)
        vec_ref[index : index + 1, :] = dot(row, at)[0:1, :]
    few, half = gain_ref.shape[1], width // 2
    at = one_hot(lax.bitwise_and(iota((few, half), 1), HEAD - 1) == iota((few, half), 0) + pack * few)
    gains = dot(gain_ref[...], at)
    vec_ref[QK_GAIN : QK_GAIN + 1, :half] = gains[0:1, :]
    vec_ref[QK_GAIN : QK_GAIN + 1, half:] = gains[1:2, :]


def fill_sequence(part, seq, mode_ref, sorted_ref, got_ref, rows_ref):
    half = rows_ref.shape[0]
    chunk = half // 4
    home = sorted_ref[rows_at(part * half + seq * chunk, chunk), :]
    for step in range(4):
        rows = home if step == 0 else got_ref[part, step * chunk : (step + 1) * chunk, :]
        if part == 1:
            local = sorted_ref[half + step * chunk : half + (step + 1) * chunk, :]
            rows = jnp.where(mode_ref[0:1, 0:1] > 0, rows.astype(F32), local.astype(F32))
        rows_ref[step * chunk : (step + 1) * chunk, :] = rows.astype(BF16)


def image_mask(mode_ref, rows):
    same = lax.shift_right_logical(iota((rows, rows), 0), 6) == lax.shift_right_logical(
        iota((rows, rows), 1), 6
    )
    return jnp.where(same, 1.0, mode_ref[0:1, 0:1])


def project(part, rows_ref, weight_ref, vec_ref, kept, raw_ref):
    normed_ref, unit_ref, low_ref, value_ref, head_unit_ref, head_scale_ref = (
        ref.at[part] for ref in kept
    )
    half, width = rows_ref.shape
    inner = value_ref.shape[1]
    chunk = half // 4
    for step in range(4):
        rows = slice(step * chunk, (step + 1) * chunk)
        unit, _ = row_norm(rows_ref[rows, :].astype(F32))
        unit_ref[rows, :] = unit.astype(BF16)
        normed = unit * vec_ref[LN1_GAIN : LN1_GAIN + 1, :] + vec_ref[LN1_BIAS : LN1_BIAS + 1, :]
        normed_ref[rows, :] = normed.astype(BF16)
    raw_ref[:, :inner] = dot(normed_ref[...], weight_ref[0])
    raw_ref[:, inner:] = dot(normed_ref[...], weight_ref[1])
    value_ref[...] = dot(normed_ref[...], weight_ref[2]).astype(BF16)
    group = 4 * HEAD
    means = head_mean_matrix(group)
    for first in range(0, 2 * inner, group):
        cols = slice(first, first + group)
        raw = raw_ref[:, cols]
        centred = raw - two_part(raw, means)
        scale = lax.rsqrt(two_part(centred * centred, means) + EPSILON)
        unit = centred * scale
        head_unit_ref[:, cols] = unit
        head_scale_ref[:, cols] = scale
        low_ref[:, cols] = (unit * vec_ref[QK_GAIN : QK_GAIN + 1, cols]).astype(BF16)


def attend(part, kept, mask_ref, attended_ref):
    low_ref, value_ref = kept[2].at[part], kept[3].at[part]
    half, inner = value_ref.shape
    pair = 2 * HEAD
    lane = iota((half, pair), 1)

    def one_pair(index, carry):
        cols = pl.ds(pl.multiple_of(index * pair, pair), pair)
        key_cols = pl.ds(pl.multiple_of(inner + index * pair, pair), pair)
        query = low_ref[:, cols] * SCALE
        key = low_ref[:, key_cols]
        value = jnp.concatenate([value_ref[:, cols], jnp.ones((half, pair), BF16)], axis=1)
        found = []
        for head in range(2):
            mine = lane < HEAD if head == 0 else lane >= HEAD
            scores = dot_nt(jnp.where(mine, query, jnp.zeros_like(query)), key)
            weights = jnp.exp(scores).astype(BF16)
            if part == 1:
                weights = weights * mask_ref[...]
            both = dot(weights, value)
            found.append(both[:, :pair] / both[:, pair:])
        attended_ref[part, :, cols] = jnp.where(lane < HEAD, found[0], found[1]).astype(BF16)
        return carry

    lax.fori_loop(0, inner // pair, one_pair, 0)


KEPT = 6


def front_kernel(gathers, *refs):
    tok_ref, cot_ref, seg_ref, qkv_ref, out_ref, fc1_ref, fc2_ref = refs[:7]
    vec_in_refs, refs = (refs[7:14], refs[14:]) if gathers else (refs[7:8], refs[8:])
    (
        tok_other_ref,
        cot_other_ref,
        place_row_ref,
        place_col_ref,
        mode_ref,
        vec_ref,
        mine_ref,
        theirs_ref,
        qkv_all_ref,
        out_all_ref,
        out_theirs_ref,
        fc1_all_ref,
        fc2_all_ref,
    ) = refs[:13]
    kept_out = refs[13 : 13 + KEPT]
    (
        sorted_ref,
        got_ref,
        rows_ref,
        raw_ref,
        mask_ref,
        attended_ref,
        back_ref,
        vec_got_ref,
        hot_ref,
        places_ref,
        out_pair_ref,
    ) = refs[13 + KEPT : 24 + KEPT]
    share_refs = refs[24 + KEPT : 27 + KEPT]
    kept = refs[27 + KEPT : 27 + 2 * KEPT]
    send_sem, recv_sem, local_sem = refs[27 + 2 * KEPT :]
    pack, seq, side = lax.axis_index("dp"), lax.axis_index("seq"), lax.axis_index("hidden")
    core = lax.bitwise_and(seq, 1)
    half, width = tok_ref.shape
    chunk = half // 4
    steps = range(1, 4)
    across = {"hidden": 1 - side}
    seq_mate = [{"seq": other_of(seq, step)} for step in range(4)]
    pack_mate = [{"dp": other_of(pack, step)} for step in range(4)]
    greet([across] + seq_mate[1:] + (pack_mate[1:] if gathers else []))
    copies, locals_ = Copies(send_sem, recv_sem), Locals(local_sem)

    wide = width // 3
    pieces = [slice(first, first + wide) for first in range(0, width, wide)]
    tokens = [copies.start(tok_ref.at[:, c], tok_other_ref.at[:, c], across) for c in pieces]
    whole = fc1_ref.shape[0]
    in_flight = []

    def rows_of(ref, index, piece, size):
        rows = rows_at(index * whole + piece * size, size)
        return ref.at[:, rows, :] if len(ref.shape) == 3 else ref.at[rows, :]

    class Half:
        def __init__(self, source, target):
            self.target, self.size = target, whole // 2
            self.first = [
                copies.start(
                    rows_of(source, 0, core, self.size),
                    rows_of(target, pack, core, self.size),
                    pack_mate[k],
                )
                for k in steps
            ]

        def share(self):
            for k in steps:
                self.first[k - 1].wait_recv()
                there = rows_of(self.target, other_of(pack, k), core, self.size)
                in_flight.append(copies.start(there, there, seq_mate[1]))

    class Quarter:
        def __init__(self, source, target):
            self.target, self.size = target, whole // 4
            self.first = [
                copies.start(
                    rows_of(source, 0, seq, self.size),
                    rows_of(target, pack, seq, self.size),
                    pack_mate[k],
                )
                for k in steps
            ]
            self.second = []

        def there(self, k, piece):
            return rows_of(self.target, other_of(pack, k), piece, self.size)

        def pass_on(self):
            for k in steps:
                self.first[k - 1].wait_recv()
                there = self.there(k, seq)
                self.second.append(copies.start(there, there, seq_mate[2]))
            for k in steps:
                there = self.there(k, seq)
                in_flight.append(copies.start(there, there, seq_mate[1]))

        def share(self):
            for k in steps:
                self.second[k - 1].wait_recv()
                there = self.there(k, other_of(seq, 2))
                in_flight.append(copies.start(there, there, seq_mate[1]))

    if gathers:
        gather_qkv = Quarter(qkv_ref, qkv_all_ref)
        put_vectors(vec_in_refs[:6], vec_in_refs[6], pack, vec_got_ref.at[3])
        gather_vec = [
            copies.start(vec_got_ref.at[3], vec_got_ref.at[k - 1], pack_mate[k]) for k in steps
        ]
        pair_out = copies.start(out_ref, out_pair_ref, across)
        gather_out = Half(out_ref, out_all_ref)
        gather_fc2 = Quarter(fc2_ref, fc2_all_ref)
        keep = [locals_.start(qkv_ref, qkv_all_ref.at[:, rows_at(pack * whole, whole), :])] + [
            locals_.start(source, target)
            for source, target in zip((out_ref, fc1_ref, fc2_ref), share_refs)
        ]
    else:
        keep = [locals_.start(qkv_ref, qkv_all_ref)]
    rows = 2 * half
    labels = seg_ref[...]
    place_rows(
        sum(
            jnp.where(seq == index, labels[index * rows : (index + 1) * rows].reshape(1, rows), 0)
            for index in range(4)
        ),
        place_row_ref,
        place_col_ref,
        mode_ref,
        places_ref,
    )
    sorting(place_row_ref, side, hot_ref)
    mask_ref[...] = image_mask(mode_ref, half).astype(BF16)

    if gathers:
        gather_qkv.pass_on()
    moved = [[], []]
    for piece, cols in enumerate(pieces):
        tokens[piece].wait_recv()
        for part in range(2):
            span = slice(part * half, (part + 1) * half)
            found = dot(hot_ref[0, span, :], tok_ref[:, cols])
            found = found + dot(hot_ref[1, span, :], tok_other_ref[:, cols])
            sorted_ref[span, cols] = found.astype(BF16)
            for k in steps:
                start = part * half + other_of(seq, k) * chunk
                moved[part].append(
                    copies.start(
                        sorted_ref.at[rows_at(start, chunk), cols],
                        got_ref.at[part, k * chunk : (k + 1) * chunk, cols],
                        seq_mate[k],
                    )
                )
    cots = copies.start(cot_ref, cot_other_ref, across)
    if gathers:
        pair_out.wait_recv()
        for copy in keep[1:]:
            copy.wait()
        for source, target in zip(
            (*share_refs, out_pair_ref), (out_all_ref, fc1_all_ref, fc2_all_ref, out_theirs_ref)
        ):
            locals_.start(source, target.at[rows_at(pack * whole, whole), :])
        gather_theirs = Half(out_pair_ref, out_theirs_ref)
        gather_fc1 = Half(fc1_ref, fc1_all_ref)
        gather_qkv.share()
        needed = list(in_flight)
        for k in steps:
            gather_vec[k - 1].wait_recv()
        vec_ref[...] = (vec_got_ref[3] + vec_got_ref[0]) + (vec_got_ref[1] + vec_got_ref[2])
        for copy in needed:
            copy.wait_recv()
            in_flight.remove(copy)
    else:
        vec_ref[...] = vec_in_refs[0][...]
    keep[0].wait()

    def begin(part):
        for copy in moved[part]:
            copy.wait_recv()
        fill_sequence(part, seq, mode_ref, sorted_ref, got_ref, rows_ref)
        project(part, rows_ref, qkv_all_ref, vec_ref, kept, raw_ref)

    def give_back(part, target_ref):
        target_ref[rows_at(seq * chunk, chunk), :] = attended_ref[part, 0:chunk, :]
        given = [
            copies.start(
                attended_ref.at[part, k * chunk : (k + 1) * chunk, :],
                target_ref.at[rows_at(seq * chunk, chunk), :],
                seq_mate[k],
            )
            for k in steps
        ]
        for ref, out in zip(kept, kept_out):
            locals_.start(ref.at[part], out.at[part])
        return given

    begin(0)
    attend(0, kept, mask_ref, attended_ref)
    given = give_back(0, mine_ref)
    begin(1)
    attend(1, kept, mask_ref, attended_ref)
    given_long = give_back(1, back_ref)
    if gathers:
        gather_fc2.pass_on()
        gather_out.share()
    for copy in given:
        copy.wait_recv()
    first = copies.start(mine_ref.at[0:half, :], theirs_ref.at[0:half, :], across)
    for copy in given_long:
        copy.wait_recv()
    mine_ref[half:, :] = jnp.where(
        mode_ref[0:1, 0:1] > 0, back_ref[...].astype(F32), attended_ref[1].astype(F32)
    ).astype(BF16)
    second = copies.start(mine_ref.at[half : 2 * half, :], theirs_ref.at[half : 2 * half, :], across)
    if gathers:
        gather_theirs.share()
        gather_fc2.share()
        gather_fc1.share()
        for copy in in_flight:
            copy.wait_recv()
    cots.wait_recv()
    first.wait_recv()
    second.wait_recv()
    copies.finish()
    for copy in locals_.made[4 if gathers else 1 :]:
        copy.wait()


def front(gathers, tokens, cotangent, segment, vectors, qkv, out, fc1, fc2):
    half, width = tokens.shape
    rows = 2 * half
    share, inner = out.shape
    units = fc1.shape[1]
    kept = [
        ((2, half, width), BF16),
        ((2, half, width), BF16),
        ((2, half, 2 * inner), BF16),
        ((2, half, inner), BF16),
        ((2, half, 2 * inner), F32),
        ((2, half, 2 * inner), F32),
    ]
    whole = width if gathers else share
    outs = [
        (shape((half, width)), VMEM),
        (shape((half, width)), HERE),
        (shape((2, half), jnp.int32), VMEM),
        (shape((rows, 1), jnp.int32), VMEM),
        (shape((8, 128), F32), VMEM),
        (shape((8, width), F32), VMEM),
        (shape((rows, inner)), VMEM),
        (shape((rows, inner)), VMEM),
        (shape((3, width, inner)), VMEM),
        (shape((whole, inner)), HERE),
        (shape((whole, inner)), HERE),
        (shape((whole, units)), HERE),
        (shape((whole, units)), HERE),
    ] + [(shape(dims, kind), HERE) for dims, kind in kept]
    copies = 3 + 18 + 1 + 6 + 2 + (3 + 1 + 2 * 12 + 3 * 6 if gathers else 0)
    return pl.pallas_call(
        functools.partial(front_kernel, gathers),
        out_shape=[o[0] for o in outs],
        in_specs=[VMEM, HERE, VMEM] + [HERE] * 4 + [VMEM] * len(vectors),
        out_specs=[o[1] for o in outs],
        scratch_shapes=[
            pltpu.VMEM((rows, width), BF16),
            pltpu.VMEM((2, half, width), BF16),
            pltpu.VMEM((half, width), BF16),
            pltpu.VMEM((half, 2 * inner), F32),
            pltpu.VMEM((half, half), BF16),
            pltpu.VMEM((2, half, inner), BF16),
            pltpu.VMEM((half, inner), BF16),
            pltpu.VMEM((4, 8, width), F32),
            pltpu.VMEM((2, rows, half), BF16),
            pltpu.VMEM((8, rows), jnp.int32),
            pltpu.VMEM((share, inner), BF16),
            pltpu.VMEM((share, inner), BF16),
            pltpu.VMEM((share, units), BF16),
            pltpu.VMEM((share, units), BF16),
        ]
        + [pltpu.VMEM(dims, kind) for dims, kind in kept]
        + [
            pltpu.SemaphoreType.DMA((copies,)),
            pltpu.SemaphoreType.DMA((copies,)),
            pltpu.SemaphoreType.DMA((8 + 2 * KEPT,)),
        ],
        compiler_params=params(collective_id=0, has_side_effects=True),
        name="front",
    )(tokens, cotangent, segment, qkv, out, fc1, fc2, *vectors)


def middle_kernel(*refs):
    (
        tok_ref,
        tok_other_ref,
        cot_ref,
        cot_other_ref,
        place_ref,
        mine_ref,
        theirs_ref,
        vec_ref,
        out_mine_ref,
        out_theirs_ref,
        fc1_all_ref,
        fc2_all_ref,
    ) = refs[:12]
    (
        grad_mixed_out,
        back_mine_ref,
        back_got_ref,
        result_out,
        result_other_out,
        fc1_out,
        fc2_out,
        out_out,
        sum_ref,
    ) = refs[12:21]
    (
        fc1_ref,
        fc2_ref,
        act_ref,
        hidden_ref,
        normed_ref,
        grad_other_ref,
        grad_got_ref,
        grad_own_ref,
        mixed_ref,
        attended_ref,
        back_theirs_ref,
        low_ref,
        turned_ref,
        grad_mixed_ref,
        result_ref,
        result_other_ref,
        fc1_part_ref,
        fc2_part_ref,
        out_part_ref,
        send_sem,
        recv_sem,
        local_sem,
    ) = refs[21:]
    half, width = tok_ref.shape
    rows, inner = mine_ref.shape
    units = fc1_ref.shape[1]
    side = lax.axis_index("hidden")
    across = {"hidden": 1 - side}
    copies, locals_ = Copies(send_sem, recv_sem), Locals(local_sem)
    load_fc1 = locals_.start(fc1_all_ref, fc1_ref)
    load_fc2 = locals_.start(fc2_all_ref, fc2_ref)
    greet([across])
    tiles = 3
    tile = half // tiles
    spans = [slice(index * tile, (index + 1) * tile) for index in range(tiles)]
    sum_ref[...] = jnp.zeros_like(sum_ref)

    def feed(own, index):
        block, span = (0 if own else 1), spans[index]
        start = (side if own else 1 - side) * half + index * tile
        place = place_ref[pl.ds(pl.multiple_of(start, 16), tile), :]
        back = one_hot(place == iota((tile, rows), 1))
        mine = dot(back, mine_ref[...]).astype(BF16)
        theirs = dot(back, theirs_ref[...]).astype(BF16)
        tok = (tok_ref if own else tok_other_ref)[span, :]
        cot = (cot_ref if own else cot_other_ref)[span, :]
        mixed = (
            tok.astype(F32)
            + (dot_nt(mine, out_mine_ref[...]) + dot_nt(theirs, out_theirs_ref[...]))
            + vec_ref[OUT_BIAS : OUT_BIAS + 1, :]
        )
        unit, _ = row_norm(mixed)
        normed = unit * vec_ref[LN2_GAIN : LN2_GAIN + 1, :] + vec_ref[LN2_BIAS : LN2_BIAS + 1, :]
        normed = normed.astype(BF16)
        normed_ref[block, span, :] = normed
        if own:
            mixed_ref[span, :] = mixed
            attended_ref[span, :inner] = mine
            attended_ref[span, inner:] = theirs
            sum_ref[FC2_BIAS : FC2_BIAS + 1, :] += jnp.sum(cot.astype(F32), axis=0, keepdims=True)
        elif index == 0:
            load_fc1.wait()
            load_fc2.wait()
        total = None
        step = 512
        for first in range(0, units, step):
            cols = slice(first, first + step)
            pre = dot(normed, fc1_ref[:, cols])
            grad_act = dot(cot, fc2_ref[:, cols])
            cdf, density = normal_cdf(pre)
            act_ref[block, span, cols] = (pre * cdf).astype(BF16)
            grad_hidden = (grad_act * (cdf + pre * density)).astype(BF16)
            hidden_ref[block, span, cols] = grad_hidden
            add = dot_nt(grad_hidden, fc1_ref[:, cols])
            total = add if total is None else total + add
        sum_ref[LN2_GAIN : LN2_GAIN + 1, :] += jnp.sum(total * unit, axis=0, keepdims=True)
        sum_ref[LN2_BIAS : LN2_BIAS + 1, :] += jnp.sum(total, axis=0, keepdims=True)
        if own:
            grad_own_ref[span, :] = total
        else:
            grad_other_ref[span, :] = total.astype(BF16)

    crossing = []
    for index, span in enumerate(spans):
        feed(False, index)
        crossing.append(copies.start(grad_other_ref.at[span, :], grad_got_ref.at[span, :], across))
    for index in range(tiles):
        feed(True, index)

    back = []
    for index, span in enumerate(spans):
        crossing[index].wait_recv()
        unit, scale = row_norm(mixed_ref[span, :])
        grad = grad_own_ref[span, :] + grad_got_ref[span, :].astype(F32)
        grad = row_norm_back(grad * vec_ref[LN2_GAIN : LN2_GAIN + 1, :], unit, scale)
        grad = grad + cot_ref[span, :].astype(F32)
        grad_mixed_ref[span, :] = grad
        low = grad.astype(BF16)
        low_ref[span, :] = low
        back_theirs_ref[span, :] = dot(low, out_theirs_ref[...]).astype(BF16)
        back.append(copies.start(back_theirs_ref.at[span, :], back_got_ref.at[span, :], across))
        back_mine_ref[span, :] = dot(low, out_mine_ref[...]).astype(BF16)
        sum_ref[OUT_BIAS : OUT_BIAS + 1, :] += jnp.sum(low.astype(F32), axis=0, keepdims=True)
    locals_.start(grad_mixed_ref, grad_mixed_out)

    result_other_ref[...] = dot_nt(act_ref[1], fc2_ref[...]).astype(BF16)
    locals_.start(result_other_ref, result_other_out)
    result_ref[...] = (
        dot_nt(act_ref[0], fc2_ref[...])
        + mixed_ref[...]
        + vec_ref[FC2_BIAS : FC2_BIAS + 1, :]
    )
    locals_.start(result_ref, result_out)

    def outer(first, second, right_ref, part_ref):
        turned_ref[0] = first.T
        turned_ref[1] = second.T
        step = 256

        def one(index, carry):
            cols = pl.ds(pl.multiple_of(index * step, step), step)
            part_ref[:, cols] = (
                dot(turned_ref[0], right_ref[0, :, cols]) + dot(turned_ref[1], right_ref[1, :, cols])
            ).astype(BF16)
            return carry

        lax.fori_loop(0, units // step, one, 0)

    outer(cot_ref[...], cot_other_ref[...], act_ref, fc2_part_ref)
    locals_.start(fc2_part_ref, fc2_out)
    outer(normed_ref[0], normed_ref[1], hidden_ref, fc1_part_ref)
    locals_.start(fc1_part_ref, fc1_out)
    turned_ref[0] = low_ref[...].T
    out_part_ref[...] = dot(turned_ref[0], attended_ref[...]).astype(BF16)
    locals_.start(out_part_ref, out_out)
    for copy in back:
        copy.wait_recv()
    copies.finish()
    for copy in locals_.made[2:]:
        copy.wait()


def middle(token, token_other, cot, cot_other, place, mine, theirs, vectors, out_mine, out_theirs, fc1, fc2):
    half, width = token.shape
    rows, inner = mine.shape
    units = fc1.shape[1]
    block = lambda cols, kind=BF16: pltpu.VMEM((half, cols), kind)
    pair = lambda cols: pltpu.VMEM((2, half, cols), BF16)
    return pl.pallas_call(
        middle_kernel,
        out_shape=(
            shape((half, width), F32),
            shape((half, inner)),
            shape((half, inner)),
            shape((half, width), F32),
            shape((half, width)),
            shape((width, units)),
            shape((width, units)),
            shape((width, 2 * inner)),
            shape((8, width), F32),
        ),
        in_specs=[VMEM] * 10 + [HERE] * 2,
        out_specs=(HERE, VMEM, VMEM, HERE, HERE, HERE, HERE, HERE, VMEM),
        scratch_shapes=[
            pltpu.VMEM((width, units), BF16),
            pltpu.VMEM((width, units), BF16),
            pair(units),
            pair(units),
            pair(width),
            block(width),
            block(width),
            block(width, F32),
            block(width, F32),
            block(2 * inner),
            block(inner),
            block(width),
            pltpu.VMEM((2, width, half), BF16),
            block(width, F32),
            block(width, F32),
            block(width),
            pltpu.VMEM((width, units), BF16),
            pltpu.VMEM((width, units), BF16),
            pltpu.VMEM((width, 2 * inner), BF16),
            pltpu.SemaphoreType.DMA((6,)),
            pltpu.SemaphoreType.DMA((6,)),
            pltpu.SemaphoreType.DMA((8,)),
        ],
        compiler_params=params(60 << 20, collective_id=1, has_side_effects=True),
        name="middle",
    )(token, token_other, cot, cot_other, place, mine, theirs, vectors, out_mine, out_theirs, fc1, fc2)


def attend_back(rows_ref, low_ref, value_ref, mask_ref, raw_ref, grad_low_ref):
    half, inner = rows_ref.shape
    pair = 2 * HEAD
    lane = iota((half, pair), 1)

    def one_pair(index, carry):
        cols = pl.ds(pl.multiple_of(index * pair, pair), pair)
        key_cols = pl.ds(pl.multiple_of(inner + index * pair, pair), pair)
        value_cols = pl.ds(pl.multiple_of(2 * inner + index * pair, pair), pair)
        query = low_ref[:, cols] * SCALE
        key = low_ref[:, key_cols]
        value = value_ref[:, cols]
        grad = rows_ref[:, cols]
        key_turned = (key.astype(F32) * SCALE).T.astype(BF16)
        grad_values, grad_keys, grad_queries = [], [], []
        for head in range(2):
            mine = lane < HEAD if head == 0 else lane >= HEAD
            query_head = jnp.where(mine, query, jnp.zeros_like(query))
            grad_head = jnp.where(mine, grad, jnp.zeros_like(grad))
            weights = jnp.exp(dot_nt(key, query_head))
            if mask_ref is not None:
                weights = weights * mask_ref[...]
            weights = weights * (1.0 / jnp.sum(weights, axis=0, keepdims=True))
            grad_weights = dot_nt(value, grad_head)
            shared = jnp.sum(weights * grad_weights, axis=0, keepdims=True)
            grad_scores = (weights * (grad_weights - shared)).astype(BF16)
            grad_values.append(dot(weights.astype(BF16), grad))
            grad_keys.append(dot(grad_scores, query))
            grad_queries.append(dot(key_turned[head * HEAD : (head + 1) * HEAD, :], grad_scores))
        raw_ref[:, cols] = jnp.concatenate(grad_queries, axis=0).T
        raw_ref[:, key_cols] = jnp.where(lane < HEAD, grad_keys[0], grad_keys[1])
        grad_low_ref[:, value_cols] = jnp.where(lane < HEAD, grad_values[0], grad_values[1]).astype(BF16)
        return carry

    lax.fori_loop(0, inner // pair, one_pair, 0)


def head_norm_back(raw_ref, unit_ref, scale_ref, vec_ref, grad_low_ref, sum_ref):
    group = 4 * HEAD
    means = head_mean_matrix(group)
    for first in range(0, raw_ref.shape[1], group):
        cols = slice(first, first + group)
        grad = raw_ref[:, cols]
        unit = unit_ref[:, cols]
        sum_ref[QK_GAIN : QK_GAIN + 1, cols] += jnp.sum(grad * unit, axis=0, keepdims=True)
        grad = grad * vec_ref[QK_GAIN : QK_GAIN + 1, cols]
        grad = scale_ref[:, cols] * (
            grad - two_part(grad, means) - unit * two_part(grad * unit, means)
        )
        grad_low_ref[:, cols] = grad.astype(BF16)


class Reduce:
    def __init__(self, place, copies, part_ref, scratch, out_ref):
        self.place, self.copies, self.out_ref = place, copies, out_ref
        (
            self.got_ref,
            self.low_ref,
            self.near_ref,
            self.far_ref,
            self.last_ref,
            self.total_ref,
        ) = scratch
        self.less_ref = None
        pack, seq, core, seq_mate, pack_mate = place
        self.cross = copies.start(part_ref.at[:, 1 - core], self.got_ref, seq_mate[1])

    def add(self, own_ref, locals_wait):
        core = self.place[2]
        locals_wait()
        self.cross.wait_recv()
        for index in range(4):
            self.low_ref[index] = (
                own_ref[index].astype(F32) + self.got_ref[index].astype(F32)
            ).astype(BF16)

    def near(self):
        pack, seq, core, seq_mate, pack_mate = self.place
        odd = lax.bitwise_and(pack, 1)
        self.first = [
            self.copies.start(
                self.low_ref.at[(1 - odd) + 2 * index], self.near_ref.at[index], pack_mate[1]
            )
            for index in range(2)
        ]

    def far(self):
        pack, seq, core, seq_mate, pack_mate = self.place
        odd, high = lax.bitwise_and(pack, 1), lax.shift_right_logical(pack, 1)
        for index in range(2):
            self.first[index].wait_recv()
            self.near_ref[index] = (
                self.low_ref[odd + 2 * index].astype(F32) + self.near_ref[index].astype(F32)
            ).astype(BF16)
        self.second = self.copies.start(self.near_ref.at[1 - high], self.far_ref.at[0], pack_mate[2])

    def along(self):
        pack, seq, core, seq_mate, pack_mate = self.place
        high = lax.shift_right_logical(pack, 1)
        self.second.wait_recv()
        self.far_ref[1] = (
            self.near_ref[high].astype(F32) + self.far_ref[0].astype(F32)
        ).astype(BF16)
        self.third = self.copies.start(self.far_ref.at[1], self.last_ref, seq_mate[2])

    def piece(self, mine):
        place = lax.shift_right_logical(self.place[1], 1)
        size = self.low_ref.shape[1] // 2
        return rows_at((place if mine else 1 - place) * size, size)

    def split(self, less_ref, from_ref):
        self.less_ref, self.from_ref = less_ref, from_ref
        source = self.low_ref.at[:, self.piece(False), :]
        self.zeroth = self.copies.start(source, from_ref, self.place[3][2])

    def straight(self):
        pack, seq, core, seq_mate, pack_mate = self.place
        self.zeroth.wait_recv()
        for index in range(4):
            self.less_ref[index] = (
                self.low_ref[index, self.piece(True), :].astype(F32)
                + self.from_ref[index].astype(F32)
            ).astype(BF16)
        self.first = [
            self.copies.start(
                self.less_ref.at[other_of(pack, k)], self.near_ref.at[k - 1], pack_mate[k]
            )
            for k in range(1, 4)
        ]

    def straight_along(self):
        pack, seq, core, seq_mate, pack_mate = self.place
        for copy in self.first:
            copy.wait_recv()
        mine, near = self.less_ref[pack].astype(F32), self.near_ref
        self.far_ref[0] = (
            (mine + near[0].astype(F32)) + (near[1].astype(F32) + near[2].astype(F32))
        ).astype(BF16)
        self.third = self.copies.start(self.far_ref.at[0], self.last_ref, seq_mate[2])

    def own(self, locals_):
        pack, seq, core, seq_mate, pack_mate = self.place
        self.third.wait_recv()
        if self.less_ref is None:
            self.total_ref[...] = (
                self.far_ref[1].astype(F32) + self.last_ref[...].astype(F32)
            ).astype(BF16)
        else:
            self.total_ref[self.piece(True), :] = self.far_ref[0]
            self.total_ref[self.piece(False), :] = self.last_ref[...]
        rows = self.total_ref.shape[0]
        here = self.out_ref.at[rows_at(core * rows, rows), :]
        self.fourth = self.copies.start(self.total_ref, here, seq_mate[1])
        locals_.start(self.total_ref, here)

    def finish(self):
        self.fourth.wait_recv()


def back_kernel(reduces, *refs):
    (
        place_row_ref,
        place_col_ref,
        mode_ref,
        vec_ref,
        back_mine_ref,
        back_other_ref,
        weight_ref,
        sum_in_ref,
        low_all,
        value_all,
        normed_all,
        unit_all,
        head_unit_all,
        head_scale_all,
        result_other_all,
        fc1_all,
        fc2_all,
        out_all,
    ) = refs[:18]
    (
        own_out,
        other_got_ref,
        result_got_ref,
        qkv_out_ref,
        out_out_ref,
        fc1_out_ref,
        fc2_out_ref,
        sum_ref,
    ) = refs[18:26]
    (
        low_ref,
        value_ref,
        normed_ref,
        unit_ref,
        head_unit_ref,
        head_scale_ref,
        sorted_ref,
        got_ref,
        rows_ref,
        raw_ref,
        mask_ref,
        grad_low_ref,
        grad_normed_ref,
        ordered_ref,
        long_ref,
        own_ref,
        other_ref,
        turned_ref,
        qkv_part_ref,
        sum_got_ref,
    ) = refs[26:46]
    reduce_refs = refs[46:-3]
    send_sem, recv_sem, local_sem = refs[-3:]
    half, width = own_ref.shape
    inner = back_mine_ref.shape[1]
    rows = 2 * half
    chunk = half // 4
    steps = range(1, 4)
    pack, seq, side = lax.axis_index("dp"), lax.axis_index("seq"), lax.axis_index("hidden")
    core = lax.bitwise_and(seq, 1)
    across = {"hidden": 1 - side}
    seq_mate = [{"seq": other_of(seq, step)} for step in range(4)]
    pack_mate = [{"dp": other_of(pack, step)} for step in range(4)]
    copies, locals_ = Copies(send_sem, recv_sem), Locals(local_sem)
    place = (pack, seq, core, seq_mate, pack_mate)

    def load(part):
        return [
            locals_.start(source.at[part], target)
            for source, target in (
                (low_all, low_ref),
                (value_all, value_ref),
                (head_unit_all, head_unit_ref),
                (head_scale_all, head_scale_ref),
                (unit_all, unit_ref),
            )
        ]

    load_normed = locals_.start(normed_all, normed_ref)
    loading = load(0)
    greet([across] + seq_mate[1:] + (pack_mate[1:] if reduces else []))

    first = side == 0
    place_own = jnp.where(first, place_row_ref[0:1, :], place_row_ref[1:2, :])
    place_other = jnp.where(first, place_row_ref[1:2, :], place_row_ref[0:1, :])
    moved = []
    for part in range(2):
        target = iota((half, half), 0) + part * half
        found = dot(one_hot(target == place_own), back_mine_ref[...])
        found = found + dot(one_hot(target == place_other), back_other_ref[...])
        sorted_ref[part * half : (part + 1) * half, :] = found.astype(BF16)
        moved.append(
            [
                copies.start(
                    sorted_ref.at[rows_at(part * half + other_of(seq, k) * chunk, chunk), :],
                    got_ref.at[part, k * chunk : (k + 1) * chunk, :],
                    seq_mate[k],
                )
                for k in steps
            ]
        )
    if reduces:
        scratch = [reduce_refs[index * 7 : (index + 1) * 7] for index in range(6)]
        parts = []
        for index, (source, target) in enumerate(
            ((fc1_all, fc1_out_ref), (fc2_all, fc2_out_ref), (out_all, out_out_ref))
        ):
            mine = locals_.start(source.at[:, core], scratch[index][0])
            parts.append((Reduce(place, copies, source, scratch[index][1:], target), mine))
        (fc1_sum, fc1_mine), (fc2_sum, fc2_mine), (out_sum, out_mine) = parts
        out_wide_ref, out_got_ref = reduce_refs[42:44]
    work_ref = sum_got_ref.at[9]
    work_ref[...] = sum_in_ref[...]
    if reduces:
        fc1_sum.add(scratch[0][0], fc1_mine.wait)
        fc1_sum.near()
        out_mine.wait()
        out_sum.cross.wait_recv()
        for index in range(4):
            both = scratch[2][0][index].astype(F32) + scratch[2][1][index].astype(F32)
            scratch[2][2][index] = both[:, :inner].astype(BF16)
            out_wide_ref[index] = both[:, inner:].astype(BF16)
        out_cross = copies.start(out_wide_ref, out_got_ref, across)
        fc2_sum.add(scratch[1][0], fc2_mine.wait)
        fc2_sum.split(*reduce_refs[50:52])
    result_cross = copies.start(result_other_all, result_got_ref, across)
    load_normed.wait()
    for part in range(2):
        turned_ref[part] = normed_ref[part].T
    mask_ref[...] = image_mask(mode_ref, half)

    wide = width // 2
    pieces = [slice(0, wide), slice(wide, width)]

    def attention(part):
        for copy in moved[part]:
            copy.wait_recv()
        fill_sequence(part, seq, mode_ref, sorted_ref, got_ref, rows_ref)
        for copy in loading:
            copy.wait()
        grad_low = grad_low_ref.at[part]
        attend_back(rows_ref, low_ref, value_ref, mask_ref if part else None, raw_ref, grad_low)
        head_norm_back(raw_ref, head_unit_ref, head_scale_ref, vec_ref, grad_low, work_ref)
        total = dot_nt(grad_low[:, :inner], weight_ref[0])
        total = total + dot_nt(grad_low[:, inner : 2 * inner], weight_ref[1])
        total = total + dot_nt(grad_low[:, 2 * inner :], weight_ref[2])
        work_ref[LN1_GAIN : LN1_GAIN + 1, :] += jnp.sum(
            total * unit_ref[...].astype(F32), axis=0, keepdims=True
        )
        work_ref[LN1_BIAS : LN1_BIAS + 1, :] += jnp.sum(total, axis=0, keepdims=True)
        grad_normed_ref[part] = total.astype(BF16)
        target_ref = ordered_ref if part == 0 else long_ref
        target_ref[rows_at(seq * chunk, chunk), :] = grad_normed_ref[part, 0:chunk, :]
        return [
            [
                copies.start(
                    grad_normed_ref.at[part, k * chunk : (k + 1) * chunk, cols],
                    target_ref.at[rows_at(seq * chunk, chunk), cols],
                    seq_mate[k],
                )
                for k in steps
            ]
            for cols in ([slice(0, width)] if part == 0 else pieces)
        ]

    returned = attention(0)
    loading = load(1)
    if reduces:
        fc1_sum.far()
        out_cross.wait_recv()
        for index in range(4):
            out_sum.low_ref[index] = (
                out_sum.low_ref[index].astype(F32) + out_got_ref[index].astype(F32)
            ).astype(BF16)
        out_sum.near()
    returned += attention(1)

    sums = copies.start(work_ref, sum_got_ref.at[0], across)
    def qkv_block(kind, index, which):
        share = width // 8
        span = rows_at((2 * index + which) * share, share)
        cols = slice(kind * inner, (kind + 1) * inner)
        qkv_part_ref[kind, index, which] = (
            dot(turned_ref[0, span, :], grad_low_ref[0, :, cols])
            + dot(turned_ref[1, span, :], grad_low_ref[1, :, cols])
        ).astype(BF16)

    qkv_sums = []
    for kind in (2, 1, 0):
        for index in range(4):
            qkv_block(kind, index, 1 - core)
        if reduces:
            qkv_sums.append(
                Reduce(
                    place, copies, qkv_part_ref.at[kind], scratch[3 + kind][1:], qkv_out_ref.at[kind]
                )
            )
        for index in range(4):
            qkv_block(kind, index, core)
    if reduces:
        fc2_sum.straight()
        out_sum.far()
        for kind, each in zip((2, 1, 0), qkv_sums):
            each.cross.wait_recv()
            for index in range(4):
                each.low_ref[index] = (
                    qkv_part_ref[kind, index, core].astype(F32) + each.got_ref[index].astype(F32)
                ).astype(BF16)
            each.split(*reduce_refs[44 + 2 * kind : 46 + 2 * kind])
    else:
        keep = locals_.start(qkv_part_ref, qkv_out_ref)

    def unsort(target_ref, which, cols):
        start = pl.multiple_of(which * half, 16)
        back = one_hot(place_col_ref[pl.ds(start, half), :] == iota((half, rows), 1))
        target_ref[:, cols] = dot(back, ordered_ref[:, cols]).astype(BF16)

    for copy in returned[0]:
        copy.wait_recv()
    crossing = []
    for cols, coming in zip(pieces, returned[1:]):
        for copy in coming:
            copy.wait_recv()
        ordered_ref[half:, cols] = jnp.where(
            mode_ref[0:1, 0:1] > 0,
            long_ref[:, cols].astype(F32),
            grad_normed_ref[1, :, cols].astype(F32),
        ).astype(BF16)
        unsort(other_ref, 1 - side, cols)
        crossing.append(copies.start(other_ref.at[:, cols], other_got_ref.at[:, cols], across))
    if reduces:
        fc1_sum.along()
    sums.wait_recv()
    sum_got_ref[1] = work_ref[...] + sum_got_ref[0]
    around = [copies.start(sum_got_ref.at[1], sum_got_ref.at[1 + k], seq_mate[k]) for k in steps]
    if reduces:
        for each in qkv_sums:
            each.straight()
    unsort(own_ref, side, slice(0, width))
    own_copy = locals_.start(own_ref, own_out)
    for copy in around:
        copy.wait_recv()
    sum_got_ref[5] = (sum_got_ref[1] + sum_got_ref[2]) + (sum_got_ref[3] + sum_got_ref[4])
    if reduces:
        through = [copies.start(sum_got_ref.at[5], sum_got_ref.at[5 + k], pack_mate[k]) for k in steps]
        fc2_sum.straight_along()
        out_sum.along()
        fc1_sum.own(locals_)
        for each in qkv_sums:
            each.straight_along()
        fc2_sum.own(locals_)
        out_sum.own(locals_)
        for copy in through:
            copy.wait_recv()
        sum_ref[...] = (sum_got_ref[5] + sum_got_ref[6]) + (sum_got_ref[7] + sum_got_ref[8])
        for each in qkv_sums:
            each.own(locals_)
        for each in (fc1_sum, fc2_sum, out_sum, *qkv_sums):
            each.finish()
    else:
        sum_ref[...] = sum_got_ref[5]
        keep.wait()
    for copy in crossing:
        copy.wait_recv()
    result_cross.wait_recv()
    copies.finish()
    own_copy.wait()
    if reduces:
        for copy in locals_.made[-6:]:
            copy.wait()


def back(reduces, place_row, place_col, mode, vectors, back_mine, back_other, weight, sums, kept, result_other, fc1_part, fc2_part, out_part, packs):
    normed, unit, low, value, head_unit, head_scale = kept
    half, width = result_other.shape
    inner = back_mine.shape[1]
    units = fc1_part.shape[1]
    share = width // packs
    rows = 2 * half
    block = lambda cols, kind=BF16: pltpu.VMEM((half, cols), kind)
    pair = lambda cols: pltpu.VMEM((2, half, cols), BF16)
    cut = (4, 2, width // 8)
    piece = width // 8

    def summing(columns, wide, owns, split):
        last = piece // 2 if split else piece
        return [
            pltpu.VMEM((4, piece, wide) if owns else (8, 128), BF16),
            pltpu.VMEM((4, piece, wide), BF16),
            pltpu.VMEM((4, piece, columns), BF16),
            pltpu.VMEM((3 if split else 2, last, columns), BF16),
            pltpu.VMEM((2, last, columns), BF16),
            pltpu.VMEM((last, columns), BF16),
            pltpu.VMEM((piece, columns), BF16),
        ]

    reduce_scratch = []
    if reduces:
        reduce_scratch = (
            summing(units, units, True, False)
            + summing(units, units, True, True)
            + summing(inner, 2 * inner, True, False)
            + summing(inner, inner, False, True) * 3
            + [pltpu.VMEM((4, piece, inner), BF16)] * 2
            + [pltpu.VMEM((4, piece // 2, inner), BF16)] * 6
            + [pltpu.VMEM((4, piece // 2, units), BF16)] * 2
        )
    copies = 6 + 1 + 9 + 1 + 3 + 2 + (3 + 2 * 6 + 1 + 4 * 7 if reduces else 0)
    return pl.pallas_call(
        functools.partial(back_kernel, reduces),
        out_shape=(
            shape((half, width)),
            shape((half, width)),
            shape((half, width)),
            shape((3, share, inner) if reduces else (3, *cut, inner)),
            shape((share, inner)),
            shape((share, units)),
            shape((share, units)),
            shape((8, width), F32),
        ),
        in_specs=[VMEM] * 8 + [HERE] * 10,
        out_specs=(HERE,) * 7 + (VMEM,),
        scratch_shapes=[
            block(2 * inner),
            block(inner),
            pair(width),
            block(width),
            block(2 * inner, F32),
            block(2 * inner, F32),
            pltpu.VMEM((rows, inner), BF16),
            pair(inner),
            block(inner),
            block(2 * inner, F32),
            pltpu.VMEM((half, half), F32),
            pair(3 * inner),
            pair(width),
            pltpu.VMEM((rows, width), BF16),
            block(width),
            block(width),
            block(width),
            pltpu.VMEM((2, width, half), BF16),
            pltpu.VMEM((3, *cut, inner), BF16),
            pltpu.VMEM((10, 8, width), F32),
        ]
        + reduce_scratch
        + [
            pltpu.SemaphoreType.DMA((copies,)),
            pltpu.SemaphoreType.DMA((copies,)),
            pltpu.SemaphoreType.DMA((24,)),
        ],
        compiler_params=params(63 << 20, collective_id=2, has_side_effects=True),
        name="back",
    )(
        place_row,
        place_col,
        mode,
        vectors,
        back_mine,
        back_other,
        weight,
        sums,
        low,
        value,
        normed,
        unit,
        head_unit,
        head_scale,
        result_other,
        fc1_part.reshape(*cut, -1),
        fc2_part.reshape(*cut, -1),
        out_part.reshape(*cut, -1),
    )


def finish_kernel(*refs):
    tok_ref, own_ref, got_ref, grad_mixed_ref, result_ref, result_got_ref, vec_ref, sum_ref = refs[:8]
    sources, refs = refs[8:12], refs[12:]
    output_ref, input_grad_ref = refs[:2]
    vec_outs, gain_out, targets = refs[2:8], refs[8], refs[9:13]
    for source, target in zip(sources, targets):
        target[...] = source[...].astype(F32)

    @pl.when(pl.program_id(0) == 0)
    def _():
        pack = lax.axis_index("dp")
        share, width = vec_outs[0].shape[0], vec_ref.shape[1]
        sums = sum_ref[...]
        mine = sum(
            jnp.where(pack == index, sums[:, index * share : (index + 1) * share], 0.0)
            for index in range(width // share)
        )
        for index, out_ref in enumerate(vec_outs):
            out_ref[...] = mine[index : index + 1, :].reshape(share)
        few = gain_out.shape[1]
        for index in range(2):
            row = sums[QK_GAIN : QK_GAIN + 1, index * width // 2 : (index + 1) * width // 2]
            row = sum(row[:, first : first + HEAD] for first in range(0, width // 2, HEAD))
            gain_out[index : index + 1, :] = sum(
                jnp.where(pack == place, row[:, place * few : (place + 1) * few], 0.0)
                for place in range(HEAD // few)
            )

    output_ref[...] = (result_ref[...] + result_got_ref[...].astype(F32)).astype(BF16)
    unit, scale = row_norm(tok_ref[...].astype(F32))
    grad = own_ref[...].astype(F32) + got_ref[...].astype(F32)
    grad = row_norm_back(grad * vec_ref[LN1_GAIN : LN1_GAIN + 1, :], unit, scale)
    input_grad_ref[...] = (grad_mixed_ref[...] + grad).astype(BF16)


def finish(token, own, got, grad_mixed, result, result_got, vectors, sums, arrays, share, few):
    half, width = token.shape
    tile = half // 4
    by_row = pl.BlockSpec((tile, width), lambda i: (i, 0))
    whole = pl.BlockSpec((8, width), lambda i: (0, 0))
    parts = 4 if share % 32 == 0 else 1

    def block(array):
        lead = array.shape[:-2]
        dims = (*lead, share // parts, array.shape[-1])
        return pl.BlockSpec(dims, lambda i: (*(0,) * len(lead), i if parts > 1 else 0, 0))

    return pl.pallas_call(
        finish_kernel,
        out_shape=[shape((half, width))] * 2
        + [shape((share,), F32)] * 6
        + [shape((2, few), F32)]
        + [shape(array.shape, F32) for array in arrays],
        grid=(half // tile,),
        in_specs=[by_row] * 6 + [whole] * 2 + [block(array) for array in arrays],
        out_specs=[by_row] * 2
        + [pl.BlockSpec((share,), lambda i: (0,))] * 6
        + [pl.BlockSpec((2, few), lambda i: (0, 0))]
        + [block(array) for array in arrays],
        compiler_params=params(60 << 20, dimension_semantics=("arbitrary",)),
        name="finish",
    )(token, own, got, grad_mixed, result, result_got, vectors, sums, *arrays)


def swap(array, axis, step):
    pairs = [(index, index ^ step) for index in range(lax.axis_size(axis))]
    return lax.ppermute(array, axis, pairs)


def owned_sum(part, dim):
    total = lax.psum_scatter(part.astype(BF16), "dp", scatter_dimension=dim, tiled=True)
    total = (total.astype(F32) + swap(total, "seq", 1).astype(F32)).astype(BF16)
    return total.astype(F32) + swap(total, "seq", 2).astype(F32)


def local(
    tokens,
    segment,
    cotangent,
    ln1_gain,
    ln1_bias,
    qkv_weight,
    qk_gain,
    out_weight,
    out_bias,
    ln2_gain,
    ln2_bias,
    fc1_weight,
    fc2_weight,
    fc2_bias,
):
    half, width = tokens.shape
    packs = lax.axis_size("dp")
    inner = qkv_weight.shape[2]
    share = ln1_gain.shape[0]
    gathers = packs == 4
    pack = lax.axis_index("dp")
    pieces = [ln1_gain, ln1_bias, out_bias, ln2_gain, ln2_bias, fc2_bias]
    if gathers:
        vectors = [*pieces, qk_gain]
    else:
        few = qk_gain.shape[1]
        lanes = jnp.arange(width)
        wide = jnp.where(lanes // share == pack, jnp.tile(jnp.stack(pieces).astype(F32), (1, packs)), 0.0)
        gains = jnp.tile(qk_gain.astype(F32), (1, width // (2 * few))).reshape(1, width)
        gains = jnp.where(lanes % HEAD // few == pack, gains, 0.0)
        vectors = jnp.concatenate([wide, gains, jnp.zeros((1, width), F32)], axis=0)
        vectors = [lax.psum(vectors, "dp")]
        qkv_weight = lax.all_gather(qkv_weight, "dp", axis=1, tiled=True)
    (
        tokens_other,
        cot_other,
        place_row,
        place_col,
        mode,
        vectors,
        mine,
        theirs,
        qkv_full,
        out_mine,
        out_theirs,
        fc1_full,
        fc2_full,
        *kept,
    ) = front(
        gathers, tokens, cotangent, segment, vectors, qkv_weight, out_weight.T, fc1_weight,
        fc2_weight.T,
    )
    if not gathers:
        out_mine = lax.all_gather(out_weight.T, "dp", axis=0, tiled=True)
        out_theirs = swap(out_mine, "hidden", 1)
        fc1_full = lax.all_gather(fc1_weight, "dp", axis=0, tiled=True)
        fc2_full = lax.all_gather(fc2_weight.T, "dp", axis=0, tiled=True)
    (
        grad_mixed,
        back_mine,
        back_other,
        result,
        result_other,
        fc1_part,
        fc2_part,
        out_part,
        sums,
    ) = middle(
        tokens, tokens_other, cotangent, cot_other, place_col, mine, theirs, vectors, out_mine,
        out_theirs, fc1_full, fc2_full,
    )
    own, got, result_got, qkv_owned, out_owned, fc1_owned, fc2_owned, sums = back(
        gathers, place_row, place_col, mode, vectors, back_mine, back_other, qkv_full, sums, kept,
        result_other, fc1_part, fc2_part, out_part, packs,
    )
    if not gathers:
        sums = lax.psum(sums, "dp")
        qkv_owned = owned_sum(qkv_owned.reshape(3, width, inner), 1)
        out_part = out_part[:, :inner].astype(F32) + swap(out_part[:, inner:], "hidden", 1).astype(F32)
        out_owned = owned_sum(out_part, 0)
        fc1_owned = owned_sum(fc1_part, 0)
        fc2_owned = owned_sum(fc2_part, 0)
    output, input_grad, *sums, qk_owned, qkv_owned, out_owned, fc1_owned, fc2_owned = finish(
        tokens, own, got, grad_mixed, result, result_got, vectors, sums,
        [qkv_owned, out_owned, fc1_owned, fc2_owned], share, qk_gain.shape[1],
    )
    return (
        output,
        input_grad,
        sums[LN1_GAIN],
        sums[LN1_BIAS],
        qkv_owned,
        qk_owned,
        out_owned.T,
        sums[OUT_BIAS],
        sums[LN2_GAIN],
        sums[LN2_BIAS],
        fc1_owned,
        fc2_owned.T,
        sums[FC2_BIAS],
    )


def solution(mesh):
    rows = P(("dp", "seq", "hidden"), None)
    in_specs = (
        rows,
        P("dp"),
        rows,
        P("dp"),
        P("dp"),
        P(None, "dp", "hidden"),
        P(None, "dp"),
        P("hidden", "dp"),
        P("dp"),
        P("dp"),
        P("dp"),
        P("dp", "hidden"),
        P("hidden", "dp"),
        P("dp"),
    )
    out_specs = (
        rows,
        rows,
        P("dp"),
        P("dp"),
        P(None, "dp", "hidden"),
        P(None, "dp"),
        P("hidden", "dp"),
        P("dp"),
        P("dp"),
        P("dp"),
        P("dp", "hidden"),
        P("hidden", "dp"),
        P("dp"),
    )
    return jax.shard_map(local, mesh=mesh, in_specs=in_specs, out_specs=out_specs, check_vma=False)
```

```python
import functools

import jax
import jax.numpy as jnp
from jax import lax
from jax.experimental import pallas as pl
from jax.experimental.pallas import tpu as pltpu
from jax.sharding import PartitionSpec as P

HEAD = 64
LONG = 576
IMAGE = 64
LABELS = 128
EPSILON = 1e-06
SCALE = HEAD ** (-0.5)
F32 = jnp.float32
BF16 = jnp.bfloat16

VMEM = pl.BlockSpec(memory_space=pltpu.VMEM)
SMEM = pl.BlockSpec(memory_space=pltpu.SMEM)
HERE = pl.BlockSpec(memory_space=pl.ANY)
LN1_GAIN, LN1_BIAS, OUT_BIAS, LN2_GAIN, LN2_BIAS, FC2_BIAS, QK_GAIN = range(7)


def params(limit=56 << 20, **more):
    return pltpu.CompilerParams(vmem_limit_bytes=limit, **more)


def shape(dims, dtype=BF16):
    return jax.ShapeDtypeStruct(dims, dtype)


def dot(left, right):
    return jnp.dot(left, right, preferred_element_type=F32)


def dot_nt(left, right):
    return lax.dot_general(left, right, (((1,), (1,)), ((), ())), preferred_element_type=F32)


def dot_tn(left, right):
    return lax.dot_general(left, right, (((0,), (0,)), ((), ())), preferred_element_type=F32)


def iota(dims, dim):
    return lax.broadcasted_iota(jnp.int32, dims, dim)


def one_hot(test):
    return jnp.where(test, 1.0, 0.0).astype(BF16)


def two_part(values, matrix):
    high = values.astype(BF16)
    rest = (values - high.astype(F32)).astype(BF16)
    return dot(high, matrix) + dot(rest, matrix)


def head_mean_matrix(width):
    return jnp.where(
        iota((width, width), 0) // HEAD == iota((width, width), 1) // HEAD, 1.0 / HEAD, 0.0
    ).astype(BF16)


def row_norm(values):
    mean = jnp.mean(values, axis=-1, keepdims=True)
    centred = values - mean
    spread = jnp.mean(centred * centred, axis=-1, keepdims=True)
    scale = lax.rsqrt(spread + EPSILON)
    return centred * scale, scale


def row_norm_back(grad_unit, unit, scale):
    first = jnp.mean(grad_unit, axis=-1, keepdims=True)
    second = jnp.mean(grad_unit * unit, axis=-1, keepdims=True)
    return scale * (grad_unit - first - unit * second)


def normal_cdf(values):
    size = jnp.abs(values) * (2.0 ** -0.5)
    bell = jnp.exp(-0.5 * values * values)
    t = 1.0 / (1.0 + 0.3275911 * size)
    poly = 1.061405429 * t - 1.453152027
    poly = poly * t + 1.421413741
    poly = poly * t - 0.284496736
    poly = poly * t + 0.254829592
    tail = 0.5 * (poly * t) * bell
    return jnp.where(values < 0, tail, 1.0 - tail), bell * 0.3989422804014327


def other_of(value, step):
    return lax.bitwise_xor(value, jnp.int32(step))


def rows_at(start, size):
    return pl.ds(pl.multiple_of(start, 16), size)


class Copies:
    def __init__(self, send_sem, recv_sem):
        self.send_sem, self.recv_sem = send_sem, recv_sem
        self.made = []

    def start(self, source, target, device):
        index = len(self.made)
        copy = pltpu.make_async_remote_copy(
            src_ref=source,
            dst_ref=target,
            send_sem=self.send_sem.at[index],
            recv_sem=self.recv_sem.at[index],
            device_id=device,
            device_id_type=pl.DeviceIdType.MESH,
        )
        copy.start()
        self.made.append(copy)
        return copy

    def finish(self):
        for copy in self.made:
            copy.wait_send()


class Locals:
    def __init__(self, sem):
        self.sem, self.made = sem, []

    def start(self, source, target):
        copy = pltpu.make_async_copy(source, target, self.sem.at[len(self.made)])
        copy.start()
        self.made.append(copy)
        return copy

    def finish(self):
        for copy in self.made:
            copy.wait()


def greet(devices):
    barrier = pltpu.get_barrier_semaphore()
    for device in devices:
        pl.semaphore_signal(barrier, inc=1, device_id=device, device_id_type=pl.DeviceIdType.MESH)
    pl.semaphore_wait(barrier, len(devices))


def place_rows(labels, place_row_ref, place_col_ref, mode_ref, places_ref):
    rows = labels.shape[1]
    half = rows // 2
    chunk = LONG // 4
    by_row = jnp.where(labels == iota((LABELS, rows), 0), 1.0, 0.0)
    count = jnp.sum(by_row, axis=1, keepdims=True)
    cut = 0.5 * (chunk + IMAGE)
    long = jnp.where(count > cut, count, 0.0)
    small = count - long
    total = jnp.sum(long, axis=0, keepdims=True)
    left = iota((LABELS, LABELS), 0)
    right = iota((LABELS, LABELS), 1)

    def before(counts):
        turned = jnp.broadcast_to(counts, (LABELS, LABELS)).T
        return jnp.sum(jnp.where(right < left, turned, 0.0), axis=1, keepdims=True)

    base = jnp.where(long > 0, before(long), total + before(small))
    earlier = one_hot(left < right)
    for first in range(0, rows, LABELS):
        cols = slice(first, first + LABELS)
        block = by_row[:, cols]
        place = base + dot(block.astype(BF16), earlier)
        base = base + jnp.sum(block, axis=1, keepdims=True)
        place = jnp.sum(block * place, axis=0, keepdims=True)
        places_ref[0:1, cols] = place.astype(jnp.int32)
        turned = jnp.broadcast_to(place, (LABELS, LABELS)).T
        place_col_ref[cols, :] = turned[:, 0:1].astype(jnp.int32)
    place_row_ref[0:1, :] = places_ref[0:1, :half]
    place_row_ref[1:2, :] = places_ref[0:1, half:]
    mode_ref[...] = jnp.broadcast_to(jnp.where(total > rows - IMAGE, 1.0, 0.0), mode_ref.shape)


def sorting(place_ref, side, hot_ref):
    half = place_ref.shape[1]
    first = side == 0
    place_own = jnp.where(first, place_ref[0:1, :], place_ref[1:2, :])
    place_other = jnp.where(first, place_ref[1:2, :], place_ref[0:1, :])
    for part in range(2):
        target = iota((half, half), 0) + part * half
        hot_ref[0, part * half : (part + 1) * half, :] = one_hot(target == place_own)
        hot_ref[1, part * half : (part + 1) * half, :] = one_hot(target == place_other)


def put_vectors(pieces, gain_ref, pack, vec_ref):
    share, width = pieces[0].shape[0], vec_ref.shape[1]
    at = one_hot(iota((share, width), 1) == iota((share, width), 0) + pack * share)
    vec_ref[...] = jnp.zeros_like(vec_ref)
    for index, piece in enumerate(pieces):
        row = piece[...].astype(F32).reshape(1, share)
        row = jnp.broadcast_to(row, (8, share)).astype(BF16)
        vec_ref[index : index + 1, :] = dot(row, at)[0:1, :]
    few, half = gain_ref.shape[1], width // 2
    at = one_hot(lax.bitwise_and(iota((few, half), 1), HEAD - 1) == iota((few, half), 0) + pack * few)
    gains = dot(gain_ref[...], at)
    vec_ref[QK_GAIN : QK_GAIN + 1, :half] = gains[0:1, :]
    vec_ref[QK_GAIN : QK_GAIN + 1, half:] = gains[1:2, :]


def fill_sequence(part, seq, mode_ref, sorted_ref, got_ref, rows_ref):
    half = rows_ref.shape[0]
    chunk = half // 4
    home = sorted_ref[rows_at(part * half + seq * chunk, chunk), :]
    for step in range(4):
        rows = home if step == 0 else got_ref[part, step * chunk : (step + 1) * chunk, :]
        if part == 1:
            local = sorted_ref[half + step * chunk : half + (step + 1) * chunk, :]
            rows = jnp.where(mode_ref[0:1, 0:1] > 0, rows.astype(F32), local.astype(F32))
        rows_ref[step * chunk : (step + 1) * chunk, :] = rows.astype(BF16)


def image_mask(mode_ref, rows):
    same = lax.shift_right_logical(iota((rows, rows), 0), 6) == lax.shift_right_logical(
        iota((rows, rows), 1), 6
    )
    return jnp.where(same, 1.0, mode_ref[0:1, 0:1])


def project(part, rows_ref, weight_ref, vec_ref, kept, raw_ref):
    normed_ref, unit_ref, low_ref, value_ref, head_unit_ref, head_scale_ref = (
        ref.at[part] for ref in kept
    )
    half, width = rows_ref.shape
    inner = value_ref.shape[1]
    chunk = half // 4
    for step in range(4):
        rows = slice(step * chunk, (step + 1) * chunk)
        unit, _ = row_norm(rows_ref[rows, :].astype(F32))
        unit_ref[rows, :] = unit.astype(BF16)
        normed = unit * vec_ref[LN1_GAIN : LN1_GAIN + 1, :] + vec_ref[LN1_BIAS : LN1_BIAS + 1, :]
        normed_ref[rows, :] = normed.astype(BF16)
    raw_ref[:, :inner] = dot(normed_ref[...], weight_ref[0])
    raw_ref[:, inner:] = dot(normed_ref[...], weight_ref[1])
    value_ref[...] = dot(normed_ref[...], weight_ref[2]).astype(BF16)
    group = 4 * HEAD
    means = head_mean_matrix(group)
    for first in range(0, 2 * inner, group):
        cols = slice(first, first + group)
        raw = raw_ref[:, cols]
        centred = raw - two_part(raw, means)
        scale = lax.rsqrt(two_part(centred * centred, means) + EPSILON)
        unit = centred * scale
        head_unit_ref[:, cols] = unit
        head_scale_ref[:, cols] = scale
        low_ref[:, cols] = (unit * vec_ref[QK_GAIN : QK_GAIN + 1, cols]).astype(BF16)


def attend(part, kept, mask_ref, attended_ref):
    low_ref, value_ref = kept[2].at[part], kept[3].at[part]
    half, inner = value_ref.shape
    pair = 2 * HEAD
    lane = iota((half, pair), 1)

    def one_pair(index, carry):
        cols = pl.ds(pl.multiple_of(index * pair, pair), pair)
        key_cols = pl.ds(pl.multiple_of(inner + index * pair, pair), pair)
        query = low_ref[:, cols] * SCALE
        key = low_ref[:, key_cols]
        value = jnp.concatenate([value_ref[:, cols], jnp.ones((half, pair), BF16)], axis=1)
        found = []
        for head in range(2):
            mine = lane < HEAD if head == 0 else lane >= HEAD
            scores = dot_nt(jnp.where(mine, query, jnp.zeros_like(query)), key)
            weights = jnp.exp(scores).astype(BF16)
            if part == 1:
                weights = weights * mask_ref[...]
            both = dot(weights, value)
            found.append(both[:, :pair] / both[:, pair:])
        attended_ref[part, :, cols] = jnp.where(lane < HEAD, found[0], found[1]).astype(BF16)
        return carry

    lax.fori_loop(0, inner // pair, one_pair, 0)


KEPT = 6


def front_kernel(gathers, *refs):
    tok_ref, cot_ref, seg_ref, qkv_ref, out_ref, fc1_ref, fc2_ref = refs[:7]
    vec_in_refs, refs = (refs[7:14], refs[14:]) if gathers else (refs[7:8], refs[8:])
    (
        tok_other_ref,
        cot_other_ref,
        place_row_ref,
        place_col_ref,
        mode_ref,
        vec_ref,
        mine_ref,
        theirs_ref,
        qkv_all_ref,
        out_all_ref,
        out_theirs_ref,
        fc1_all_ref,
        fc2_all_ref,
    ) = refs[:13]
    kept_out = refs[13 : 13 + KEPT]
    (
        sorted_ref,
        got_ref,
        rows_ref,
        raw_ref,
        mask_ref,
        attended_ref,
        back_ref,
        vec_got_ref,
        hot_ref,
        places_ref,
        out_pair_ref,
    ) = refs[13 + KEPT : 24 + KEPT]
    share_refs = refs[24 + KEPT : 27 + KEPT]
    kept = refs[27 + KEPT : 27 + 2 * KEPT]
    send_sem, recv_sem, local_sem = refs[27 + 2 * KEPT :]
    pack, seq, side = lax.axis_index("dp"), lax.axis_index("seq"), lax.axis_index("hidden")
    core = lax.bitwise_and(seq, 1)
    half, width = tok_ref.shape
    chunk = half // 4
    steps = range(1, 4)
    across = {"hidden": 1 - side}
    seq_mate = [{"seq": other_of(seq, step)} for step in range(4)]
    pack_mate = [{"dp": other_of(pack, step)} for step in range(4)]
    greet([across] + seq_mate[1:] + (pack_mate[1:] if gathers else []))
    copies, locals_ = Copies(send_sem, recv_sem), Locals(local_sem)

    wide = width // 3
    pieces = [slice(first, first + wide) for first in range(0, width, wide)]
    tokens = [copies.start(tok_ref.at[:, c], tok_other_ref.at[:, c], across) for c in pieces]
    whole = fc1_ref.shape[0]
    in_flight = []

    def rows_of(ref, index, piece, size):
        rows = rows_at(index * whole + piece * size, size)
        return ref.at[:, rows, :] if len(ref.shape) == 3 else ref.at[rows, :]

    class Half:
        def __init__(self, source, target):
            self.target, self.size = target, whole // 2
            self.first = [
                copies.start(
                    rows_of(source, 0, core, self.size),
                    rows_of(target, pack, core, self.size),
                    pack_mate[k],
                )
                for k in steps
            ]

        def share(self):
            for k in steps:
                self.first[k - 1].wait_recv()
                there = rows_of(self.target, other_of(pack, k), core, self.size)
                in_flight.append(copies.start(there, there, seq_mate[1]))

    class Quarter:
        def __init__(self, source, target):
            self.target, self.size = target, whole // 4
            self.first = [
                copies.start(
                    rows_of(source, 0, seq, self.size),
                    rows_of(target, pack, seq, self.size),
                    pack_mate[k],
                )
                for k in steps
            ]
            self.second = []

        def there(self, k, piece):
            return rows_of(self.target, other_of(pack, k), piece, self.size)

        def pass_on(self):
            for k in steps:
                self.first[k - 1].wait_recv()
                there = self.there(k, seq)
                self.second.append(copies.start(there, there, seq_mate[2]))
            for k in steps:
                there = self.there(k, seq)
                in_flight.append(copies.start(there, there, seq_mate[1]))

        def share(self):
            for k in steps:
                self.second[k - 1].wait_recv()
                there = self.there(k, other_of(seq, 2))
                in_flight.append(copies.start(there, there, seq_mate[1]))

    if gathers:
        gather_qkv = Quarter(qkv_ref, qkv_all_ref)
        put_vectors(vec_in_refs[:6], vec_in_refs[6], pack, vec_got_ref.at[3])
        gather_vec = [
            copies.start(vec_got_ref.at[3], vec_got_ref.at[k - 1], pack_mate[k]) for k in steps
        ]
        pair_out = copies.start(out_ref, out_pair_ref, across)
        gather_out = Half(out_ref, out_all_ref)
        gather_fc2 = Quarter(fc2_ref, fc2_all_ref)
        keep = [locals_.start(qkv_ref, qkv_all_ref.at[:, rows_at(pack * whole, whole), :])] + [
            locals_.start(source, target)
            for source, target in zip((out_ref, fc1_ref, fc2_ref), share_refs)
        ]
    else:
        keep = [locals_.start(qkv_ref, qkv_all_ref)]
    rows = 2 * half
    labels = seg_ref[...]
    place_rows(
        sum(
            jnp.where(seq == index, labels[index * rows : (index + 1) * rows].reshape(1, rows), 0)
            for index in range(4)
        ),
        place_row_ref,
        place_col_ref,
        mode_ref,
        places_ref,
    )
    sorting(place_row_ref, side, hot_ref)
    mask_ref[...] = image_mask(mode_ref, half).astype(BF16)

    if gathers:
        gather_qkv.pass_on()
    moved = [[], []]
    for piece, cols in enumerate(pieces):
        tokens[piece].wait_recv()
        for part in range(2):
            span = slice(part * half, (part + 1) * half)
            found = dot(hot_ref[0, span, :], tok_ref[:, cols])
            found = found + dot(hot_ref[1, span, :], tok_other_ref[:, cols])
            sorted_ref[span, cols] = found.astype(BF16)
            for k in steps:
                start = part * half + other_of(seq, k) * chunk
                moved[part].append(
                    copies.start(
                        sorted_ref.at[rows_at(start, chunk), cols],
                        got_ref.at[part, k * chunk : (k + 1) * chunk, cols],
                        seq_mate[k],
                    )
                )
    cots = copies.start(cot_ref, cot_other_ref, across)
    if gathers:
        pair_out.wait_recv()
        for copy in keep[1:]:
            copy.wait()
        for source, target in zip(
            (*share_refs, out_pair_ref), (out_all_ref, fc1_all_ref, fc2_all_ref, out_theirs_ref)
        ):
            locals_.start(source, target.at[rows_at(pack * whole, whole), :])
        gather_theirs = Half(out_pair_ref, out_theirs_ref)
        gather_fc1 = Half(fc1_ref, fc1_all_ref)
        gather_qkv.share()
        needed = list(in_flight)
        for k in steps:
            gather_vec[k - 1].wait_recv()
        vec_ref[...] = (vec_got_ref[3] + vec_got_ref[0]) + (vec_got_ref[1] + vec_got_ref[2])
        for copy in needed:
            copy.wait_recv()
            in_flight.remove(copy)
    else:
        vec_ref[...] = vec_in_refs[0][...]
    keep[0].wait()

    def begin(part):
        for copy in moved[part]:
            copy.wait_recv()
        fill_sequence(part, seq, mode_ref, sorted_ref, got_ref, rows_ref)
        project(part, rows_ref, qkv_all_ref, vec_ref, kept, raw_ref)

    def give_back(part, target_ref):
        target_ref[rows_at(seq * chunk, chunk), :] = attended_ref[part, 0:chunk, :]
        given = [
            copies.start(
                attended_ref.at[part, k * chunk : (k + 1) * chunk, :],
                target_ref.at[rows_at(seq * chunk, chunk), :],
                seq_mate[k],
            )
            for k in steps
        ]
        for ref, out in zip(kept, kept_out):
            locals_.start(ref.at[part], out.at[part])
        return given

    begin(0)
    attend(0, kept, mask_ref, attended_ref)
    given = give_back(0, mine_ref)
    begin(1)
    attend(1, kept, mask_ref, attended_ref)
    given_long = give_back(1, back_ref)
    if gathers:
        gather_fc2.pass_on()
        gather_out.share()
    for copy in given:
        copy.wait_recv()
    first = copies.start(mine_ref.at[0:half, :], theirs_ref.at[0:half, :], across)
    for copy in given_long:
        copy.wait_recv()
    mine_ref[half:, :] = jnp.where(
        mode_ref[0:1, 0:1] > 0, back_ref[...].astype(F32), attended_ref[1].astype(F32)
    ).astype(BF16)
    second = copies.start(mine_ref.at[half : 2 * half, :], theirs_ref.at[half : 2 * half, :], across)
    if gathers:
        gather_theirs.share()
        gather_fc2.share()
        gather_fc1.share()
        for copy in in_flight:
            copy.wait_recv()
    cots.wait_recv()
    first.wait_recv()
    second.wait_recv()
    copies.finish()
    for copy in locals_.made[4 if gathers else 1 :]:
        copy.wait()


def front(gathers, tokens, cotangent, segment, vectors, qkv, out, fc1, fc2):
    half, width = tokens.shape
    rows = 2 * half
    share, inner = out.shape
    units = fc1.shape[1]
    kept = [
        ((2, half, width), BF16),
        ((2, half, width), BF16),
        ((2, half, 2 * inner), BF16),
        ((2, half, inner), BF16),
        ((2, half, 2 * inner), F32),
        ((2, half, 2 * inner), F32),
    ]
    whole = width if gathers else share
    outs = [
        (shape((half, width)), VMEM),
        (shape((half, width)), HERE),
        (shape((2, half), jnp.int32), VMEM),
        (shape((rows, 1), jnp.int32), VMEM),
        (shape((8, 128), F32), VMEM),
        (shape((8, width), F32), VMEM),
        (shape((rows, inner)), VMEM),
        (shape((rows, inner)), VMEM),
        (shape((3, width, inner)), VMEM),
        (shape((whole, inner)), HERE),
        (shape((whole, inner)), HERE),
        (shape((whole, units)), HERE),
        (shape((whole, units)), HERE),
    ] + [(shape(dims, kind), HERE) for dims, kind in kept]
    copies = 3 + 18 + 1 + 6 + 2 + (3 + 1 + 2 * 12 + 3 * 6 if gathers else 0)
    return pl.pallas_call(
        functools.partial(front_kernel, gathers),
        out_shape=[o[0] for o in outs],
        in_specs=[VMEM, HERE, VMEM] + [HERE] * 4 + [VMEM] * len(vectors),
        out_specs=[o[1] for o in outs],
        scratch_shapes=[
            pltpu.VMEM((rows, width), BF16),
            pltpu.VMEM((2, half, width), BF16),
            pltpu.VMEM((half, width), BF16),
            pltpu.VMEM((half, 2 * inner), F32),
            pltpu.VMEM((half, half), BF16),
            pltpu.VMEM((2, half, inner), BF16),
            pltpu.VMEM((half, inner), BF16),
            pltpu.VMEM((4, 8, width), F32),
            pltpu.VMEM((2, rows, half), BF16),
            pltpu.VMEM((8, rows), jnp.int32),
            pltpu.VMEM((share, inner), BF16),
            pltpu.VMEM((share, inner), BF16),
            pltpu.VMEM((share, units), BF16),
            pltpu.VMEM((share, units), BF16),
        ]
        + [pltpu.VMEM(dims, kind) for dims, kind in kept]
        + [
            pltpu.SemaphoreType.DMA((copies,)),
            pltpu.SemaphoreType.DMA((copies,)),
            pltpu.SemaphoreType.DMA((8 + 2 * KEPT,)),
        ],
        compiler_params=params(collective_id=0, has_side_effects=True),
        name="front",
    )(tokens, cotangent, segment, qkv, out, fc1, fc2, *vectors)


def middle_kernel(*refs):
    (
        tok_all_ref,
        tok_other_ref,
        cot_all_ref,
        cot_other_ref,
        place_ref,
        mine_ref,
        theirs_ref,
        vec_ref,
        out_mine_ref,
        out_theirs_ref,
        fc1_all_ref,
        fc2_all_ref,
    ) = refs[:12]
    (
        grad_mixed_out,
        back_mine_ref,
        back_got_ref,
        result_out,
        result_other_out,
        fc1_out,
        fc2_out,
        out_out,
        sum_ref,
    ) = refs[12:21]
    (
        fc1_ref,
        fc2_ref,
        act_ref,
        hidden_ref,
        normed_ref,
        grad_other_ref,
        grad_got_ref,
        grad_own_ref,
        mixed_ref,
        attended_ref,
        back_theirs_ref,
        low_ref,
        turned_ref,
        grad_mixed_ref,
        result_ref,
        result_other_ref,
        fc1_part_ref,
        fc2_part_ref,
        out_part_ref,
        tok_ref,
        cot_ref,
        send_sem,
        recv_sem,
        local_sem,
    ) = refs[21:]
    half, width = tok_ref.shape
    rows, inner = mine_ref.shape
    units = fc1_ref.shape[1]
    side = lax.axis_index("hidden")
    across = {"hidden": 1 - side}
    copies, locals_ = Copies(send_sem, recv_sem), Locals(local_sem)
    load_fc1 = locals_.start(fc1_all_ref, fc1_ref)
    load_fc2 = locals_.start(fc2_all_ref, fc2_ref)
    late = [locals_.start(tok_all_ref, tok_ref), locals_.start(cot_all_ref, cot_ref)]
    greet([across])
    tile = half // 3
    spans = [slice(first, first + tile) for first in range(0, half, tile)]
    tile = half // 2
    own_spans = [slice(first, first + tile) for first in range(0, half, tile)]
    sum_ref[...] = jnp.zeros_like(sum_ref)

    def feed(own, span):
        block, tile = (0 if own else 1), span.stop - span.start
        start = (side if own else 1 - side) * half + span.start
        place = place_ref[pl.ds(pl.multiple_of(start, 16), tile), :]
        back = one_hot(place == iota((tile, rows), 1))
        mine = dot(back, mine_ref[...]).astype(BF16)
        theirs = dot(back, theirs_ref[...]).astype(BF16)
        tok = (tok_ref if own else tok_other_ref)[span, :]
        cot = (cot_ref if own else cot_other_ref)[span, :]
        mixed = (
            tok.astype(F32)
            + (dot_nt(mine, out_mine_ref[...]) + dot_nt(theirs, out_theirs_ref[...]))
            + vec_ref[OUT_BIAS : OUT_BIAS + 1, :]
        )
        unit, _ = row_norm(mixed)
        normed = unit * vec_ref[LN2_GAIN : LN2_GAIN + 1, :] + vec_ref[LN2_BIAS : LN2_BIAS + 1, :]
        normed = normed.astype(BF16)
        normed_ref[block, span, :] = normed
        if own:
            mixed_ref[span, :] = mixed
            attended_ref[span, :inner] = mine
            attended_ref[span, inner:] = theirs
            sum_ref[FC2_BIAS : FC2_BIAS + 1, :] += jnp.sum(cot.astype(F32), axis=0, keepdims=True)
        elif span.start == 0:
            load_fc1.wait()
            load_fc2.wait()
        total = None
        step = 512
        for first in range(0, units, step):
            cols = slice(first, first + step)
            pre = dot(normed, fc1_ref[:, cols])
            grad_act = dot(cot, fc2_ref[:, cols])
            cdf, density = normal_cdf(pre)
            act_ref[block, span, cols] = (pre * cdf).astype(BF16)
            grad_hidden = (grad_act * (cdf + pre * density)).astype(BF16)
            hidden_ref[block, span, cols] = grad_hidden
            add = dot_nt(grad_hidden, fc1_ref[:, cols])
            total = add if total is None else total + add
        sum_ref[LN2_GAIN : LN2_GAIN + 1, :] += jnp.sum(total * unit, axis=0, keepdims=True)
        sum_ref[LN2_BIAS : LN2_BIAS + 1, :] += jnp.sum(total, axis=0, keepdims=True)
        if own:
            grad_own_ref[span, :] = total
        else:
            grad_other_ref[span, :] = total.astype(BF16)

    crossing = []
    for span in spans:
        feed(False, span)
        crossing.append(copies.start(grad_other_ref.at[span, :], grad_got_ref.at[span, :], across))
    for load in late:
        load.wait()
    for span in own_spans:
        feed(True, span)

    back = []
    for index, span in enumerate(spans):
        crossing[index].wait_recv()
        unit, scale = row_norm(mixed_ref[span, :])
        grad = grad_own_ref[span, :] + grad_got_ref[span, :].astype(F32)
        grad = row_norm_back(grad * vec_ref[LN2_GAIN : LN2_GAIN + 1, :], unit, scale)
        grad = grad + cot_ref[span, :].astype(F32)
        grad_mixed_ref[span, :] = grad
        low = grad.astype(BF16)
        low_ref[span, :] = low
        back_theirs_ref[span, :] = dot(low, out_theirs_ref[...]).astype(BF16)
        back.append(copies.start(back_theirs_ref.at[span, :], back_got_ref.at[span, :], across))
        back_mine_ref[span, :] = dot(low, out_mine_ref[...]).astype(BF16)
        sum_ref[OUT_BIAS : OUT_BIAS + 1, :] += jnp.sum(low.astype(F32), axis=0, keepdims=True)
    locals_.start(grad_mixed_ref, grad_mixed_out)

    result_other_ref[...] = dot_nt(act_ref[1], fc2_ref[...]).astype(BF16)
    locals_.start(result_other_ref, result_other_out)
    result_ref[...] = (
        dot_nt(act_ref[0], fc2_ref[...])
        + mixed_ref[...]
        + vec_ref[FC2_BIAS : FC2_BIAS + 1, :]
    )
    locals_.start(result_ref, result_out)

    def outer(first, second, right_ref, part_ref):
        turned_ref[0] = first.T
        turned_ref[1] = second.T
        step = 256

        def one(index, carry):
            cols = pl.ds(pl.multiple_of(index * step, step), step)
            part_ref[:, cols] = (
                dot(turned_ref[0], right_ref[0, :, cols]) + dot(turned_ref[1], right_ref[1, :, cols])
            ).astype(BF16)
            return carry

        lax.fori_loop(0, units // step, one, 0)

    outer(cot_ref[...], cot_other_ref[...], act_ref, fc2_part_ref)
    locals_.start(fc2_part_ref, fc2_out)
    outer(normed_ref[0], normed_ref[1], hidden_ref, fc1_part_ref)
    locals_.start(fc1_part_ref, fc1_out)
    turned_ref[0] = low_ref[...].T
    out_part_ref[...] = dot(turned_ref[0], attended_ref[...]).astype(BF16)
    locals_.start(out_part_ref, out_out)
    for copy in back:
        copy.wait_recv()
    copies.finish()
    for copy in locals_.made[4:]:
        copy.wait()


def middle(token, token_other, cot, cot_other, place, mine, theirs, vectors, out_mine, out_theirs, fc1, fc2):
    half, width = token.shape
    rows, inner = mine.shape
    units = fc1.shape[1]
    block = lambda cols, kind=BF16: pltpu.VMEM((half, cols), kind)
    pair = lambda cols: pltpu.VMEM((2, half, cols), BF16)
    return pl.pallas_call(
        middle_kernel,
        out_shape=(
            shape((half, width), F32),
            shape((half, inner)),
            shape((half, inner)),
            shape((half, width), F32),
            shape((half, width)),
            shape((width, units)),
            shape((width, units)),
            shape((width, 2 * inner)),
            shape((8, width), F32),
        ),
        in_specs=[HERE, VMEM, HERE] + [VMEM] * 7 + [HERE] * 2,
        out_specs=(HERE, VMEM, VMEM, HERE, HERE, HERE, HERE, HERE, VMEM),
        scratch_shapes=[
            pltpu.VMEM((width, units), BF16),
            pltpu.VMEM((width, units), BF16),
            pair(units),
            pair(units),
            pair(width),
            block(width),
            block(width),
            block(width, F32),
            block(width, F32),
            block(2 * inner),
            block(inner),
            block(width),
            pltpu.VMEM((2, width, half), BF16),
            block(width, F32),
            block(width, F32),
            block(width),
            pltpu.VMEM((width, units), BF16),
            pltpu.VMEM((width, units), BF16),
            pltpu.VMEM((width, 2 * inner), BF16),
            block(width),
            block(width),
            pltpu.SemaphoreType.DMA((6,)),
            pltpu.SemaphoreType.DMA((6,)),
            pltpu.SemaphoreType.DMA((10,)),
        ],
        compiler_params=params(60 << 20, collective_id=1, has_side_effects=True),
        name="middle",
    )(token, token_other, cot, cot_other, place, mine, theirs, vectors, out_mine, out_theirs, fc1, fc2)


def attend_back(rows_ref, low_ref, value_ref, mask_ref, raw_ref, grad_low_ref):
    half, inner = rows_ref.shape
    pair = 2 * HEAD
    lane = iota((half, pair), 1)

    def one_pair(index, carry):
        cols = pl.ds(pl.multiple_of(index * pair, pair), pair)
        key_cols = pl.ds(pl.multiple_of(inner + index * pair, pair), pair)
        value_cols = pl.ds(pl.multiple_of(2 * inner + index * pair, pair), pair)
        query = low_ref[:, cols] * SCALE
        key = low_ref[:, key_cols]
        value = value_ref[:, cols]
        grad = rows_ref[:, cols]
        key_turned = (key.astype(F32) * SCALE).T.astype(BF16)
        grad_values, grad_keys, grad_queries = [], [], []
        for head in range(2):
            mine = lane < HEAD if head == 0 else lane >= HEAD
            query_head = jnp.where(mine, query, jnp.zeros_like(query))
            grad_head = jnp.where(mine, grad, jnp.zeros_like(grad))
            weights = jnp.exp(dot_nt(key, query_head))
            if mask_ref is not None:
                weights = weights * mask_ref[...]
            weights = weights * (1.0 / jnp.sum(weights, axis=0, keepdims=True))
            grad_weights = dot_nt(value, grad_head)
            shared = jnp.sum(weights * grad_weights, axis=0, keepdims=True)
            grad_scores = (weights * (grad_weights - shared)).astype(BF16)
            grad_values.append(dot(weights.astype(BF16), grad))
            grad_keys.append(dot(grad_scores, query))
            grad_queries.append(dot(key_turned[head * HEAD : (head + 1) * HEAD, :], grad_scores))
        raw_ref[:, cols] = jnp.concatenate(grad_queries, axis=0).T
        raw_ref[:, key_cols] = jnp.where(lane < HEAD, grad_keys[0], grad_keys[1])
        grad_low_ref[:, value_cols] = jnp.where(lane < HEAD, grad_values[0], grad_values[1]).astype(BF16)
        return carry

    lax.fori_loop(0, inner // pair, one_pair, 0)


def head_norm_back(raw_ref, unit_ref, scale_ref, vec_ref, grad_low_ref, sum_ref):
    group = 4 * HEAD
    means = head_mean_matrix(group)
    for first in range(0, raw_ref.shape[1], group):
        cols = slice(first, first + group)
        grad = raw_ref[:, cols]
        unit = unit_ref[:, cols]
        sum_ref[QK_GAIN : QK_GAIN + 1, cols] += jnp.sum(grad * unit, axis=0, keepdims=True)
        grad = grad * vec_ref[QK_GAIN : QK_GAIN + 1, cols]
        grad = scale_ref[:, cols] * (
            grad - two_part(grad, means) - unit * two_part(grad * unit, means)
        )
        grad_low_ref[:, cols] = grad.astype(BF16)


class Reduce:
    def __init__(self, place, copies, part_ref, scratch, out_ref):
        self.place, self.copies, self.out_ref = place, copies, out_ref
        (
            self.got_ref,
            self.low_ref,
            self.near_ref,
            self.far_ref,
            self.last_ref,
            self.total_ref,
        ) = scratch
        self.less_ref = None
        pack, seq, core, seq_mate, pack_mate = place
        self.cross = copies.start(part_ref.at[:, 1 - core], self.got_ref, seq_mate[1])

    def add(self, own_ref, locals_wait):
        core = self.place[2]
        locals_wait()
        self.cross.wait_recv()
        for index in range(4):
            self.low_ref[index] = (
                own_ref[index].astype(F32) + self.got_ref[index].astype(F32)
            ).astype(BF16)

    def near(self):
        pack, seq, core, seq_mate, pack_mate = self.place
        odd = lax.bitwise_and(pack, 1)
        self.first = [
            self.copies.start(
                self.low_ref.at[(1 - odd) + 2 * index], self.near_ref.at[index], pack_mate[1]
            )
            for index in range(2)
        ]

    def far(self):
        pack, seq, core, seq_mate, pack_mate = self.place
        odd, high = lax.bitwise_and(pack, 1), lax.shift_right_logical(pack, 1)
        for index in range(2):
            self.first[index].wait_recv()
            self.near_ref[index] = (
                self.low_ref[odd + 2 * index].astype(F32) + self.near_ref[index].astype(F32)
            ).astype(BF16)
        self.second = self.copies.start(self.near_ref.at[1 - high], self.far_ref.at[0], pack_mate[2])

    def along(self):
        pack, seq, core, seq_mate, pack_mate = self.place
        high = lax.shift_right_logical(pack, 1)
        self.second.wait_recv()
        self.far_ref[1] = (
            self.near_ref[high].astype(F32) + self.far_ref[0].astype(F32)
        ).astype(BF16)
        self.third = self.copies.start(self.far_ref.at[1], self.last_ref, seq_mate[2])

    def piece(self, mine):
        place = lax.shift_right_logical(self.place[1], 1)
        size = self.low_ref.shape[1] // 2
        return rows_at((place if mine else 1 - place) * size, size)

    def split(self, less_ref, from_ref):
        self.less_ref, self.from_ref = less_ref, from_ref
        source = self.low_ref.at[:, self.piece(False), :]
        self.zeroth = self.copies.start(source, from_ref, self.place[3][2])

    def straight(self):
        pack, seq, core, seq_mate, pack_mate = self.place
        self.zeroth.wait_recv()
        for index in range(4):
            self.less_ref[index] = (
                self.low_ref[index, self.piece(True), :].astype(F32)
                + self.from_ref[index].astype(F32)
            ).astype(BF16)
        self.first = [
            self.copies.start(
                self.less_ref.at[other_of(pack, k)], self.near_ref.at[k - 1], pack_mate[k]
            )
            for k in range(1, 4)
        ]

    def straight_along(self):
        pack, seq, core, seq_mate, pack_mate = self.place
        for copy in self.first:
            copy.wait_recv()
        mine, near = self.less_ref[pack].astype(F32), self.near_ref
        self.far_ref[0] = (
            (mine + near[0].astype(F32)) + (near[1].astype(F32) + near[2].astype(F32))
        ).astype(BF16)
        self.third = self.copies.start(self.far_ref.at[0], self.last_ref, seq_mate[2])

    def own(self, locals_):
        pack, seq, core, seq_mate, pack_mate = self.place
        self.third.wait_recv()
        if self.less_ref is None:
            self.total_ref[...] = (
                self.far_ref[1].astype(F32) + self.last_ref[...].astype(F32)
            ).astype(BF16)
        else:
            self.total_ref[self.piece(True), :] = self.far_ref[0]
            self.total_ref[self.piece(False), :] = self.last_ref[...]
        rows = self.total_ref.shape[0]
        here = self.out_ref.at[rows_at(core * rows, rows), :]
        self.fourth = self.copies.start(self.total_ref, here, seq_mate[1])
        locals_.start(self.total_ref, here)

    def finish(self):
        self.fourth.wait_recv()


def back_kernel(reduces, *refs):
    (
        place_row_ref,
        place_col_ref,
        mode_ref,
        vec_ref,
        back_mine_ref,
        back_other_ref,
        weight_ref,
        sum_in_ref,
        low_all,
        value_all,
        normed_all,
        unit_all,
        head_unit_all,
        head_scale_all,
        result_other_all,
        fc1_all,
        fc2_all,
        out_all,
    ) = refs[:18]
    (
        own_out,
        other_got_ref,
        result_got_ref,
        qkv_out_ref,
        out_out_ref,
        fc1_out_ref,
        fc2_out_ref,
        sum_ref,
    ) = refs[18:26]
    (
        low_ref,
        value_ref,
        normed_ref,
        unit_ref,
        head_unit_ref,
        head_scale_ref,
        sorted_ref,
        got_ref,
        rows_ref,
        raw_ref,
        mask_ref,
        grad_low_ref,
        grad_normed_ref,
        ordered_ref,
        long_ref,
        own_ref,
        other_ref,
        turned_ref,
        qkv_part_ref,
        sum_got_ref,
    ) = refs[26:46]
    reduce_refs = refs[46:-3]
    send_sem, recv_sem, local_sem = refs[-3:]
    half, width = own_ref.shape
    inner = back_mine_ref.shape[1]
    rows = 2 * half
    chunk = half // 4
    steps = range(1, 4)
    pack, seq, side = lax.axis_index("dp"), lax.axis_index("seq"), lax.axis_index("hidden")
    core = lax.bitwise_and(seq, 1)
    across = {"hidden": 1 - side}
    seq_mate = [{"seq": other_of(seq, step)} for step in range(4)]
    pack_mate = [{"dp": other_of(pack, step)} for step in range(4)]
    copies, locals_ = Copies(send_sem, recv_sem), Locals(local_sem)
    place = (pack, seq, core, seq_mate, pack_mate)

    def load(part):
        return [
            locals_.start(source.at[part], target)
            for source, target in (
                (low_all, low_ref),
                (value_all, value_ref),
                (head_unit_all, head_unit_ref),
                (head_scale_all, head_scale_ref),
                (unit_all, unit_ref),
            )
        ]

    load_normed = locals_.start(normed_all, normed_ref)
    loading = load(0)
    greet([across] + seq_mate[1:] + (pack_mate[1:] if reduces else []))

    first = side == 0
    place_own = jnp.where(first, place_row_ref[0:1, :], place_row_ref[1:2, :])
    place_other = jnp.where(first, place_row_ref[1:2, :], place_row_ref[0:1, :])
    moved = []
    for part in range(2):
        target = iota((half, half), 0) + part * half
        found = dot(one_hot(target == place_own), back_mine_ref[...])
        found = found + dot(one_hot(target == place_other), back_other_ref[...])
        sorted_ref[part * half : (part + 1) * half, :] = found.astype(BF16)
        moved.append(
            [
                copies.start(
                    sorted_ref.at[rows_at(part * half + other_of(seq, k) * chunk, chunk), :],
                    got_ref.at[part, k * chunk : (k + 1) * chunk, :],
                    seq_mate[k],
                )
                for k in steps
            ]
        )
    if reduces:
        scratch = [reduce_refs[index * 7 : (index + 1) * 7] for index in range(6)]
        parts = []
        for index, (source, target) in enumerate(
            ((fc1_all, fc1_out_ref), (fc2_all, fc2_out_ref), (out_all, out_out_ref))
        ):
            mine = locals_.start(source.at[:, core], scratch[index][0])
            parts.append((Reduce(place, copies, source, scratch[index][1:], target), mine))
        (fc1_sum, fc1_mine), (fc2_sum, fc2_mine), (out_sum, out_mine) = parts
        out_wide_ref, out_got_ref = reduce_refs[42:44]
    work_ref = sum_got_ref.at[9]
    work_ref[...] = sum_in_ref[...]
    if reduces:
        fc1_sum.add(scratch[0][0], fc1_mine.wait)
        fc1_sum.near()
        out_mine.wait()
        out_sum.cross.wait_recv()
        for index in range(4):
            both = scratch[2][0][index].astype(F32) + scratch[2][1][index].astype(F32)
            scratch[2][2][index] = both[:, :inner].astype(BF16)
            out_wide_ref[index] = both[:, inner:].astype(BF16)
        out_cross = copies.start(out_wide_ref, out_got_ref, across)
        fc2_sum.add(scratch[1][0], fc2_mine.wait)
        fc2_sum.split(*reduce_refs[50:52])
    result_cross = copies.start(result_other_all, result_got_ref, across)
    load_normed.wait()
    for part in range(2):
        turned_ref[part] = normed_ref[part].T
    mask_ref[...] = image_mask(mode_ref, half)

    wide = width // 2
    pieces = [slice(0, wide), slice(wide, width)]

    def attention(part):
        for copy in moved[part]:
            copy.wait_recv()
        fill_sequence(part, seq, mode_ref, sorted_ref, got_ref, rows_ref)
        for copy in loading:
            copy.wait()
        grad_low = grad_low_ref.at[part]
        attend_back(rows_ref, low_ref, value_ref, mask_ref if part else None, raw_ref, grad_low)
        head_norm_back(raw_ref, head_unit_ref, head_scale_ref, vec_ref, grad_low, work_ref)
        total = dot_nt(grad_low[:, :inner], weight_ref[0])
        total = total + dot_nt(grad_low[:, inner : 2 * inner], weight_ref[1])
        total = total + dot_nt(grad_low[:, 2 * inner :], weight_ref[2])
        work_ref[LN1_GAIN : LN1_GAIN + 1, :] += jnp.sum(
            total * unit_ref[...].astype(F32), axis=0, keepdims=True
        )
        work_ref[LN1_BIAS : LN1_BIAS + 1, :] += jnp.sum(total, axis=0, keepdims=True)
        grad_normed_ref[part] = total.astype(BF16)
        target_ref = ordered_ref if part == 0 else long_ref
        target_ref[rows_at(seq * chunk, chunk), :] = grad_normed_ref[part, 0:chunk, :]
        return [
            [
                copies.start(
                    grad_normed_ref.at[part, k * chunk : (k + 1) * chunk, cols],
                    target_ref.at[rows_at(seq * chunk, chunk), cols],
                    seq_mate[k],
                )
                for k in steps
            ]
            for cols in ([slice(0, width)] if part == 0 else pieces)
        ]

    returned = attention(0)
    loading = load(1)
    if reduces:
        fc1_sum.far()
        out_cross.wait_recv()
        for index in range(4):
            out_sum.low_ref[index] = (
                out_sum.low_ref[index].astype(F32) + out_got_ref[index].astype(F32)
            ).astype(BF16)
        out_sum.near()
    returned += attention(1)

    sums = copies.start(work_ref, sum_got_ref.at[0], across)
    def qkv_block(kind, index, which):
        share = width // 8
        span = rows_at((2 * index + which) * share, share)
        cols = slice(kind * inner, (kind + 1) * inner)
        qkv_part_ref[kind, index, which] = (
            dot(turned_ref[0, span, :], grad_low_ref[0, :, cols])
            + dot(turned_ref[1, span, :], grad_low_ref[1, :, cols])
        ).astype(BF16)

    qkv_sums = []
    for kind in (2, 1, 0):
        for index in range(4):
            qkv_block(kind, index, 1 - core)
        if reduces:
            qkv_sums.append(
                Reduce(
                    place, copies, qkv_part_ref.at[kind], scratch[3 + kind][1:], qkv_out_ref.at[kind]
                )
            )
        for index in range(4):
            qkv_block(kind, index, core)
    if reduces:
        fc2_sum.straight()
        out_sum.far()
        for kind, each in zip((2, 1, 0), qkv_sums):
            each.cross.wait_recv()
            for index in range(4):
                each.low_ref[index] = (
                    qkv_part_ref[kind, index, core].astype(F32) + each.got_ref[index].astype(F32)
                ).astype(BF16)
            each.split(*reduce_refs[44 + 2 * kind : 46 + 2 * kind])
    else:
        keep = locals_.start(qkv_part_ref, qkv_out_ref)

    def unsort(target_ref, which, cols):
        start = pl.multiple_of(which * half, 16)
        back = one_hot(place_col_ref[pl.ds(start, half), :] == iota((half, rows), 1))
        target_ref[:, cols] = dot(back, ordered_ref[:, cols]).astype(BF16)

    for copy in returned[0]:
        copy.wait_recv()
    crossing = []
    for cols, coming in zip(pieces, returned[1:]):
        for copy in coming:
            copy.wait_recv()
        ordered_ref[half:, cols] = jnp.where(
            mode_ref[0:1, 0:1] > 0,
            long_ref[:, cols].astype(F32),
            grad_normed_ref[1, :, cols].astype(F32),
        ).astype(BF16)
        unsort(other_ref, 1 - side, cols)
        crossing.append(copies.start(other_ref.at[:, cols], other_got_ref.at[:, cols], across))
    if reduces:
        fc1_sum.along()
    sums.wait_recv()
    sum_got_ref[1] = work_ref[...] + sum_got_ref[0]
    around = [copies.start(sum_got_ref.at[1], sum_got_ref.at[1 + k], seq_mate[k]) for k in steps]
    if reduces:
        for each in qkv_sums:
            each.straight()
    unsort(own_ref, side, slice(0, width))
    own_copy = locals_.start(own_ref, own_out)
    for copy in around:
        copy.wait_recv()
    sum_got_ref[5] = (sum_got_ref[1] + sum_got_ref[2]) + (sum_got_ref[3] + sum_got_ref[4])
    if reduces:
        through = [copies.start(sum_got_ref.at[5], sum_got_ref.at[5 + k], pack_mate[k]) for k in steps]
        fc2_sum.straight_along()
        out_sum.along()
        fc1_sum.own(locals_)
        for each in qkv_sums:
            each.straight_along()
        fc2_sum.own(locals_)
        out_sum.own(locals_)
        for copy in through:
            copy.wait_recv()
        sum_ref[...] = (sum_got_ref[5] + sum_got_ref[6]) + (sum_got_ref[7] + sum_got_ref[8])
        for each in qkv_sums:
            each.own(locals_)
        for each in (fc1_sum, fc2_sum, out_sum, *qkv_sums):
            each.finish()
    else:
        sum_ref[...] = sum_got_ref[5]
        keep.wait()
    for copy in crossing:
        copy.wait_recv()
    result_cross.wait_recv()
    copies.finish()
    own_copy.wait()
    if reduces:
        for copy in locals_.made[-6:]:
            copy.wait()


def back(reduces, place_row, place_col, mode, vectors, back_mine, back_other, weight, sums, kept, result_other, fc1_part, fc2_part, out_part, packs):
    normed, unit, low, value, head_unit, head_scale = kept
    half, width = result_other.shape
    inner = back_mine.shape[1]
    units = fc1_part.shape[1]
    share = width // packs
    rows = 2 * half
    block = lambda cols, kind=BF16: pltpu.VMEM((half, cols), kind)
    pair = lambda cols: pltpu.VMEM((2, half, cols), BF16)
    cut = (4, 2, width // 8)
    piece = width // 8

    def summing(columns, wide, owns, split):
        last = piece // 2 if split else piece
        return [
            pltpu.VMEM((4, piece, wide) if owns else (8, 128), BF16),
            pltpu.VMEM((4, piece, wide), BF16),
            pltpu.VMEM((4, piece, columns), BF16),
            pltpu.VMEM((3 if split else 2, last, columns), BF16),
            pltpu.VMEM((2, last, columns), BF16),
            pltpu.VMEM((last, columns), BF16),
            pltpu.VMEM((piece, columns), BF16),
        ]

    reduce_scratch = []
    if reduces:
        reduce_scratch = (
            summing(units, units, True, False)
            + summing(units, units, True, True)
            + summing(inner, 2 * inner, True, False)
            + summing(inner, inner, False, True) * 3
            + [pltpu.VMEM((4, piece, inner), BF16)] * 2
            + [pltpu.VMEM((4, piece // 2, inner), BF16)] * 6
            + [pltpu.VMEM((4, piece // 2, units), BF16)] * 2
        )
    copies = 6 + 1 + 9 + 1 + 3 + 2 + (3 + 2 * 6 + 1 + 4 * 7 if reduces else 0)
    return pl.pallas_call(
        functools.partial(back_kernel, reduces),
        out_shape=(
            shape((half, width)),
            shape((half, width)),
            shape((half, width)),
            shape((3, share, inner) if reduces else (3, *cut, inner)),
            shape((share, inner)),
            shape((share, units)),
            shape((share, units)),
            shape((8, width), F32),
        ),
        in_specs=[VMEM] * 8 + [HERE] * 10,
        out_specs=(HERE,) * 7 + (VMEM,),
        scratch_shapes=[
            block(2 * inner),
            block(inner),
            pair(width),
            block(width),
            block(2 * inner, F32),
            block(2 * inner, F32),
            pltpu.VMEM((rows, inner), BF16),
            pair(inner),
            block(inner),
            block(2 * inner, F32),
            pltpu.VMEM((half, half), F32),
            pair(3 * inner),
            pair(width),
            pltpu.VMEM((rows, width), BF16),
            block(width),
            block(width),
            block(width),
            pltpu.VMEM((2, width, half), BF16),
            pltpu.VMEM((3, *cut, inner), BF16),
            pltpu.VMEM((10, 8, width), F32),
        ]
        + reduce_scratch
        + [
            pltpu.SemaphoreType.DMA((copies,)),
            pltpu.SemaphoreType.DMA((copies,)),
            pltpu.SemaphoreType.DMA((24,)),
        ],
        compiler_params=params(63 << 20, collective_id=2, has_side_effects=True),
        name="back",
    )(
        place_row,
        place_col,
        mode,
        vectors,
        back_mine,
        back_other,
        weight,
        sums,
        low,
        value,
        normed,
        unit,
        head_unit,
        head_scale,
        result_other,
        fc1_part.reshape(*cut, -1),
        fc2_part.reshape(*cut, -1),
        out_part.reshape(*cut, -1),
    )


def finish_kernel(*refs):
    tok_ref, own_ref, got_ref, grad_mixed_ref, result_ref, result_got_ref, vec_ref, sum_ref = refs[:8]
    sources, refs = refs[8:12], refs[12:]
    output_ref, input_grad_ref = refs[:2]
    vec_outs, gain_out, targets = refs[2:8], refs[8], refs[9:13]
    for source, target in zip(sources, targets):
        target[...] = source[...].astype(F32)

    @pl.when(pl.program_id(0) == 0)
    def _():
        pack = lax.axis_index("dp")
        share, width = vec_outs[0].shape[0], vec_ref.shape[1]
        sums = sum_ref[...]
        mine = sum(
            jnp.where(pack == index, sums[:, index * share : (index + 1) * share], 0.0)
            for index in range(width // share)
        )
        for index, out_ref in enumerate(vec_outs):
            out_ref[...] = mine[index : index + 1, :].reshape(share)
        few = gain_out.shape[1]
        for index in range(2):
            row = sums[QK_GAIN : QK_GAIN + 1, index * width // 2 : (index + 1) * width // 2]
            row = sum(row[:, first : first + HEAD] for first in range(0, width // 2, HEAD))
            gain_out[index : index + 1, :] = sum(
                jnp.where(pack == place, row[:, place * few : (place + 1) * few], 0.0)
                for place in range(HEAD // few)
            )

    output_ref[...] = (result_ref[...] + result_got_ref[...].astype(F32)).astype(BF16)
    unit, scale = row_norm(tok_ref[...].astype(F32))
    grad = own_ref[...].astype(F32) + got_ref[...].astype(F32)
    grad = row_norm_back(grad * vec_ref[LN1_GAIN : LN1_GAIN + 1, :], unit, scale)
    input_grad_ref[...] = (grad_mixed_ref[...] + grad).astype(BF16)


def finish(token, own, got, grad_mixed, result, result_got, vectors, sums, arrays, share, few):
    half, width = token.shape
    tile = half // 2
    by_row = pl.BlockSpec((tile, width), lambda i: (i, 0))
    whole = pl.BlockSpec((8, width), lambda i: (0, 0))
    parts = 2 if share % 32 == 0 else 1

    def block(array):
        lead = array.shape[:-2]
        dims = (*lead, share // parts, array.shape[-1])
        return pl.BlockSpec(dims, lambda i: (*(0,) * len(lead), i if parts > 1 else 0, 0))

    return pl.pallas_call(
        finish_kernel,
        out_shape=[shape((half, width))] * 2
        + [shape((share,), F32)] * 6
        + [shape((2, few), F32)]
        + [shape(array.shape, F32) for array in arrays],
        grid=(half // tile,),
        in_specs=[by_row] * 6 + [whole] * 2 + [block(array) for array in arrays],
        out_specs=[by_row] * 2
        + [pl.BlockSpec((share,), lambda i: (0,))] * 6
        + [pl.BlockSpec((2, few), lambda i: (0, 0))]
        + [block(array) for array in arrays],
        compiler_params=params(60 << 20, dimension_semantics=("arbitrary",)),
        name="finish",
    )(token, own, got, grad_mixed, result, result_got, vectors, sums, *arrays)


def swap(array, axis, step):
    pairs = [(index, index ^ step) for index in range(lax.axis_size(axis))]
    return lax.ppermute(array, axis, pairs)


def owned_sum(part, dim):
    total = lax.psum_scatter(part.astype(BF16), "dp", scatter_dimension=dim, tiled=True)
    total = (total.astype(F32) + swap(total, "seq", 1).astype(F32)).astype(BF16)
    return total.astype(F32) + swap(total, "seq", 2).astype(F32)


def local(
    tokens,
    segment,
    cotangent,
    ln1_gain,
    ln1_bias,
    qkv_weight,
    qk_gain,
    out_weight,
    out_bias,
    ln2_gain,
    ln2_bias,
    fc1_weight,
    fc2_weight,
    fc2_bias,
):
    half, width = tokens.shape
    packs = lax.axis_size("dp")
    inner = qkv_weight.shape[2]
    share = ln1_gain.shape[0]
    gathers = packs == 4
    pack = lax.axis_index("dp")
    pieces = [ln1_gain, ln1_bias, out_bias, ln2_gain, ln2_bias, fc2_bias]
    if gathers:
        vectors = [*pieces, qk_gain]
    else:
        few = qk_gain.shape[1]
        lanes = jnp.arange(width)
        wide = jnp.where(lanes // share == pack, jnp.tile(jnp.stack(pieces).astype(F32), (1, packs)), 0.0)
        gains = jnp.tile(qk_gain.astype(F32), (1, width // (2 * few))).reshape(1, width)
        gains = jnp.where(lanes % HEAD // few == pack, gains, 0.0)
        vectors = jnp.concatenate([wide, gains, jnp.zeros((1, width), F32)], axis=0)
        vectors = [lax.psum(vectors, "dp")]
        qkv_weight = lax.all_gather(qkv_weight, "dp", axis=1, tiled=True)
    (
        tokens_other,
        cot_other,
        place_row,
        place_col,
        mode,
        vectors,
        mine,
        theirs,
        qkv_full,
        out_mine,
        out_theirs,
        fc1_full,
        fc2_full,
        *kept,
    ) = front(
        gathers, tokens, cotangent, segment, vectors, qkv_weight, out_weight.T, fc1_weight,
        fc2_weight.T,
    )
    if not gathers:
        out_mine = lax.all_gather(out_weight.T, "dp", axis=0, tiled=True)
        out_theirs = swap(out_mine, "hidden", 1)
        fc1_full = lax.all_gather(fc1_weight, "dp", axis=0, tiled=True)
        fc2_full = lax.all_gather(fc2_weight.T, "dp", axis=0, tiled=True)
    (
        grad_mixed,
        back_mine,
        back_other,
        result,
        result_other,
        fc1_part,
        fc2_part,
        out_part,
        sums,
    ) = middle(
        tokens, tokens_other, cotangent, cot_other, place_col, mine, theirs, vectors, out_mine,
        out_theirs, fc1_full, fc2_full,
    )
    own, got, result_got, qkv_owned, out_owned, fc1_owned, fc2_owned, sums = back(
        gathers, place_row, place_col, mode, vectors, back_mine, back_other, qkv_full, sums, kept,
        result_other, fc1_part, fc2_part, out_part, packs,
    )
    if not gathers:
        sums = lax.psum(sums, "dp")
        qkv_owned = owned_sum(qkv_owned.reshape(3, width, inner), 1)
        out_part = out_part[:, :inner].astype(F32) + swap(out_part[:, inner:], "hidden", 1).astype(F32)
        out_owned = owned_sum(out_part, 0)
        fc1_owned = owned_sum(fc1_part, 0)
        fc2_owned = owned_sum(fc2_part, 0)
    output, input_grad, *sums, qk_owned, qkv_owned, out_owned, fc1_owned, fc2_owned = finish(
        tokens, own, got, grad_mixed, result, result_got, vectors, sums,
        [qkv_owned, out_owned, fc1_owned, fc2_owned], share, qk_gain.shape[1],
    )
    return (
        output,
        input_grad,
        sums[LN1_GAIN],
        sums[LN1_BIAS],
        qkv_owned,
        qk_owned,
        out_owned.T,
        sums[OUT_BIAS],
        sums[LN2_GAIN],
        sums[LN2_BIAS],
        fc1_owned,
        fc2_owned.T,
        sums[FC2_BIAS],
    )


def solution(mesh):
    rows = P(("dp", "seq", "hidden"), None)
    in_specs = (
        rows,
        P("dp"),
        rows,
        P("dp"),
        P("dp"),
        P(None, "dp", "hidden"),
        P(None, "dp"),
        P("hidden", "dp"),
        P("dp"),
        P("dp"),
        P("dp"),
        P("dp", "hidden"),
        P("hidden", "dp"),
        P("dp"),
    )
    out_specs = (
        rows,
        rows,
        P("dp"),
        P("dp"),
        P(None, "dp", "hidden"),
        P(None, "dp"),
        P("hidden", "dp"),
        P("dp"),
        P("dp"),
        P("dp"),
        P("dp", "hidden"),
        P("hidden", "dp"),
        P("dp"),
    )
    return jax.shard_map(local, mesh=mesh, in_specs=in_specs, out_specs=out_specs, check_vma=False)
```
